32 devices in a mesh: section: 2 (over x), dp: 16 (over z, y, core).
Axes of the slice: x: 2, y: 2, z: 4, core: 2. Of those that a mesh axis runs over, the one named last changes fastest.
Arguments:
- tokens: bfloat16 [2, 16, 512, 384], P(None, 'dp'), may hold values from -6 to 6
- segments: int32 [2, 16, 512], P(None, 'dp'), may hold values from 0 to 3, never falling along the last dimension, each value on 1 to 256 neighbouring positions
- routes: int32 [2, 2, 16, 512, 2], P('section', None, 'dp'), may hold values from 0 to 15, all different within a row; in each aligned block of 512 rows (0 to 511, 512 to 1023, ..., all dimensions but the last counted through in order) at most 72 rows name the same one
- grad_top: bfloat16 [2, 16, 512, 384], P(None, 'dp'), may hold values from -6 to 6
- w_attn: bfloat16 [2, 1536, 384], P('section', 'dp'), may hold values from -3 to 3
- norm_gains: bfloat16 [2, 768], P('section', 'dp'), may hold values from 0.5 to 1.5
- w_route: bfloat16 [2, 6144], P('section', 'dp'), may hold values from -0.21875 to 0.21875
- w_gate: bfloat16 [2, 16, 384, 768], P('section', 'dp'), may hold values from -0.3125 to 0.3125
- w_up: bfloat16 [2, 16, 384, 768], P('section', 'dp'), may hold values from -0.3125 to 0.3125
- w_down: bfloat16 [2, 16, 768, 384], P('section', 'dp'), may hold values from -0.3125 to 0.3125
Outputs:
- layer_out: bfloat16 [2, 2, 16, 512, 384], P('section', None, 'dp')
- input_grads: float32 [2, 2, 16, 512, 384], P('section', None, 'dp')
- grad_attn: float32 [2, 1536, 384], P('section', 'dp')
- grad_gains: float32 [2, 768], P('section', 'dp')
- grad_route: float32 [2, 6144], P('section', 'dp')
- grad_gate: float32 [2, 16, 384, 768], P('section', 'dp')
- grad_up: float32 [2, 16, 384, 768], P('section', 'dp')
- grad_down: float32 [2, 16, 768, 384], P('section', 'dp')
The draws below stay inside these ranges and needn't reach their ends.
Inputs may be any that keep to these rules, and one draw needn't show every extreme that they name: `segments`: segment ids never fall along a row; each id of a row covers 1 to 256 consecutive tokens, one exactly 256. `routes`: each token names two different experts; among the tokens of one index of dp in one micro-batch and layer, no expert is named more than 72 times, and 72 is reached.
All inputs are finite; a program needn't handle non-finite values.
Results may differ from the reference program's by a relative error of at most 0.02.
Values may be sent and summed in bfloat16 or wider, within the bound.
No kernel may reach another device: no remote copies, remote signals or barrier semaphores. Data moves between devices by JAX's collectives and lax.ppermute only.
A program may use at most 192 MiB of HBM per device.

```python
import math
import jax
import jax.numpy as jnp
import numpy as np
from jax import lax

D = 384
HEADS = 6
FF = 768
LEN = 512
SEGS = 4
SEG_MAX = 256
MICRO = 2
ROWS_DEV = 1
LAYERS = 2
EXPERTS = 16
SPLIT = 1
ROWS = 16
CAP = 72
N_DP = 16


def draw_w_attn(key, part):
    key = jax.random.fold_in(key, 7)
    normal_draw = jax.random.truncated_normal(key, -3.0, 3.0, (LAYERS, 4 * D, D), jnp.float32)
    rows_index = jnp.arange(4 * D)[None, :, None]
    factor = jnp.where(rows_index >= 3 * D, 32.0 ** 0.5, 1.0) * D ** (-0.5)
    return (normal_draw * factor).astype(jnp.bfloat16)


def with_spikes(entries, rng, source, target, parts, factor):
    def block_of(axis_at):
        return (jnp.arange(entries.shape[axis_at]) // (entries.shape[axis_at] // parts)).reshape((-1,) + (1,) * (entries.ndim - 1 - axis_at))

    near = jax.random.permutation(rng, parts)[block_of(target)]
    second = (block_of(target) + parts // 2) % parts
    return jnp.where((block_of(source) == near) | (block_of(source) == second), factor * entries, entries)


def shard_levels(stream_key, extent, shards, low, high):
    gain, own = 1.0, jax.random.fold_in(stream_key, 6)
    for dim, blocks in shards:
        heights = jnp.exp(jax.random.uniform(jax.random.fold_in(own, dim), (blocks,), jnp.float32, low / len(shards), high / len(shards)))
        gain = gain * jnp.repeat(heights, extent[dim] // blocks).reshape([-1 if axis == dim else 1 for axis in range(len(extent))])
    return gain


def split_up(number_of, total, bound, slope):
    weights = [(1 << 20) // math.isqrt(standing ** slope) + 1 for standing in range(2, number_of + 1)]
    rest, given = total - bound - (number_of - 1), [1] * (number_of - 1)
    while rest > 0:
        free = [i for i in range(number_of - 1) if given[i] < bound]
        whole, remaining = sum([weights[i] for i in free]), rest
        for i in free:
            addition = min(bound - given[i], max(1, remaining * weights[i] // whole), rest)
            given[i] = given[i] + addition
            rest = rest - addition
    return np.array([bound] + given)


def uneven(rng, count, total, limit, lean):
    if count == 2:
        one = jax.random.randint(rng, (), max(1, total - limit), min(limit, total - 1) + 1)
        return jnp.stack([one, total - one])
    lengths = jnp.asarray(split_up(count, total, limit, lean), jnp.int32)
    couples = (count - 1) // 2
    giver, sink = lengths[1:1 + 2 * couples:2], lengths[2:2 + 2 * couples:2]
    margin = jnp.minimum(giver - 1, limit - sink)
    moved = jax.random.randint(jax.random.fold_in(rng, 1), (couples,), 0, 1 << 20) % (margin + 1)
    lengths = lengths.at[1:1 + 2 * couples:2].set(giver - moved).at[2:2 + 2 * couples:2].set(sink + moved)
    return lengths[jax.random.permutation(jax.random.fold_in(rng, 2), count)]


def shared_out(stream_key, own, number, rows, number_of, top, most, slope):
    sequence = jax.random.permutation(stream_key, number_of)
    crowded, ordinary = load_shares(number_of, rows * top, most, slope, True), load_shares(number_of, rows * top, most, slope, False)
    places = jnp.arange(number_of)

    def named(tallies, rotation):
        used = int((tallies > 0).sum())
        fixed = max(1, used // 4)
        moved = fixed + (places - fixed + rotation * (used - fixed)) % max(1, number_of - fixed)
        return jnp.zeros((number_of,), jnp.int32).at[sequence[jnp.where(places < fixed, places, moved)]].set(jnp.asarray(tallies, jnp.int32))

    tallies = jnp.where(number % 4 == 0, named(crowded, number // 4), named(ordinary, number - number // 4 - 1))
    mixed = jax.random.permutation(jax.random.fold_in(own, 3), number_of)
    source_of, sink = mixed[0:number_of // 2 * 2:2], mixed[1:number_of // 2 * 2:2]
    margin = jnp.minimum(tallies[source_of] - 1, most - tallies[sink]) // 2
    margin = jnp.where((source_of == sequence[0]) | (sink == sequence[0]) | (tallies[sink] == 0), 0, jnp.maximum(margin, 0))
    moved = jax.random.randint(jax.random.fold_in(own, 4), (number_of // 2,), 0, 1 << 20) % (margin + 1)
    tallies = tallies.at[source_of].add(-moved).at[sink].add(moved)
    items = jnp.searchsorted(jnp.cumsum(tallies), jnp.arange(rows * top), side="right").astype(jnp.int32)
    table = items.reshape(top, rows).T
    table = table[jax.random.permutation(jax.random.fold_in(own, 1), rows)]
    rotation = jax.random.randint(jax.random.fold_in(own, 2), (rows, 1), 0, top)
    return jnp.take_along_axis(table, (jnp.arange(top)[None, :] + rotation) % top, axis=1)


def load_shares(amount, total, limit, slope, full):
    weights = [(1 << 20) // math.isqrt(rank ** slope) + 1 for rank in range(1, amount + 1)]
    largest = limit if full else min(limit, max(-(-total // amount), total * weights[0] // sum(weights)))
    least = 1 if total - largest >= amount - 1 else 0
    holding, surplus = [largest] + [least] * (amount - 1), total - largest - least * (amount - 1)
    while surplus > 0:
        candidates = [i for i in range(1, amount) if holding[i] < largest] or [i for i in range(1, amount) if holding[i] < limit]
        pool, remaining = sum([weights[i] for i in candidates]), surplus
        for i in candidates:
            addition = min(limit - holding[i], max(1, remaining * weights[i] // pool), surplus)
            holding[i] = holding[i] + addition
            surplus = surplus - addition
    return np.array(holding)


def normal_values(stream_key, dims, width, bound, pieces=(), kind=jnp.bfloat16):
    array = jax.random.normal(stream_key, dims, jnp.float32) * width
    if len(pieces) > 0:
        array = shard_levels(stream_key, dims, pieces, -0.22, 0.18) * array
    return jnp.clip(array, min=-bound, max=bound).astype(kind)


def gaussian_with(rng, shape, scale, limit, shards, heavy, kind=jnp.bfloat16):
    array = scale * jax.random.normal(rng, shape, jnp.float32)
    if shards:
        array = array * shard_levels(rng, shape, shards, -0.22, 0.18)
    return jnp.clip(with_spikes(array, jax.random.fold_in(rng, 3), *heavy), -limit, limit).astype(kind)


def setup_inputs(seed: int = 0) -> dict:
    splits = jax.random.split(jax.random.key(seed), 11)
    tokens = gaussian_with(splits[0], (MICRO, ROWS, LEN, D), 1.0, 6.0, ((1, 16),), (1, 3, 16, 2.0))
    segments = jax.vmap(lambda own: jnp.searchsorted(jnp.cumsum(uneven(own, SEGS, LEN, SEG_MAX, 1)), jnp.arange(LEN), side="right"))(jax.random.split(splits[1], MICRO * ROWS)).reshape((MICRO, ROWS, LEN)).astype(jnp.int32)
    routes_keys = jax.random.split(jax.random.fold_in(splits[2], 1), LAYERS * MICRO * ROWS * LEN // (ROWS_DEV * LEN))
    routes_turns = jax.random.permutation(jax.random.fold_in(splits[2], 3), LAYERS * MICRO * ROWS * LEN // (ROWS_DEV * LEN))
    routes = jax.vmap(lambda own, number: shared_out(jax.random.fold_in(splits[2], 2), own, number, ROWS_DEV * LEN, EXPERTS, 2, CAP, 1))(routes_keys, routes_turns).reshape((LAYERS, MICRO, ROWS, LEN, 2))
    grad_top = normal_values(splits[3], (MICRO, ROWS, LEN, D), 1.0, 6.0, ((1, 16),))
    w_attn = draw_w_attn(jax.random.fold_in(splits[10], 71), 0)
    norm_gains = jnp.clip(1.0 + 0.1 * jax.random.normal(splits[5], (LAYERS, 2 * D), jnp.float32), 0.5, 1.5).astype(jnp.bfloat16)
    w_route = normal_values(splits[6], (LAYERS, D * EXPERTS), (2 * D) ** -0.5, 0.21875, ((0, 2), (1, 16)))
    w_gate = normal_values(splits[7], (LAYERS, EXPERTS * SPLIT, D, FF // SPLIT), D ** -0.5, 0.3125, ((0, 2), (1, 16)))
    w_up = normal_values(splits[8], (LAYERS, EXPERTS * SPLIT, D, FF // SPLIT), D ** -0.5, 0.3125, ((0, 2), (1, 16)))
    w_down = normal_values(splits[9], (LAYERS, EXPERTS * SPLIT, FF // SPLIT, D), (FF // 2) ** -0.5, 0.3125, ((0, 2), (1, 16)))
    return dict(tokens=tokens, segments=segments, routes=routes, grad_top=grad_top, w_attn=w_attn, norm_gains=norm_gains, w_route=w_route, w_gate=w_gate, w_up=w_up, w_down=w_down)


@jax.custom_vjp
def low(v):
    return lax.optimization_barrier(v.astype(jnp.bfloat16)).astype(jnp.float32)

@jax.custom_vjp
def low_back(v):
    return v

def low_keep(v):
    return (low(v), None)

def low_pass(kept, grad):
    return (grad,)

def back_keep(v):
    return (v, None)

def back_low(kept, grad):
    return (low(grad),)
low.defvjp(low_keep, low_pass)
low_back.defvjp(back_keep, back_low)
NORM_EPSILON = 1e-05
HIGHEST = lax.Precision.HIGHEST

def norm_apply(values, gain_row):
    normed = values * lax.rsqrt(lax.optimization_barrier(jnp.mean(values * values, axis=-1, keepdims=True)) + NORM_EPSILON)
    return normed * gain_row

def rope_tables(segment, head_width):
    length_row = segment.shape[-1]
    places = jnp.arange(length_row, dtype=jnp.int32)
    starts_new = jnp.concatenate([jnp.ones(segment.shape[:-1] + (1,), dtype=bool), segment[..., 1:] != segment[..., :-1]], axis=-1)
    firsts = lax.cummax(jnp.where(starts_new, places, 0), axis=segment.ndim - 1)
    offsets = (places - firsts).astype(jnp.float32).reshape(-1, 1)
    half_width = head_width // 2
    freqs_row = jnp.exp(jnp.arange(half_width, dtype=jnp.float32) * (-2.0 * math.log(10000.0) / head_width))
    angles = offsets * freqs_row
    return (jnp.cos(angles)[:, None, :], jnp.sin(angles)[:, None, :])

def rotate(values, cosine_table, sine_table):
    half_width = values.shape[-1] // 2
    first_half = values[..., :half_width]
    second_half = values[..., half_width:]
    return jnp.concatenate([first_half * cosine_table - second_half * sine_table, second_half * cosine_table + first_half * sine_table], axis=-1)

def slot_table(chosen, expert_count, capacity):
    flat_ids = chosen.reshape(-1)
    hit_table = (flat_ids[:, None] == jnp.arange(expert_count, dtype=jnp.int32)[None, :]).astype(jnp.int32)
    rank_within = lax.optimization_barrier(jnp.sum(jnp.cumsum(hit_table, axis=0) * hit_table, axis=1)) - 1
    return flat_ids * capacity + rank_within

def attend_row(packed):
    query_row, key_row, value_row, segment_row = packed
    scale_factor = 1.0 / math.sqrt(query_row.shape[-1])
    scores = jnp.einsum('hqd,hkd->hqk', query_row, key_row, precision=HIGHEST) * scale_factor
    scores = low_back(scores)
    allowed = (segment_row[:, None] == segment_row[None, :])[None]
    scores = jnp.where(allowed, scores, -1e+30)
    largest = lax.optimization_barrier(jnp.max(scores, axis=-1, keepdims=True))
    exponent_terms = jnp.exp(scores - largest)
    probabilities = low(exponent_terms / lax.optimization_barrier(jnp.sum(exponent_terms, axis=-1, keepdims=True)))
    return jnp.einsum('hqk,hkd->hqd', probabilities, value_row, precision=HIGHEST)

def layer_apply(inputs, segment, chosen, layer_params):
    w_stack, gain_stack, w_route, w_gate, w_up, w_down = layer_params
    token_count, model_width = inputs.shape
    row_count, length_row = segment.shape
    head_width = model_width // HEADS
    first_in = low(norm_apply(inputs, gain_stack[:model_width]))
    cosine_table, sine_table = rope_tables(segment, head_width)

    def project(weight):
        return jnp.dot(first_in, weight, precision=HIGHEST).reshape(token_count, HEADS, head_width)
    query_heads = low(rotate(low_back(project(w_stack[:model_width])), cosine_table, sine_table))
    key_heads = low(rotate(low_back(project(w_stack[model_width:2 * model_width])), cosine_table, sine_table))
    value_heads = low(low_back(project(w_stack[2 * model_width:3 * model_width])))

    def by_rows(tensor):
        return tensor.reshape(row_count, length_row, HEADS, head_width).transpose(0, 2, 1, 3)
    mixed_heads = lax.map(jax.checkpoint(attend_row), (by_rows(query_heads), by_rows(key_heads), by_rows(value_heads), segment))
    attended = low(low_back(mixed_heads.transpose(0, 2, 1, 3).reshape(token_count, model_width)))
    hidden = inputs + low_back(jnp.dot(attended, w_stack[3 * model_width:], precision=HIGHEST))
    second_in = low(norm_apply(hidden, gain_stack[model_width:]))
    logits = low_back(jnp.dot(second_in, w_route.reshape(model_width, EXPERTS), precision=HIGHEST))
    picked = jnp.take_along_axis(logits, chosen, axis=1)
    gap_logits = picked[:, 0] - picked[:, 1]
    gate_pair = jnp.stack([jax.nn.sigmoid(gap_logits), jax.nn.sigmoid(-gap_logits)], axis=1)
    slot_index = slot_table(chosen, EXPERTS, CAP)
    send_buffer = jnp.zeros((EXPERTS * CAP, model_width), jnp.float32).at[slot_index].set(jnp.repeat(second_in, 2, axis=0))
    copies = jnp.broadcast_to(send_buffer.reshape(EXPERTS, 1, CAP, model_width), (EXPERTS, SPLIT, CAP, model_width))
    received = low_back(copies)
    gate_pieces = w_gate.reshape(EXPERTS, SPLIT, model_width, -1)
    up_pieces = w_up.reshape(EXPERTS, SPLIT, model_width, -1)
    down_pieces = w_down.reshape(EXPERTS, SPLIT, -1, model_width)
    gate_act = low_back(jnp.einsum('escd,esdf->escf', received, gate_pieces, precision=HIGHEST))
    up_act = low_back(jnp.einsum('escd,esdf->escf', received, up_pieces, precision=HIGHEST))
    hidden_act = low(jax.nn.silu(gate_act) * up_act)
    partial_out = low(jnp.einsum('escf,esfd->escd', hidden_act, down_pieces, precision=HIGHEST))
    returned = low_back(lax.optimization_barrier(jnp.sum(partial_out, axis=1)))
    back_rows = returned.reshape(EXPERTS * CAP, model_width)[slot_index].reshape(token_count, 2, model_width)
    return hidden + lax.optimization_barrier(jnp.sum(gate_pair[:, :, None] * back_rows, axis=1))

def two_layers(token_block, shim_zeros, segment, chosen_first, chosen_second, first_params, second_params):
    middle = low(layer_apply(token_block, segment, chosen_first, first_params))
    upper = low(layer_apply(low_back(middle) + shim_zeros, segment, chosen_second, second_params))
    return (middle, upper)

def reference(tokens, segments, routes, grad_top, w_attn, norm_gains, w_route, w_gate, w_up, w_down):
    model_width = tokens.shape[-1]
    group_size = math.gcd(N_DP, max(1, 4096 // (ROWS_DEV * LEN)))
    block_count = MICRO * N_DP // group_size
    token_blocks = tokens.astype(jnp.float32).reshape(block_count, group_size, ROWS_DEV * LEN, model_width)
    segment_blocks = segments.reshape(block_count, group_size, ROWS_DEV, LEN)
    route_blocks = routes.reshape(LAYERS, block_count, group_size, ROWS_DEV * LEN, 2)
    top_blocks = grad_top.astype(jnp.float32).reshape(block_count, group_size, ROWS_DEV * LEN, model_width)
    weights = (w_attn, norm_gains, w_route, w_gate, w_up, w_down)
    first_params = tuple((weight[0].astype(jnp.float32) for weight in weights))
    second_params = tuple((weight[1].astype(jnp.float32) for weight in weights))
    batched = jax.vmap(two_layers, in_axes=(0, 0, 0, 0, 0, None, None))

    def one_block(totals, block_data):
        token_block, segment_block, chosen_first, chosen_second, top_block = block_data
        shim_zeros = jnp.zeros_like(token_block)

        def forward(token_in, shim_in, params_one, params_two):
            return batched(token_in, shim_in, segment_block, chosen_first, chosen_second, params_one, params_two)
        (middle, upper), pull_back = jax.vjp(forward, token_block, shim_zeros, first_params, second_params)
        grad_tokens, grad_shim, grad_first, grad_second = pull_back((jnp.zeros_like(middle), top_block))
        totals = jax.tree.map(jnp.add, totals, (grad_first, grad_second))
        return (totals, (middle, upper, grad_tokens, grad_shim))
    zero_totals = jax.tree.map(jnp.zeros_like, (first_params, second_params))
    totals, (middle, upper, grad_tokens, grad_shim) = lax.scan(one_block, zero_totals, (token_blocks, segment_blocks, route_blocks[0], route_blocks[1], top_blocks))
    full_shape = (LAYERS, MICRO, ROWS, LEN, model_width)
    layer_out = jnp.stack([middle, upper]).reshape(full_shape).astype(jnp.bfloat16)
    input_grads = jnp.stack([grad_tokens, grad_shim]).reshape(full_shape)
    stacked_grads = [jnp.stack([totals[0][number], totals[1][number]]) for number in range(6)]
    return (layer_out, input_grads, stacked_grads[0], stacked_grads[1], stacked_grads[2], stacked_grads[3], stacked_grads[4], stacked_grads[5])
```

```python
import functools
import math

import jax
import jax.numpy as jnp
from jax import lax
from jax.experimental import pallas as pl
from jax.experimental.pallas import tpu as pltpu
from jax.sharding import PartitionSpec as P

HEADS = 6
NORM_EPSILON = 1e-05
LANES = 128
F32 = jnp.float32
BF16 = jnp.bfloat16
I32 = jnp.int32
VMEM_LIMIT = 56 * 1024 * 1024
SPREAD = (False, False)


def dot(left, right, left_dim=1, right_dim=0):
    return lax.dot_general(
        left, right, (((left_dim,), (right_dim,)), ((), ())), preferred_element_type=F32
    )


def places(shape, dim):
    return lax.broadcasted_iota(I32, shape, dim)


def round_up(value, step):
    return -(-value // step) * step


def call(body, outs, args, name, flops, scratch=(), scalars=()):
    specs = [
        pl.BlockSpec(memory_space=pltpu.SMEM if index in scalars else pltpu.VMEM)
        for index in range(len(args))
    ]
    shapes = [jax.ShapeDtypeStruct(shape, dtype) for shape, dtype in outs]
    moved = sum(math.prod(a.shape) * a.dtype.itemsize for a in list(args) + shapes)
    return pl.pallas_call(
        body,
        out_shape=shapes,
        in_specs=specs,
        out_specs=[pl.BlockSpec(memory_space=pltpu.VMEM) for _ in shapes],
        scratch_shapes=list(scratch),
        compiler_params=pltpu.CompilerParams(vmem_limit_bytes=VMEM_LIMIT),
        cost_estimate=pl.CostEstimate(flops=flops, bytes_accessed=moved, transcendentals=0),
        name=name,
    )(*args)


def norm_parts(values):
    inverse = lax.rsqrt(jnp.mean(values * values, axis=-1, keepdims=True) + NORM_EPSILON)
    return values * inverse, inverse


def norm_pull(grad_out, normed, inverse, gain):
    grad_gain = jnp.sum(grad_out * normed, axis=0, keepdims=True)
    grad_normed = grad_out * gain
    inner = jnp.mean(grad_normed * normed, axis=-1, keepdims=True)
    return inverse * (grad_normed - normed * inner), grad_gain


def swap_halves(values, half):
    low = places((1, LANES), 1) % (2 * half) < half
    return jnp.where(
        low, pltpu.roll(values, LANES - half, 1), pltpu.roll(values, half, 1)
    )


def head_lanes(values, head, width):
    lane = places((1, LANES), 1)
    return jnp.where((lane >= head * width) & (lane < (head + 1) * width), values, 0.0)


def weights_of(keys, queries, seg_col, seg_row):
    scores = dot(keys, queries, 1, 1)
    scores = jnp.where(seg_col == seg_row, scores, -1e30)
    terms = jnp.exp(scores - jnp.max(scores, axis=0, keepdims=True))
    return terms * (1.0 / jnp.sum(terms, axis=0, keepdims=True))


def attend(queries, keys, values, seg_col, seg_row, width, tile):
    count = queries.shape[0]
    turned = jnp.transpose(values).astype(BF16)
    parts = []
    for head in range(LANES // width):
        head_keys = head_lanes(keys, head, width).astype(BF16)
        pieces = []
        for at in range(0, count, tile):
            weights = weights_of(
                head_keys, queries[at : at + tile], seg_col, seg_row[:, at : at + tile]
            )
            pieces.append(dot(turned[head * width : (head + 1) * width], weights.astype(BF16)))
        parts.append(jnp.concatenate(pieces, axis=1))
    return jnp.transpose(jnp.concatenate(parts, axis=0))


def attend_pull(queries, keys, values, grads, seg_col, seg_row, width, tile):
    count = queries.shape[0]
    keys32, values32 = keys.astype(F32), values.astype(F32)
    turned = jnp.transpose(keys32).astype(BF16)
    query_parts, grad_keys, grad_values = [], 0.0, 0.0
    for head in range(LANES // width):
        head_keys = head_lanes(keys32, head, width).astype(BF16)
        head_values = head_lanes(values32, head, width).astype(BF16)
        pieces, sum_keys, sum_values = [], 0.0, 0.0
        for at in range(0, count, tile):
            query_part, grad_part = queries[at : at + tile], grads[at : at + tile]
            weights = weights_of(head_keys, query_part, seg_col, seg_row[:, at : at + tile])
            pulled = dot(head_values, grad_part, 1, 1)
            inner = jnp.sum(weights * pulled, axis=0, keepdims=True)
            grad_scores = (weights * (pulled - inner)).astype(BF16)
            pieces.append(dot(turned[head * width : (head + 1) * width], grad_scores))
            sum_keys = sum_keys + dot(grad_scores, query_part)
            sum_values = sum_values + dot(weights.astype(BF16), grad_part)
        query_parts.append(jnp.concatenate(pieces, axis=1))
        grad_keys = grad_keys + head_lanes(sum_keys, head, width)
        grad_values = grad_values + head_lanes(sum_values, head, width)
    return jnp.transpose(jnp.concatenate(query_parts, axis=0)), grad_keys, grad_values


def one_hot(hits):
    return jnp.where(hits, 1.0, 0.0).astype(BF16)


def scatter_rows(out_ref, owner_ref, stride, slot_rows, loads, extra_ref=None, extra_at=0):
    blocks = out_ref.shape[0] // stride
    count = slot_rows.shape[1]
    first, second = slot_rows[0:1], slot_rows[1:2]

    def hits(slots, block):
        return (slots - owner_ref[block] * stride) == places((stride, count), 0)

    def write(step, carry):
        pair = (2 * step, 2 * step + 1)
        if len(loads) == 1:
            chosen = one_hot(
                jnp.concatenate([hits(first, b) | hits(second, b) for b in pair], axis=0)
            )
            rows = dot(chosen, loads[0])
        else:
            rows = dot(
                one_hot(jnp.concatenate([hits(first, b) for b in pair], axis=0)), loads[0]
            ) + dot(one_hot(jnp.concatenate([hits(second, b) for b in pair], axis=0)), loads[1])
        if extra_ref is not None:
            line = places((stride, 1), 0)
            rows = jnp.concatenate(
                [
                    jnp.where(
                        line == extra_at,
                        extra_ref[pl.ds(b, 1), :],
                        rows[i * stride : (i + 1) * stride],
                    )
                    for i, b in enumerate(pair)
                ],
                axis=0,
            )
        at = pl.multiple_of(step * 2 * stride, 16)
        out_ref[pl.ds(at, 2 * stride), :] = rows.astype(BF16)
        return carry

    lax.fori_loop(0, blocks // 2, write, 0, unroll=blocks <= 16)


def gather_rows(slots, base_ref, rows_ref, chunk):
    total = 0.0
    for at in range(0, rows_ref.shape[0], chunk):
        total = total + dot(
            one_hot(slots == base_ref[:, at : at + chunk]), rows_ref[at : at + chunk, :]
        )
    return total


def slots_kernel(strides, expert_count, cols_ref, rows_ref, *outs):
    count = cols_ref.shape[0]
    before = one_hot(places((count, count), 0) > places((count, count), 1))
    after = one_hot(places((count, count), 0) < places((count, count), 1))
    for layer, stride in enumerate(strides):
        col_out, row_out = outs[2 * layer], outs[2 * layer + 1]
        picks = [cols_ref[:, 2 * layer + k : 2 * layer + k + 1] for k in range(2)]
        marks = [pick == places((count, expert_count), 1) for pick in picks]
        ranks = dot(before, one_hot(marks[0] | marks[1]))
        for k in range(2):
            rank = jnp.sum(jnp.where(marks[k], ranks, 0.0), axis=1, keepdims=True)
            col_out[:, k : k + 1] = picks[k] * stride + rank.astype(I32)
        picks = [rows_ref[2 * layer + k : 2 * layer + k + 1, :] for k in range(2)]
        marks = [pick == places((expert_count, count), 0) for pick in picks]
        ranks = dot(one_hot(marks[0] | marks[1]), after)
        for k in range(2):
            rank = jnp.sum(jnp.where(marks[k], ranks, 0.0), axis=0, keepdims=True)
            row_out[k : k + 1, :] = picks[k] * stride + rank.astype(I32)


def scatter_kernel(stride, owner_ref, slot_rows_ref, load_ref, out_ref):
    scatter_rows(out_ref, owner_ref, stride, slot_rows_ref[...], [load_ref[...]])


def forward_kernel(stride, spare, combine, chunk, head_width, tile, *refs):
    refs = list(refs)
    take = lambda number: [refs.pop(0) for _ in range(number)]
    (owner_ref,) = take(1)
    if combine:
        hidden_in, returned, gates_in, slots_in, base_in = take(5)
    else:
        (tokens_ref,) = take(1)
    cos_ref, sin_ref, seg_col, seg_row, wq, wk, wv, wo, wr, gains = take(10)
    pick_cols, pick_rows, slot_cols, slot_rows, owner_col = take(5)
    send, q_out, k_out, v_out, o_out, h_out, x1_out, x2_out, gates_out = take(9)
    if combine:
        y_out, apart_out = take(2)
    (extra_ref,) = take(1)

    if combine:
        first = gather_rows(slots_in[:, 0:1], base_in, returned, chunk)
        second = gather_rows(slots_in[:, 1:2], base_in, returned, chunk)
        whole = hidden_in[...] + gates_in[:, 0:1] * first + gates_in[:, 1:2] * second
        apart_out[...] = first - second
        leaving = whole.astype(BF16)
        y_out[...] = leaving
        entering = leaving.astype(F32)
    else:
        entering = tokens_ref[...].astype(F32)

    half = head_width // 2
    normed, _ = norm_parts(entering)
    x1 = (normed * gains[0:1, :]).astype(BF16)
    x1_out[...] = x1
    cosine, sine = cos_ref[...], sin_ref[...]
    q_all, k_all, v_all = dot(x1, wq[...]), dot(x1, wk[...]), dot(x1, wv[...])
    scale = 1.0 / math.sqrt(head_width)
    mixed = []
    for at in range(0, x1.shape[1], LANES):
        lanes = slice(at, at + LANES)
        q, k, v = q_all[:, lanes], k_all[:, lanes], v_all[:, lanes]
        q = ((q * cosine + swap_halves(q, half) * sine).astype(BF16).astype(F32) * scale).astype(BF16)
        k = (k * cosine + swap_halves(k, half) * sine).astype(BF16)
        v = v.astype(BF16)
        q_out[:, lanes] = q
        k_out[:, lanes] = k
        v_out[:, lanes] = v
        part = attend(
            q, k.astype(F32), v.astype(F32), seg_col[...], seg_row[...], head_width, tile
        ).astype(BF16)
        o_out[:, lanes] = part
        mixed.append(part)
    hidden = entering + dot(jnp.concatenate(mixed, axis=1), wo[...])
    h_out[...] = hidden
    normed, _ = norm_parts(hidden)
    x2 = (normed * gains[1:2, :]).astype(BF16)
    x2_out[...] = x2
    logits = dot(x2, wr[...])
    signs = [
        jnp.where(pick_cols[:, k : k + 1] == places(logits.shape, 1), logits, 0.0) for k in range(2)
    ]
    gap = jnp.sum(signs[0] - signs[1], axis=1, keepdims=True)
    gates_out[:, 0:1] = jax.nn.sigmoid(gap)
    gates_out[:, 1:2] = jax.nn.sigmoid(-gap)
    if spare:
        logits_row = dot(wr[...], x2, 0, 1)
        signs = [
            jnp.where(pick_rows[k : k + 1, :] == places(logits_row.shape, 0), logits_row, 0.0)
            for k in range(2)
        ]
        gap_row = jnp.sum(signs[0] - signs[1], axis=0, keepdims=True)
        high, low = 0.0, 0.0
        for k, gate in enumerate((jax.nn.sigmoid(gap_row), jax.nn.sigmoid(-gap_row))):
            rank = slot_cols[:, k : k + 1] - pick_cols[:, k : k + 1] * stride
            line = one_hot(rank == places((x2.shape[0], LANES), 1))
            held = jnp.where(owner_col[...] == pick_rows[k : k + 1, :], gate, 0.0)
            top = held.astype(BF16)
            rest = (held - top.astype(F32)).astype(BF16)
            high = high + dot(top, line)
            low = low + dot(rest, line)
        extra_ref[:, 0:LANES] = high
        extra_ref[:, LANES : 2 * LANES] = low
        extra_ref[:, 2 * LANES :] = jnp.zeros_like(extra_ref[:, 2 * LANES :])
        scatter_rows(send, owner_ref, stride, slot_rows[...], [x2], extra_ref, spare)
    else:
        scatter_rows(send, owner_ref, stride, slot_rows[...], [x2])


def expert_kernel(rows, x_ref, gate_ref, up_ref, down_ref, out_ref):
    def step(index, carry):
        at = pl.ds(pl.multiple_of(index * rows, 16), rows)
        x = x_ref[at, :]
        gate = dot(x, gate_ref[...])
        hidden = (gate * jax.nn.sigmoid(gate) * dot(x, up_ref[...])).astype(BF16)
        out_ref[at, :] = dot(hidden, down_ref[...]).astype(BF16)
        return carry

    lax.fori_loop(0, x_ref.shape[0] // rows, step, 0)


def expert_pull_kernel(
    rows, stride, spare, x_ref, g_ref, gate_ref, up_ref, down_ref, dx_ref, act_ref, dgate_ref, dup_ref
):
    def step(index, carry):
        at = pl.ds(pl.multiple_of(index * rows, 16), rows)
        x = x_ref[at, :]
        gate = dot(x, gate_ref[...])
        up = dot(x, up_ref[...])
        grad = dot(g_ref[at, :], down_ref[...], 1, 1)
        sigmoid = jax.nn.sigmoid(gate)
        silu = gate * sigmoid
        act = (silu * up).astype(BF16)
        dup = (grad * silu).astype(BF16)
        dgate = (grad * up * sigmoid * (1.0 + gate * (1.0 - sigmoid))).astype(BF16)
        act_ref[at, :] = act
        dup_ref[at, :] = dup
        dgate_ref[at, :] = dgate
        dx = dot(dgate, gate_ref[...], 1, 1) + dot(dup, up_ref[...], 1, 1)
        if spare:
            inner = jnp.sum(grad * act.astype(F32), axis=1, keepdims=True)
            line = places((stride, 1), 0)
            eye = places((stride, LANES), 0) == places((stride, LANES), 1)
            blocks = []
            for top in range(0, rows, stride):
                row = jnp.sum(
                    jnp.where(eye, inner[top : top + stride], 0.0), axis=0, keepdims=True
                )
                high = row.astype(BF16).astype(F32)
                extra = jnp.concatenate(
                    [high, row - high, jnp.zeros((1, dx.shape[1] - 2 * LANES), F32)], axis=1
                )
                blocks.append(jnp.where(line == spare, extra, dx[top : top + stride]))
            dx = jnp.concatenate(blocks, axis=0)
        dx_ref[at, :] = dx.astype(BF16)
        return carry

    lax.fori_loop(0, x_ref.shape[0] // rows, step, 0)


def down_kernel(rows, act_ref, down_ref, out_ref):
    def step(index, carry):
        at = pl.ds(pl.multiple_of(index * rows, 16), rows)
        out_ref[at, :] = dot(act_ref[at, :], down_ref[...]).astype(BF16)
        return carry

    lax.fori_loop(0, act_ref.shape[0] // rows, step, 0)


def finish_kernel(chunk, hidden, returned, gates, slots, base, out_ref):
    first = gather_rows(slots[:, 0:1], base, returned, chunk)
    second = gather_rows(slots[:, 1:2], base, returned, chunk)
    out_ref[...] = (hidden[...] + gates[:, 0:1] * first + gates[:, 1:2] * second).astype(BF16)


def backward_kernel(stride, spare, top, chunk, head_width, tile, next_stride, *refs):
    refs = list(refs)
    take = lambda number: [refs.pop(0) for _ in range(number)]
    returned, grad_top, gates, pick_cols, slot_cols, base, owner_row = take(7)
    apart = None if top else take(1)[0]
    enter_ref, hidden_ref, q_ref, k_ref, v_ref, cos_ref, sin_ref, seg_col, seg_row = take(9)
    wq, wk, wv, wo, wr, gains = take(6)
    if top:
        next_owner, next_gates, next_slots = take(3)
    grad_out, dq_out, dk_out, dv_out, branch_out, dz_out, dgain_out = take(7)
    if top:
        (send,) = take(1)

    grad_y = grad_top[...].astype(F32)
    c1, c2 = gates[:, 0:1], gates[:, 1:2]
    if top:
        parts = [
            gather_rows(slot_cols[:, k : k + 1], base, returned, chunk) for k in range(2)
        ]
        dx2 = c1 * parts[0] + c2 * parts[1]
        blocks = returned.shape[0] // stride
        lines = one_hot(
            places((blocks, returned.shape[0]), 1)
            == places((blocks, returned.shape[0]), 0) * stride + spare
        )
        extra = dot(lines, returned[...]).astype(BF16)
        inner = []
        for k in range(2):
            pick = pick_cols[:, k : k + 1]
            held = dot(one_hot(pick == owner_row[...]), extra)
            held = held[:, 0:LANES] + held[:, LANES : 2 * LANES]
            rank = slot_cols[:, k : k + 1] - pick * stride
            inner.append(
                jnp.sum(
                    jnp.where(rank == places(held.shape, 1), held, 0.0), axis=1, keepdims=True
                )
            )
        apart_grad = inner[0] - inner[1]
    else:
        total = 0.0
        for at in range(0, returned.shape[0], chunk):
            line = base[:, at : at + chunk]
            hits = (slot_cols[:, 0:1] == line) | (slot_cols[:, 1:2] == line)
            total = total + dot(one_hot(hits), returned[at : at + chunk, :])
        dx2 = total
        apart_grad = jnp.sum(grad_y * apart[...], axis=1, keepdims=True)
    grad_gap = apart_grad * c1 * c2
    ids = places((grad_y.shape[0], wr.shape[1]), 1)
    dz = (
        jnp.where(pick_cols[:, 0:1] == ids, grad_gap, 0.0)
        - jnp.where(pick_cols[:, 1:2] == ids, grad_gap, 0.0)
    ).astype(BF16)
    dz_out[...] = dz
    dx2 = dx2 + dot(dz, wr[...], 1, 1)
    normed, inverse = norm_parts(hidden_ref[...])
    middle, grad_gain = norm_pull(dx2, normed, inverse, gains[1:2, :])
    dgain_out[1:2, :] = grad_gain
    grad_hidden = grad_y + middle
    branch = grad_hidden.astype(BF16)
    branch_out[...] = branch
    grad_mixed = dot(branch, wo[...], 1, 1).astype(BF16)

    half = head_width // 2
    cosine, sine = cos_ref[...], sin_ref[...]
    scale = 1.0 / math.sqrt(head_width)
    for at in range(0, q_ref.shape[1], LANES):
        lanes = slice(at, at + LANES)
        dq, dk, dv = attend_pull(
            q_ref[:, lanes],
            k_ref[:, lanes],
            v_ref[:, lanes],
            grad_mixed[:, lanes],
            seg_col[...],
            seg_row[...],
            head_width,
            tile,
        )
        dq = dq * scale
        dq_out[:, lanes] = (dq * cosine - swap_halves(dq, half) * sine).astype(BF16)
        dk_out[:, lanes] = (dk * cosine - swap_halves(dk, half) * sine).astype(BF16)
        dv_out[:, lanes] = dv.astype(BF16)
    dx1 = (
        dot(dq_out[...], wq[...], 1, 1)
        + dot(dk_out[...], wk[...], 1, 1)
        + dot(dv_out[...], wv[...], 1, 1)
    )
    normed, inverse = norm_parts(enter_ref[...].astype(F32))
    lower, grad_gain = norm_pull(dx1, normed, inverse, gains[0:1, :])
    dgain_out[0:1, :] = grad_gain
    grad_enter = grad_hidden + lower
    grad_out[...] = grad_enter
    if top:
        leaving = grad_enter.astype(BF16).astype(F32)
        loads = [(next_gates[:, k : k + 1] * leaving).astype(BF16) for k in range(2)]
        scatter_rows(send, next_owner, next_stride, next_slots[...], loads)


def per_device(
    tokens, segments, routes, grad_top, w_attn, norm_gains, w_route, w_gate, w_up, w_down
):
    section = lax.axis_index("section")
    place = lax.axis_index("dp")
    group = lax.axis_size("dp")
    both = ("section", "dp")
    micro_count, rows_local, length, width = tokens.shape
    count = rows_local * length
    shard_rows = w_attn.shape[1]
    route_shard, gain_shard = w_route.shape[1], norm_gains.shape[1]
    experts = route_shard * group // width
    split = group // experts
    capacity = 9 * count // (4 * experts)
    head_width = width // HEADS
    strides = (round_up(capacity, 8), round_up(capacity + 1, 8))
    sizes = tuple(group * stride for stride in strides)
    chunks = tuple(min(size, 16 * stride) for size, stride in zip(sizes, strides))
    tile = min(256, count)

    def mine(own, other):
        return (
            jnp.where(section == 0, own, other),
            jnp.where(section == 0, other, own),
        )

    def across(array, pairs=((0, 1), (1, 0))):
        return lax.ppermute(array, "section", list(pairs))

    token_rows = tokens[section].reshape(count, width)
    top_rows = grad_top[section].reshape(count, width)
    offset = jnp.arange(rows_local, dtype=I32)[:, None] * length
    segment = (segments[section] + offset).reshape(count)
    own_routes = lax.dynamic_index_in_dim(routes[0], section, 0, keepdims=False)
    far_routes = lax.dynamic_index_in_dim(routes[0], 1 - section, 0, keepdims=False)
    picks = mine(own_routes.reshape(count, 2), across(far_routes.reshape(count, 2)))
    pick_rows = tuple(pick.T for pick in picks)

    small = route_shard + gain_shard
    small_rows = round_up(-(-small // width), 8)

    def pack(matrix, route, gain):
        line = jnp.concatenate([route, gain])
        line = jnp.pad(line, (0, small_rows * width - small)).reshape(small_rows, width)
        return jnp.concatenate([matrix, line], axis=0)

    own_pack = pack(w_attn[0], w_route[0], norm_gains[0])
    packs = mine(own_pack, across(own_pack))

    def gathered(shard):
        bit = group // 2
        held = shard[None]
        while bit:
            other = lax.ppermute(held, "dp", [(i, i ^ bit) for i in range(group)])
            high = (place // bit) % 2 == 1
            held = jnp.where(
                high, jnp.stack([other, held], axis=1), jnp.stack([held, other], axis=1)
            ).reshape(-1, *shard.shape)
            bit //= 2
        return held

    def unpack(full):
        matrix = full[:, :shard_rows].reshape(4 * width, width)
        line = full[:, shard_rows:].reshape(group, -1)
        route = line[:, :route_shard].reshape(width, experts)
        gain = line[:, route_shard:small].reshape(2, width).astype(F32)
        return [matrix[i * width : (i + 1) * width] for i in range(4)] + [route, gain]

    params = tuple(unpack(gathered(packs[layer])) for layer in range(2))

    half = group // 2
    members = jnp.arange(group, dtype=I32)

    def owners(layer):
        if not SPREAD[layer]:
            return members // split
        own_half = jnp.where(members // half == layer, place // half, 1 - place // half)
        return (own_half * half + members % half) // split

    owner = tuple(owners(layer) for layer in range(2))

    def exchange(rows, layer):
        blocks = rows.reshape(group, strides[layer], width)
        if SPREAD[layer]:
            sets = [
                [s * group + h * half + j for s in range(2) for j in range(half)] for h in range(2)
            ]
            moved = lax.all_to_all(
                blocks, both, split_axis=0, concat_axis=0, tiled=True, axis_index_groups=sets
            )
        else:
            moved = lax.all_to_all(blocks, "dp", split_axis=0, concat_axis=0, tiled=True)
        return moved.reshape(sizes[layer], width)

    def to_hosts(array, layer):
        turn = half if SPREAD[layer] else 0
        pairs = [(layer * group + i, (1 - layer) * group + (i ^ turn)) for i in range(group)]
        return lax.ppermute(array, both, pairs)

    def to_owner(array, layer):
        turn = half if SPREAD[layer] else 0
        pairs = [((1 - layer) * group + (i ^ turn), layer * group + i) for i in range(group)]
        return lax.ppermute(array, both, pairs)

    own_experts = (w_gate[0, 0], w_up[0, 0], w_down[0, 0])
    hosted = tuple(
        tuple(jnp.where(section == layer, own, to_hosts(own, layer)) for own in own_experts)
        for layer in range(2)
    )

    slot_out = []
    for layer in range(2):
        slot_out += [((count, 2), I32), ((2, count), I32)]
    slots = call(
        functools.partial(slots_kernel, strides, experts),
        slot_out,
        [jnp.concatenate(picks, axis=1), jnp.concatenate(pick_rows, axis=0)],
        "slots",
        4 * 2 * count * count * experts,
    )
    slot_cols, slot_rows = slots[0::2], slots[1::2]
    firsts = jnp.sum((segment[:, None] > segment[None, :]).astype(I32), axis=1)
    offsets = (jnp.arange(count, dtype=I32) - firsts).astype(F32)
    half_width = head_width // 2
    freqs = jnp.exp(
        jnp.arange(half_width, dtype=F32) * (-2.0 * math.log(10000.0) / head_width)
    )
    angles = offsets[:, None] * freqs
    cosine, sine = jnp.cos(angles), jnp.sin(angles)
    repeats = LANES // head_width
    cosine = jnp.concatenate([cosine, cosine] * repeats, axis=1)
    sine = jnp.concatenate([-sine, sine] * repeats, axis=1)
    seg_col, seg_row = segment[:, None], segment[None, :]

    def base_row(layer):
        line = jnp.arange(strides[layer], dtype=I32)
        base = owner[layer][:, None] * strides[layer] + line[None, :]
        return jnp.where(line[None, :] < capacity, base, -1).reshape(1, sizes[layer])

    bases = (base_row(0), base_row(1))
    tables = [cosine, sine, seg_col, seg_row]
    spares = (0, capacity)
    tokens_flops = 2 * count * width
    attn_flops = tokens_flops * (4 * width + 2 * count * (LANES // head_width) * 2)
    move_flops = [tokens_flops * size for size in sizes]
    hidden_units = w_gate.shape[-1]
    expert_flops = [2 * size * width * hidden_units for size in sizes]

    def block_rows(layer):
        blocks = 1
        while 2 * blocks * strides[layer] <= 384 and group % (2 * blocks) == 0:
            blocks *= 2
        return blocks * strides[layer]

    def forward(layer, lead, combine):
        size = sizes[layer]
        outs = [((size, width), BF16)]
        outs += [((count, width), BF16)] * 4
        outs += [((count, width), F32), ((count, width), BF16), ((count, width), BF16)]
        outs += [((count, 2), F32)]
        if combine:
            outs += [((count, width), BF16), ((count, width), F32)]
        args = [owner[layer]] + lead + tables + params[layer]
        args += [picks[layer], pick_rows[layer], slot_cols[layer], slot_rows[layer]]
        args += [owner[layer][:, None]]
        return call(
            functools.partial(
                forward_kernel,
                strides[layer],
                spares[layer],
                combine,
                chunks[0],
                head_width,
                tile,
            ),
            outs,
            args,
            f"layer{layer}_forward",
            attn_flops + move_flops[layer] * (3 if combine else 1),
            scratch=[pltpu.VMEM((group, width), F32)],
            scalars=(0,),
        )

    (top_send,) = call(
        functools.partial(scatter_kernel, strides[1]),
        [((sizes[1], width), BF16)],
        [owner[1], slot_rows[1], top_rows],
        "top_send",
        move_flops[1],
        scalars=(0,),
    )
    top_received = exchange(top_send, 1)

    send0, q0, k0, v0, o0, h0, x1_0, x2_0, gates0 = forward(0, [token_rows], False)
    received0 = exchange(send0, 0)
    (result0,) = call(
        functools.partial(expert_kernel, block_rows(0)),
        [((sizes[0], width), BF16)],
        [received0, *hosted[0]],
        "layer0_experts",
        3 * expert_flops[0],
    )
    returned0 = exchange(result0, 0)

    send1, q1, k1, v1, o1, h1, x1_1, x2_1, gates1, y0, apart0 = forward(
        1, [h0, returned0, gates0, slot_cols[0], bases[0]], True
    )
    received1 = exchange(send1, 1)

    hidden_out = lambda layer: ((sizes[layer], hidden_units), BF16)
    dx1_send, act1, dgate1, dup1 = call(
        functools.partial(expert_pull_kernel, block_rows(1), strides[1], spares[1]),
        [((sizes[1], width), BF16), hidden_out(1), hidden_out(1), hidden_out(1)],
        [received1, top_received, *hosted[1]],
        "layer1_experts",
        5 * expert_flops[1],
    )
    dx1_back = exchange(dx1_send, 1)
    (result1,) = call(
        functools.partial(down_kernel, block_rows(1)),
        [((sizes[1], width), BF16)],
        [act1, hosted[1][2]],
        "layer1_down",
        expert_flops[1],
    )
    returned1 = exchange(result1, 1)
    (y1,) = call(
        functools.partial(finish_kernel, chunks[1]),
        [((count, width), BF16)],
        [h1, returned1, gates1, slot_cols[1], bases[1]],
        "layer1_out",
        2 * move_flops[1],
    )

    def pulled(rows):
        return jnp.einsum("nd,nf->df", *rows, preferred_element_type=F32)

    lines = received1.reshape(group, strides[1], width)[:, capacity].astype(F32)
    gate_slots = lines[:, :LANES] + lines[:, LANES : 2 * LANES]
    gate_slots = gate_slots[:, : strides[1]].reshape(sizes[1], 1)
    scaled = (received1.astype(F32) * gate_slots).astype(BF16)
    scaled_top = (top_received.astype(F32) * gate_slots).astype(BF16)
    expert_grads1 = (
        pulled((scaled, dgate1)),
        pulled((scaled, dup1)),
        pulled((act1, scaled_top)),
    )

    def backward(layer, args, top):
        outs = [((count, width), F32)]
        outs += [((count, width), BF16)] * 4
        outs += [((count, experts), BF16), ((2, width), F32)]
        scalars = ()
        if top:
            outs += [((sizes[0], width), BF16)]
            scalars = (len(args) - 3,)
        return call(
            functools.partial(
                backward_kernel,
                strides[layer],
                spares[layer],
                top,
                chunks[layer],
                head_width,
                tile,
                strides[0],
            ),
            outs,
            args,
            f"layer{layer}_backward",
            3 * attn_flops + move_flops[layer] * (4 if top else 1),
            scalars=scalars,
        )

    grad1, dq1, dk1, dv1, branch1, dz1, dgain1, dr0_send = backward(
        1,
        [dx1_back, top_rows, gates1, picks[1], slot_cols[1], bases[1], owner[1][None, :]]
        + [y0, h1, q1, k1, v1]
        + tables
        + params[1]
        + [owner[0], gates0, slot_rows[0]],
        True,
    )
    dr0 = exchange(dr0_send, 0)

    dx0_send, act0, dgate0, dup0 = call(
        functools.partial(expert_pull_kernel, block_rows(0), strides[0], 0),
        [((sizes[0], width), BF16), hidden_out(0), hidden_out(0), hidden_out(0)],
        [received0, dr0, *hosted[0]],
        "layer0_experts_pull",
        5 * expert_flops[0],
    )
    dx0_back = exchange(dx0_send, 0)
    expert_grads0 = (
        pulled((received0, dgate0)),
        pulled((received0, dup0)),
        pulled((act0, dr0)),
    )
    grad1_in = grad1.astype(BF16)
    grad0, dq0, dk0, dv0, branch0, dz0, dgain0 = backward(
        0,
        [dx0_back, grad1_in, gates0, picks[0], slot_cols[0], bases[0], owner[0][None, :], apart0]
        + [token_rows, h0, q0, k0, v0]
        + tables
        + params[0],
        False,
    )

    def reduced(x1, x2, o, dq, dk, dv, branch, dz, dgain):
        matrix = jnp.concatenate(
            [pulled((x1, dq)), pulled((x1, dk)), pulled((x1, dv)), pulled((o, branch))], axis=0
        ).astype(BF16)
        route = pulled((x2, dz)).astype(BF16).reshape(group, route_shard)
        gain = dgain.astype(BF16).reshape(group, gain_shard)
        line = jnp.concatenate([route, gain], axis=1)
        line = jnp.pad(line, ((0, 0), (0, small_rows * width - small)))
        blocks = jnp.concatenate(
            [
                matrix.reshape(group, shard_rows, width),
                line.reshape(group, small_rows, width),
            ],
            axis=1,
        )
        moved = lax.all_to_all(blocks, "dp", split_axis=0, concat_axis=0, tiled=True)
        return jnp.sum(moved.astype(F32), axis=0)

    sums1 = reduced(x1_1, x2_1, o1, dq1, dk1, dv1, branch1, dz1, dgain1)
    sums0 = reduced(x1_0, x2_0, o0, dq0, dk0, dv0, branch0, dz0, dgain0)
    to_second, to_first = ((0, 1),), ((1, 0),)
    total = jnp.where(
        section == 0,
        sums0 + across(sums0, to_first),
        sums1 + across(sums1, to_second),
    )
    line = total[shard_rows:].reshape(-1)

    expert_out = []
    for first, second in zip(expert_grads0, expert_grads1):
        expert_out.append(
            jnp.where(
                section == 0,
                first + to_owner(first.astype(BF16), 0).astype(F32),
                second + to_owner(second.astype(BF16), 1).astype(F32),
            )[None, None]
        )

    def by_micro(first, second):
        from_second, from_first = across(first, to_first), across(second, to_second)
        return jnp.where(
            section == 0, jnp.stack([first, from_second]), jnp.stack([from_first, second])
        ).reshape(1, micro_count, rows_local, length, width)

    return (
        by_micro(y0, y1),
        by_micro(grad0, grad1),
        total[:shard_rows][None],
        line[route_shard:small][None],
        line[:route_shard][None],
        *expert_out,
    )


def solution(mesh):
    in_specs = (
        P(None, "dp", None, None),
        P(None, "dp", None),
        P("section", None, "dp", None, None),
        P(None, "dp", None, None),
        P("section", "dp", None),
        P("section", "dp"),
        P("section", "dp"),
        P("section", "dp", None, None),
        P("section", "dp", None, None),
        P("section", "dp", None, None),
    )
    out_specs = (
        P("section", None, "dp", None, None),
        P("section", None, "dp", None, None),
        P("section", "dp", None),
        P("section", "dp"),
        P("section", "dp"),
        P("section", "dp", None, None),
        P("section", "dp", None, None),
        P("section", "dp", None, None),
    )
    return jax.shard_map(
        per_device, mesh=mesh, in_specs=in_specs, out_specs=out_specs, check_vma=False
    )
```

```python
import functools
import math

import jax
import jax.numpy as jnp
from jax import lax
from jax.experimental import pallas as pl
from jax.experimental.pallas import tpu as pltpu
from jax.sharding import PartitionSpec as P

HEADS = 6
NORM_EPSILON = 1e-05
LANES = 128
F32 = jnp.float32
BF16 = jnp.bfloat16
I32 = jnp.int32
VMEM_LIMIT = 56 * 1024 * 1024
SPREAD = (False, False)


def dot(left, right, left_dim=1, right_dim=0):
    return lax.dot_general(
        left, right, (((left_dim,), (right_dim,)), ((), ())), preferred_element_type=F32
    )


def places(shape, dim):
    return lax.broadcasted_iota(I32, shape, dim)


def tie(value, *others):
    return lax.optimization_barrier((value, others))[0]


def round_up(value, step):
    return -(-value // step) * step


def call(body, outs, args, name, flops, scratch=(), scalars=()):
    specs = [
        pl.BlockSpec(memory_space=pltpu.SMEM if index in scalars else pltpu.VMEM)
        for index in range(len(args))
    ]
    shapes = [jax.ShapeDtypeStruct(shape, dtype) for shape, dtype in outs]
    moved = sum(math.prod(a.shape) * a.dtype.itemsize for a in list(args) + shapes)
    return pl.pallas_call(
        body,
        out_shape=shapes,
        in_specs=specs,
        out_specs=[pl.BlockSpec(memory_space=pltpu.VMEM) for _ in shapes],
        scratch_shapes=list(scratch),
        compiler_params=pltpu.CompilerParams(vmem_limit_bytes=VMEM_LIMIT),
        cost_estimate=pl.CostEstimate(flops=flops, bytes_accessed=moved, transcendentals=0),
        name=name,
    )(*args)


def norm_parts(values):
    inverse = lax.rsqrt(jnp.mean(values * values, axis=-1, keepdims=True) + NORM_EPSILON)
    return values * inverse, inverse


def norm_pull(grad_out, normed, inverse, gain):
    grad_gain = jnp.sum(grad_out * normed, axis=0, keepdims=True)
    grad_normed = grad_out * gain
    inner = jnp.mean(grad_normed * normed, axis=-1, keepdims=True)
    return inverse * (grad_normed - normed * inner), grad_gain


def swap_halves(values, half):
    low = places((1, LANES), 1) % (2 * half) < half
    return jnp.where(
        low, pltpu.roll(values, LANES - half, 1), pltpu.roll(values, half, 1)
    )


def head_lanes(values, head, width):
    lane = places((1, LANES), 1)
    return jnp.where((lane >= head * width) & (lane < (head + 1) * width), values, 0.0)


def weights_of(keys, queries, seg_col, seg_row):
    scores = dot(keys, queries, 1, 1)
    scores = jnp.where(seg_col == seg_row, scores, -1e30)
    terms = jnp.exp(scores - jnp.max(scores, axis=0, keepdims=True))
    return terms * (1.0 / jnp.sum(terms, axis=0, keepdims=True))


def attend(queries, keys, values, seg_col, seg_row, width, tile):
    count = queries.shape[0]
    turned = jnp.transpose(values).astype(BF16)
    parts = []
    for head in range(LANES // width):
        head_keys = head_lanes(keys, head, width).astype(BF16)
        pieces = []
        for at in range(0, count, tile):
            weights = weights_of(
                head_keys, queries[at : at + tile], seg_col, seg_row[:, at : at + tile]
            )
            pieces.append(dot(turned[head * width : (head + 1) * width], weights.astype(BF16)))
        parts.append(jnp.concatenate(pieces, axis=1))
    return jnp.transpose(jnp.concatenate(parts, axis=0))


def attend_pull(queries, keys, values, grads, seg_col, seg_row, width, tile):
    count = queries.shape[0]
    keys32, values32 = keys.astype(F32), values.astype(F32)
    turned = jnp.transpose(keys32).astype(BF16)
    query_parts, grad_keys, grad_values = [], 0.0, 0.0
    for head in range(LANES // width):
        head_keys = head_lanes(keys32, head, width).astype(BF16)
        head_values = head_lanes(values32, head, width).astype(BF16)
        pieces, sum_keys, sum_values = [], 0.0, 0.0
        for at in range(0, count, tile):
            query_part, grad_part = queries[at : at + tile], grads[at : at + tile]
            weights = weights_of(head_keys, query_part, seg_col, seg_row[:, at : at + tile])
            pulled = dot(head_values, grad_part, 1, 1)
            inner = jnp.sum(weights * pulled, axis=0, keepdims=True)
            grad_scores = (weights * (pulled - inner)).astype(BF16)
            pieces.append(dot(turned[head * width : (head + 1) * width], grad_scores))
            sum_keys = sum_keys + dot(grad_scores, query_part)
            sum_values = sum_values + dot(weights.astype(BF16), grad_part)
        query_parts.append(jnp.concatenate(pieces, axis=1))
        grad_keys = grad_keys + head_lanes(sum_keys, head, width)
        grad_values = grad_values + head_lanes(sum_values, head, width)
    return jnp.transpose(jnp.concatenate(query_parts, axis=0)), grad_keys, grad_values


def one_hot(hits):
    return jnp.where(hits, 1.0, 0.0).astype(BF16)


def scatter_rows(out_ref, owner, stride, slot_rows, loads, extra_ref=None, extra_at=0):
    blocks = out_ref.shape[0] // stride
    count = slot_rows.shape[1]
    first, second = slot_rows[0:1], slot_rows[1:2]

    def hits(slots, block):
        return (slots - owner(block) * stride) == places((stride, count), 0)

    def write(step, carry):
        pair = (2 * step, 2 * step + 1)
        if len(loads) == 1:
            chosen = one_hot(
                jnp.concatenate([hits(first, b) | hits(second, b) for b in pair], axis=0)
            )
            rows = dot(chosen, loads[0])
        else:
            rows = dot(
                one_hot(jnp.concatenate([hits(first, b) for b in pair], axis=0)), loads[0]
            ) + dot(one_hot(jnp.concatenate([hits(second, b) for b in pair], axis=0)), loads[1])
        if extra_ref is not None:
            line = places((stride, 1), 0)
            rows = jnp.concatenate(
                [
                    jnp.where(
                        line == extra_at,
                        extra_ref[pl.ds(b, 1), :],
                        rows[i * stride : (i + 1) * stride],
                    )
                    for i, b in enumerate(pair)
                ],
                axis=0,
            )
        at = pl.multiple_of(step * 2 * stride, 16)
        out_ref[pl.ds(at, 2 * stride), :] = rows.astype(BF16)
        return carry

    lax.fori_loop(0, blocks // 2, write, 0, unroll=blocks <= 16)


def owners(turn, group, split):
    return lambda member: ((member + turn) % group) // split


def slot_line(owner, group, stride, capacity):
    row = places((1, group * stride), 1)
    at = row % stride
    return jnp.where(at < capacity, owner(row // stride) * stride + at, -1)


def gather_rows(slots, line, rows_ref, chunk):
    total = 0.0
    for at in range(0, rows_ref.shape[0], chunk):
        part = line[:, at : at + chunk]
        hits = slots[0] == part
        for more in slots[1:]:
            hits = hits | (more == part)
        total = total + dot(one_hot(hits), rows_ref[at : at + chunk, :])
    return total


def tables_kernel(strides, experts, half, scalars, *refs):
    own_cols, far_cols, own_rows, far_rows, cos_ref, sin_ref = refs[:6]
    cosine, sine, *outs = refs[6:]
    count = own_cols.shape[0]
    cosine[...] = jnp.concatenate([cos_ref[...]] * (LANES // half), axis=1)
    low = places((1, LANES), 1) % (2 * half) < half
    turned = jnp.concatenate([sin_ref[...]] * (LANES // half), axis=1)
    sine[...] = jnp.where(low, -turned, turned)
    first = scalars[0] == 0
    before = one_hot(places((count, count), 0) > places((count, count), 1))
    after = one_hot(places((count, count), 0) < places((count, count), 1))
    for layer, stride in enumerate(strides):
        pick_cols, pick_rows, slot_cols, slot_rows = outs[4 * layer : 4 * layer + 4]
        own = first if layer == 0 else jnp.logical_not(first)
        cols = jnp.where(own, own_cols[...], far_cols[...])
        rows = jnp.where(own, own_rows[...], far_rows[...])
        pick_cols[...] = cols
        pick_rows[...] = rows
        marks = [cols[:, k : k + 1] == places((count, experts), 1) for k in range(2)]
        ranks = dot(before, one_hot(marks[0] | marks[1]))
        for k in range(2):
            rank = jnp.sum(jnp.where(marks[k], ranks, 0.0), axis=1, keepdims=True)
            slot_cols[:, k : k + 1] = cols[:, k : k + 1] * stride + rank.astype(I32)
        marks = [rows[k : k + 1, :] == places((experts, count), 0) for k in range(2)]
        ranks = dot(one_hot(marks[0] | marks[1]), after)
        for k in range(2):
            rank = jnp.sum(jnp.where(marks[k], ranks, 0.0), axis=0, keepdims=True)
            slot_rows[k : k + 1, :] = rows[k : k + 1, :] * stride + rank.astype(I32)


def scatter_kernel(stride, split, turn_at, scalars, slot_rows_ref, load_ref, out_ref):
    group = out_ref.shape[0] // stride
    owner = owners(scalars[turn_at], group, split)
    scatter_rows(out_ref, owner, stride, slot_rows_ref[...], [load_ref[scalars[0]]])


def unpack_rows(pack_ref, shard_rows, wide_ref, route_ref, gains_ref):
    group, rows, width = pack_ref.shape
    small = rows - shard_rows
    for i in range(group):
        wide_ref[i * shard_rows : (i + 1) * shard_rows, :] = pack_ref[i, :shard_rows, :]
    lines = jnp.concatenate(
        [pack_ref[i, shard_rows:, :].astype(F32) for i in range(group)], axis=0
    ).astype(BF16)
    experts = route_ref.shape[1]
    each = width // group
    row, line = places((width, 1), 0), places((1, group * small), 1)
    spread = dot(one_hot(line == row // each * small), lines)
    lane = places((1, width), 1)
    spread = jnp.where(lane // experts == row % each, spread, 0.0).astype(BF16)
    fold = one_hot(places((width, 1), 0) % experts == places((1, experts), 1))
    route_ref[...] = dot(spread, fold).astype(BF16)
    each = 2 * width // group
    lane = places((1, 2 * width), 1)
    spread = dot(lines, one_hot(places((width, 1), 0) == lane % each))
    line = places((group * small, 1), 0)
    spread = jnp.where(line == lane // each * small + 1, spread, 0.0)
    gains = jnp.sum(spread, axis=0, keepdims=True)
    gains_ref[0:1, :] = gains[:, :width]
    gains_ref[1:2, :] = gains[:, width:]


def sums_kernel(scalars, *refs):
    x1, x2, o, dq, dk, dv, branch, dz, dgain, keep, give, wide = refs
    width, experts = x1.shape[1], dz.shape[1]
    pairs, rows, _ = keep.shape
    group = 2 * pairs
    shard_rows = 4 * width // group
    small = rows - shard_rows
    x1_turned = jnp.transpose(x1[...].astype(F32)).astype(BF16)
    for i, grads in enumerate((dq, dk, dv)):
        wide[i * width : (i + 1) * width, :] = dot(x1_turned, grads[...]).astype(BF16)
    wide[3 * width :, :] = dot(
        jnp.transpose(o[...].astype(F32)).astype(BF16), branch[...]
    ).astype(BF16)
    route = dot(jnp.transpose(x2[...].astype(F32)).astype(BF16), dz[...]).astype(BF16)
    each = width // group
    row, lane = places((width, 1), 0), places((1, width), 1)
    spread = dot(route, one_hot(places((experts, 1), 0) == lane % experts))
    spread = jnp.where(lane // experts == row % each, spread, 0.0).astype(BF16)
    line = places((group * small, 1), 0)
    lines = dot(one_hot(line == places((1, width), 1) // each * small), spread)
    each = 2 * width // group
    lane = places((1, 2 * width), 1)
    gains = jnp.concatenate([dgain[0:1, :], dgain[1:2, :]], axis=1)
    held = jnp.where(line == lane // each * small + 1, gains, 0.0).astype(BF16)
    lines = lines + dot(held, one_hot(places((1, width), 1) == places((2 * width, 1), 0) % each))
    core = scalars[1]
    for out, side in ((keep, core), (give, 1 - core)):
        for i in range(pairs):
            at = pl.multiple_of((2 * i + side) * shard_rows, 16)
            out[i, :shard_rows, :] = wide[pl.ds(at, shard_rows), :]
            out[i, shard_rows:, :] = jnp.where(
                side == 0,
                lines[2 * i * small : (2 * i + 1) * small],
                lines[(2 * i + 1) * small : (2 * i + 2) * small],
            ).astype(BF16)


def forward_kernel(cfg, combine, packed, scalars, *refs):
    stride, spare, chunk, capacities, strides, head_width, tile, split, turn_at, shard_rows = cfg
    refs = list(refs)
    take = lambda number: [refs.pop(0) for _ in range(number)]
    if combine:
        hidden_in, returned, gates_in, slots_in = take(4)
    else:
        (tokens_ref,) = take(1)
    cos_ref, sin_ref, seg_col, seg_row = take(4)
    params = take(1 if packed else 3)
    pick_cols, pick_rows, slot_cols, slot_rows = take(4)
    send, q_out, k_out, v_out, o_out, h_out, x1_out, x2_out, gates_out = take(9)
    if combine:
        y_out, apart_out = take(2)
    if packed:
        wide, wr, gains = take(3)
        unpack_rows(params[0], shard_rows, wide, wr, gains)
    else:
        wide, wr, gains = params
    (extra_ref,) = take(1)
    group = send.shape[0] // stride
    owner = owners(scalars[turn_at], group, split)

    if combine:
        lower_owner = owners(scalars[2], group, split)
        line = slot_line(lower_owner, group, strides[0], capacities)
        first = gather_rows([slots_in[:, 0:1]], line, returned, chunk)
        second = gather_rows([slots_in[:, 1:2]], line, returned, chunk)
        whole = hidden_in[...] + gates_in[:, 0:1] * first + gates_in[:, 1:2] * second
        apart_out[...] = first - second
        leaving = whole.astype(BF16)
        y_out[...] = leaving
        entering = leaving.astype(F32)
    else:
        entering = tokens_ref[scalars[0]].astype(F32)

    half = head_width // 2
    width = entering.shape[1]
    normed, _ = norm_parts(entering)
    x1 = (normed * gains[0:1, :]).astype(BF16)
    x1_out[...] = x1
    cosine, sine = cos_ref[...], sin_ref[...]
    q_all, k_all, v_all = (dot(x1, wide[i * width : (i + 1) * width, :]) for i in range(3))
    scale = 1.0 / math.sqrt(head_width)
    mixed = []
    for at in range(0, width, LANES):
        lanes = slice(at, at + LANES)
        q, k, v = q_all[:, lanes], k_all[:, lanes], v_all[:, lanes]
        q = ((q * cosine + swap_halves(q, half) * sine).astype(BF16).astype(F32) * scale).astype(BF16)
        k = (k * cosine + swap_halves(k, half) * sine).astype(BF16)
        v = v.astype(BF16)
        q_out[:, lanes] = q
        k_out[:, lanes] = k
        v_out[:, lanes] = v
        part = attend(
            q, k.astype(F32), v.astype(F32), seg_col[...], seg_row[...], head_width, tile
        ).astype(BF16)
        o_out[:, lanes] = part
        mixed.append(part)
    hidden = entering + dot(jnp.concatenate(mixed, axis=1), wide[3 * width :, :])
    h_out[...] = hidden
    normed, _ = norm_parts(hidden)
    x2 = (normed * gains[1:2, :]).astype(BF16)
    x2_out[...] = x2
    logits = dot(x2, wr[...])
    signs = [
        jnp.where(pick_cols[:, k : k + 1] == places(logits.shape, 1), logits, 0.0) for k in range(2)
    ]
    gap = jnp.sum(signs[0] - signs[1], axis=1, keepdims=True)
    gates_out[:, 0:1] = jax.nn.sigmoid(gap)
    gates_out[:, 1:2] = jax.nn.sigmoid(-gap)
    if spare:
        logits_row = dot(wr[...], x2, 0, 1)
        signs = [
            jnp.where(pick_rows[k : k + 1, :] == places(logits_row.shape, 0), logits_row, 0.0)
            for k in range(2)
        ]
        gap_row = jnp.sum(signs[0] - signs[1], axis=0, keepdims=True)
        high, low = 0.0, 0.0
        members = owner(places((group, 1), 0))
        for k, gate in enumerate((jax.nn.sigmoid(gap_row), jax.nn.sigmoid(-gap_row))):
            rank = slot_cols[:, k : k + 1] - pick_cols[:, k : k + 1] * stride
            line = one_hot(rank == places((x2.shape[0], LANES), 1))
            held = jnp.where(members == pick_rows[k : k + 1, :], gate, 0.0)
            top = held.astype(BF16)
            rest = (held - top.astype(F32)).astype(BF16)
            high = high + dot(top, line)
            low = low + dot(rest, line)
        extra_ref[:, 0:LANES] = high
        extra_ref[:, LANES : 2 * LANES] = low
        extra_ref[:, 2 * LANES :] = jnp.zeros_like(extra_ref[:, 2 * LANES :])
        scatter_rows(send, owner, stride, slot_rows[...], [x2], extra_ref, spare)
    else:
        scatter_rows(send, owner, stride, slot_rows[...], [x2])


def expert_kernel(rows, x_ref, gate_ref, up_ref, down_ref, out_ref):
    def step(index, carry):
        at = pl.ds(pl.multiple_of(index * rows, 16), rows)
        x = x_ref[at, :]
        gate = dot(x, gate_ref[...])
        hidden = (gate * jax.nn.sigmoid(gate) * dot(x, up_ref[...])).astype(BF16)
        out_ref[at, :] = dot(hidden, down_ref[...]).astype(BF16)
        return carry

    lax.fori_loop(0, x_ref.shape[0] // rows, step, 0)


def expert_pull_kernel(
    rows, stride, spare, x_ref, g_ref, gate_ref, up_ref, down_ref, dx_ref, act_ref, dgate_ref, dup_ref
):
    def step(index, carry):
        at = pl.ds(pl.multiple_of(index * rows, 16), rows)
        x = x_ref[at, :]
        gate = dot(x, gate_ref[...])
        up = dot(x, up_ref[...])
        grad = dot(g_ref[at, :], down_ref[...], 1, 1)
        sigmoid = jax.nn.sigmoid(gate)
        silu = gate * sigmoid
        act = (silu * up).astype(BF16)
        dup = (grad * silu).astype(BF16)
        dgate = (grad * up * sigmoid * (1.0 + gate * (1.0 - sigmoid))).astype(BF16)
        act_ref[at, :] = act
        dup_ref[at, :] = dup
        dgate_ref[at, :] = dgate
        dx = dot(dgate, gate_ref[...], 1, 1) + dot(dup, up_ref[...], 1, 1)
        if spare:
            inner = jnp.sum(grad * act.astype(F32), axis=1, keepdims=True)
            line = places((stride, 1), 0)
            eye = places((stride, LANES), 0) == places((stride, LANES), 1)
            blocks = []
            for top in range(0, rows, stride):
                row = jnp.sum(
                    jnp.where(eye, inner[top : top + stride], 0.0), axis=0, keepdims=True
                )
                high = row.astype(BF16).astype(F32)
                extra = jnp.concatenate(
                    [high, row - high, jnp.zeros((1, dx.shape[1] - 2 * LANES), F32)], axis=1
                )
                blocks.append(jnp.where(line == spare, extra, dx[top : top + stride]))
            dx = jnp.concatenate(blocks, axis=0)
        dx_ref[at, :] = dx.astype(BF16)
        return carry

    lax.fori_loop(0, x_ref.shape[0] // rows, step, 0)


def down_kernel(rows, act_ref, down_ref, out_ref):
    def step(index, carry):
        at = pl.ds(pl.multiple_of(index * rows, 16), rows)
        out_ref[at, :] = dot(act_ref[at, :], down_ref[...]).astype(BF16)
        return carry

    lax.fori_loop(0, act_ref.shape[0] // rows, step, 0)


def finish_kernel(cfg, scalars, hidden, returned, gates, slots, out_ref):
    stride, capacity, chunk, split, turn_at = cfg
    group = returned.shape[0] // stride
    line = slot_line(owners(scalars[turn_at], group, split), group, stride, capacity)
    first = gather_rows([slots[:, 0:1]], line, returned, chunk)
    second = gather_rows([slots[:, 1:2]], line, returned, chunk)
    out_ref[...] = (hidden[...] + gates[:, 0:1] * first + gates[:, 1:2] * second).astype(BF16)


def backward_kernel(cfg, top, scalars, *refs):
    stride, spare, chunk, capacity, next_stride, head_width, tile, split, turn_at = cfg
    refs = list(refs)
    take = lambda number: [refs.pop(0) for _ in range(number)]
    returned, grad_top, gates, pick_cols, slot_cols = take(5)
    apart = None if top else take(1)[0]
    enter_ref, hidden_ref, q_ref, k_ref, v_ref, cos_ref, sin_ref, seg_col, seg_row = take(9)
    wide, wr, gains = take(3)
    if top:
        next_gates, next_slots = take(2)
    grad_out, dq_out, dk_out, dv_out, branch_out, dz_out, dgain_out = take(7)
    if top:
        send, low_out = take(2)

    group = returned.shape[0] // stride
    owner = owners(scalars[turn_at], group, split)
    line = slot_line(owner, group, stride, capacity)
    width = wide.shape[1]
    grad_y = (grad_top[scalars[0]] if top else grad_top[...]).astype(F32)
    c1, c2 = gates[:, 0:1], gates[:, 1:2]
    if top:
        parts = [
            gather_rows([slot_cols[:, k : k + 1]], line, returned, chunk) for k in range(2)
        ]
        dx2 = c1 * parts[0] + c2 * parts[1]
        lines = one_hot(
            places((group, returned.shape[0]), 1)
            == places((group, returned.shape[0]), 0) * stride + spare
        )
        extra = dot(lines, returned[...]).astype(BF16)
        inner = []
        for k in range(2):
            pick = pick_cols[:, k : k + 1]
            held = dot(one_hot(pick == owner(places((1, group), 1))), extra)
            held = held[:, 0:LANES] + held[:, LANES : 2 * LANES]
            rank = slot_cols[:, k : k + 1] - pick * stride
            inner.append(
                jnp.sum(
                    jnp.where(rank == places(held.shape, 1), held, 0.0), axis=1, keepdims=True
                )
            )
        apart_grad = inner[0] - inner[1]
    else:
        dx2 = gather_rows([slot_cols[:, 0:1], slot_cols[:, 1:2]], line, returned, chunk)
        apart_grad = jnp.sum(grad_y * apart[...], axis=1, keepdims=True)
    grad_gap = apart_grad * c1 * c2
    ids = places((grad_y.shape[0], wr.shape[1]), 1)
    dz = (
        jnp.where(pick_cols[:, 0:1] == ids, grad_gap, 0.0)
        - jnp.where(pick_cols[:, 1:2] == ids, grad_gap, 0.0)
    ).astype(BF16)
    dz_out[...] = dz
    dx2 = dx2 + dot(dz, wr[...], 1, 1)
    normed, inverse = norm_parts(hidden_ref[...])
    middle, grad_gain = norm_pull(dx2, normed, inverse, gains[1:2, :])
    dgain_out[1:2, :] = grad_gain
    grad_hidden = grad_y + middle
    branch = grad_hidden.astype(BF16)
    branch_out[...] = branch
    grad_mixed = dot(branch, wide[3 * width :, :], 1, 1).astype(BF16)

    half = head_width // 2
    cosine, sine = cos_ref[...], sin_ref[...]
    scale = 1.0 / math.sqrt(head_width)
    for at in range(0, q_ref.shape[1], LANES):
        lanes = slice(at, at + LANES)
        dq, dk, dv = attend_pull(
            q_ref[:, lanes],
            k_ref[:, lanes],
            v_ref[:, lanes],
            grad_mixed[:, lanes],
            seg_col[...],
            seg_row[...],
            head_width,
            tile,
        )
        dq = dq * scale
        dq_out[:, lanes] = (dq * cosine - swap_halves(dq, half) * sine).astype(BF16)
        dk_out[:, lanes] = (dk * cosine - swap_halves(dk, half) * sine).astype(BF16)
        dv_out[:, lanes] = dv.astype(BF16)
    dx1 = (
        dot(dq_out[...], wide[:width, :], 1, 1)
        + dot(dk_out[...], wide[width : 2 * width, :], 1, 1)
        + dot(dv_out[...], wide[2 * width : 3 * width, :], 1, 1)
    )
    entering = enter_ref[...] if top else enter_ref[scalars[0]]
    normed, inverse = norm_parts(entering.astype(F32))
    lower, grad_gain = norm_pull(dx1, normed, inverse, gains[0:1, :])
    dgain_out[0:1, :] = grad_gain
    grad_enter = grad_hidden + lower
    grad_out[...] = grad_enter
    if top:
        rounded = grad_enter.astype(BF16)
        low_out[...] = rounded
        loads = [(next_gates[:, k : k + 1] * rounded.astype(F32)).astype(BF16) for k in range(2)]
        next_owner = owners(scalars[2], send.shape[0] // next_stride, split)
        scatter_rows(send, next_owner, next_stride, next_slots[...], loads)


def per_device(
    tokens, segments, routes, grad_top, w_attn, norm_gains, w_route, w_gate, w_up, w_down
):
    section = lax.axis_index("section")
    place = lax.axis_index("dp")
    group = lax.axis_size("dp")
    both = ("section", "dp")
    half = group // 2
    micro_count, rows_local, length, width = tokens.shape
    count = rows_local * length
    shard_rows = w_attn.shape[1]
    route_shard, gain_shard = w_route.shape[1], norm_gains.shape[1]
    experts = route_shard * group // width
    split = group // experts
    capacity = 9 * count // (4 * experts)
    head_width = width // HEADS
    half_width = head_width // 2
    strides = (round_up(capacity, 8), round_up(capacity + 1, 8))
    spares = (0, capacity)
    sizes = tuple(group * stride for stride in strides)
    chunks = tuple(min(size, 16 * stride) for size, stride in zip(sizes, strides))
    tile = min(256, count)
    aligned = shard_rows % 16 == 0
    hidden_units = w_gate.shape[-1]

    fence = lax.optimization_barrier
    to_second, to_first = ((0, 1),), ((1, 0),)

    def across(array, pairs=((0, 1), (1, 0))):
        return lax.ppermute(array, "section", list(pairs))

    def round_dp(array, bit):
        return lax.ppermute(array, "dp", [(i, i ^ bit) for i in range(group)])

    turns = [
        ((place // half) ^ layer) * half if SPREAD[layer] else jnp.zeros_like(place)
        for layer in range(2)
    ]
    scalars = jnp.stack([section, place % 2, *turns]).astype(I32)

    small_rows = 8

    def wide_row(row):
        return jnp.pad(row, ((0, 0), (0, width - row.shape[1])))

    own_pack = jnp.concatenate(
        [
            w_attn[0],
            wide_row(w_route),
            wide_row(norm_gains),
            jnp.zeros((small_rows - 2, width), BF16),
        ]
    )
    far_pack = across(own_pack)
    packs = (
        jnp.where(section == 0, own_pack, far_pack),
        jnp.where(section == 0, far_pack, own_pack),
    )

    def doubled(held, bit):
        return merged(held, round_dp(held, bit), bit)

    def merged(held, other, bit):
        high = (place // bit) % 2 == 1
        return jnp.where(
            high, jnp.stack([other, held], axis=1), jnp.stack([held, other], axis=1)
        ).reshape(-1, *held.shape[1:])

    bits = [group >> step for step in range(1, group.bit_length())]

    def unpack(full):
        if aligned:
            return [full]
        route = full[:, shard_rows, :route_shard].reshape(width, experts)
        gain = full[:, shard_rows + 1, :gain_shard].reshape(2, width).astype(F32)
        return [full[:, :shard_rows].reshape(4 * width, width), route, gain]

    def exchange(rows, layer):
        blocks = rows.reshape(group, strides[layer], width)
        if SPREAD[layer]:
            sets = [
                [s * group + h * half + j for s in range(2) for j in range(half)] for h in range(2)
            ]
            moved = lax.all_to_all(
                blocks, both, split_axis=0, concat_axis=0, tiled=True, axis_index_groups=sets
            )
        else:
            moved = lax.all_to_all(blocks, "dp", split_axis=0, concat_axis=0, tiled=True)
        return moved.reshape(sizes[layer], width)

    turn = half if SPREAD[0] else 0

    def traded(array):
        pairs = [
            (s * group + i, (1 - s) * group + (i ^ turn)) for s in range(2) for i in range(group)
        ]
        return lax.ppermute(array, both, pairs)

    def to_owner(array, layer):
        pairs = [((1 - layer) * group + (i ^ turn), layer * group + i) for i in range(group)]
        return lax.ppermute(array.astype(BF16), both, pairs)

    own_experts = (w_gate[0, 0], w_up[0, 0], w_down[0, 0])

    own_routes = lax.dynamic_index_in_dim(routes[0], section, 0, keepdims=False).reshape(count, 2)
    far_routes = lax.dynamic_index_in_dim(routes[0], 1 - section, 0, keepdims=False)
    far_routes = across(far_routes.reshape(count, 2))
    offset = jnp.arange(rows_local, dtype=I32)[:, None] * length
    segment = (lax.dynamic_index_in_dim(segments, section, 0, keepdims=False) + offset).reshape(count)
    firsts = jnp.sum((segment[:, None] > segment[None, :]).astype(I32), axis=1)
    offsets = (jnp.arange(count, dtype=I32) - firsts).astype(F32)
    freqs = jnp.exp(
        jnp.arange(half_width, dtype=F32) * (-2.0 * math.log(10000.0) / head_width)
    )
    angles = offsets[:, None] * freqs
    seg_col, seg_row = segment[:, None], segment[None, :]
    slot_out = [((count, 2), I32), ((2, count), I32)] * 2
    cosine, sine, *slots = call(
        functools.partial(tables_kernel, strides, experts, half_width),
        [((count, LANES), F32)] * 2 + slot_out * 2,
        [scalars, own_routes, far_routes, own_routes.T, far_routes.T]
        + [jnp.cos(angles), jnp.sin(angles)],
        "tables",
        4 * 2 * count * count * experts,
        scalars=(0,),
    )
    pick_cols, pick_rows, slot_cols, slot_rows = (slots[i::4] for i in range(4))
    tables = [cosine, sine, seg_col, seg_row]
    token_block = tokens.reshape(micro_count, count, width)
    top_block = grad_top.reshape(micro_count, count, width)

    tokens_flops = 2 * count * width
    attn_flops = tokens_flops * (4 * width + 2 * count * (LANES // head_width) * 2)
    move_flops = [tokens_flops * size for size in sizes]
    expert_flops = [2 * size * width * hidden_units for size in sizes]

    def block_rows(layer):
        blocks = 1
        while 2 * blocks * strides[layer] <= 384 and group % (2 * blocks) == 0:
            blocks *= 2
        return blocks * strides[layer]

    def forward(layer, lead, combine, params):
        outs = [((sizes[layer], width), BF16)]
        outs += [((count, width), BF16)] * 4
        outs += [((count, width), F32), ((count, width), BF16), ((count, width), BF16)]
        outs += [((count, 2), F32)]
        if combine:
            outs += [((count, width), BF16), ((count, width), F32)]
        if aligned:
            outs += [((4 * width, width), BF16), ((width, experts), BF16), ((2, width), F32)]
        cfg = (strides[layer], spares[layer], chunks[0], capacity, strides, head_width, tile)
        cfg += (split, 2 + layer, shard_rows)
        results = call(
            functools.partial(forward_kernel, cfg, combine, aligned),
            outs,
            [scalars, *lead, *tables, *params]
            + [pick_cols[layer], pick_rows[layer], slot_cols[layer], slot_rows[layer]],
            f"layer{layer}_forward",
            attn_flops + move_flops[layer] * (3 if combine else 1),
            scratch=[pltpu.VMEM((group, width), F32)],
            scalars=(0,),
        )
        return results if aligned else [*results, *params]

    def backward(layer, args, top):
        outs = [((count, width), F32)]
        outs += [((count, width), BF16)] * 4
        outs += [((count, experts), BF16), ((2, width), F32)]
        if top:
            outs += [((sizes[0], width), BF16), ((count, width), BF16)]
        cfg = (strides[layer], spares[layer], chunks[layer], capacity, strides[0], head_width, tile)
        cfg += (split, 2 + layer)
        return call(
            functools.partial(backward_kernel, cfg, top),
            outs,
            [scalars, *args],
            f"layer{layer}_backward",
            3 * attn_flops + move_flops[layer] * (4 if top else 1),
            scalars=(0,),
        )

    def pulled(rows):
        return jnp.einsum("nd,nf->df", *rows, preferred_element_type=F32)

    def by_core(x1, x2, o, dq, dk, dv, branch, dz, dgain):
        if aligned:
            block = ((half, shard_rows + small_rows, width), BF16)
            return call(
                sums_kernel,
                [block, block],
                [scalars, x1, x2, o, dq, dk, dv, branch, dz, dgain],
                "own_sums",
                4 * tokens_flops * width,
                scratch=[pltpu.VMEM((4 * width, width), BF16)],
                scalars=(0,),
            )
        matrix = jnp.concatenate(
            [pulled((x1, dq)), pulled((x1, dk)), pulled((x1, dv)), pulled((o, branch))], axis=0
        )
        route = pulled((x2, dz)).reshape(group, 1, route_shard)
        gain = dgain.reshape(group, 1, gain_shard)
        blocks = jnp.concatenate(
            [
                matrix.reshape(group, shard_rows, width),
                jnp.pad(route, ((0, 0), (0, 0), (0, width - route_shard))),
                jnp.pad(gain, ((0, 0), (0, 0), (0, width - gain_shard))),
                jnp.zeros((group, small_rows - 2, width), F32),
            ],
            axis=1,
        ).astype(BF16)
        pairs = blocks.reshape(half, 2, *blocks.shape[1:])
        return (
            lax.dynamic_index_in_dim(pairs, place % 2, 1, keepdims=False),
            lax.dynamic_index_in_dim(pairs, 1 - place % 2, 1, keepdims=False),
        )

    def paired(keep, give):
        return (keep.astype(F32) + round_dp(give, 1).astype(F32)).astype(BF16)

    def spread(blocks):
        sets = [[2 * chip + c for chip in range(half)] for c in range(2)]
        return lax.all_to_all(
            blocks, "dp", split_axis=0, concat_axis=0, tiled=True, axis_index_groups=sets
        )

    def summed(moved):
        return jnp.sum(moved.astype(F32), axis=0)

    def by_micro(first, far_first, second, far_second):
        return jnp.where(
            section == 0,
            jnp.stack([first, far_first.astype(first.dtype)]),
            jnp.stack([far_second.astype(second.dtype), second]),
        ).reshape(1, micro_count, rows_local, length, width)

    def joined(first, far_first, second, far_second):
        whole = jnp.where(
            section == 0, first + far_first.astype(F32), second + far_second.astype(F32)
        )
        return whole[None, None]

    def hosted(index, far):
        own = own_experts[index]
        return jnp.where(section == 0, own, far), jnp.where(section == 0, far, own)

    def cut(array):
        rows = array.shape[0] // 2
        return array[:rows], array[rows:]

    gate_parts, up_parts = cut(own_experts[0]), cut(own_experts[1])
    gathered = doubled(packs[0][None], bits[0])
    far_gate_a = traded(tie(gate_parts[0], far_pack))
    other = round_dp(gathered, bits[1])
    other, far_gate_a = fence((other, far_gate_a))
    gathered = merged(gathered, other, bits[1])
    other = round_dp(gathered, bits[2])
    held1 = tie(packs[1][None], gathered)
    other1 = round_dp(held1, bits[0])
    far_gate_b = traded(tie(gate_parts[1], gathered))
    other, other1, far_gate_b, tables, slot_rows, slot_cols = fence(
        (other, other1, far_gate_b, tables, slot_rows, slot_cols)
    )
    gathered = merged(gathered, other, bits[2])
    held1 = merged(held1, other1, bits[0])
    for bit in bits[3:]:
        gathered = doubled(gathered, bit)

    far_up_a = traded(tie(up_parts[0], far_gate_b))
    other1 = round_dp(held1, bits[1])
    results = forward(0, [token_block], False, unpack(gathered))
    send0, q0, k0, v0, o0, h0, x1_0, x2_0, gates0, *params0 = results
    send0, far_up_a, other1 = fence((send0, far_up_a, other1))
    received0 = exchange(send0, 0)
    held1 = merged(held1, other1, bits[1])
    other1 = round_dp(held1, bits[2])
    far_up_b = traded(tie(up_parts[1], send0))
    far_down = traded(tie(own_experts[2], send0))
    (top_send,) = call(
        functools.partial(scatter_kernel, strides[1], split, 3),
        [((sizes[1], width), BF16)],
        [scalars, tie(slot_rows[1], send0), top_block],
        "top_send",
        move_flops[1],
        scalars=(0,),
    )
    far_gate = jnp.concatenate([far_gate_a, far_gate_b])
    far_up = jnp.concatenate([far_up_a, far_up_b])
    gates_up_down = [hosted(i, far) for i, far in enumerate((far_gate, far_up, far_down))]
    experts0, experts1 = zip(*gates_up_down)
    received0, top_send, experts0, experts1, other1 = fence(
        (received0, top_send, experts0, experts1, other1)
    )
    held1 = merged(held1, other1, bits[2])
    (result0,) = call(
        functools.partial(expert_kernel, block_rows(0)),
        [((sizes[0], width), BF16)],
        [received0, *experts0],
        "layer0_experts",
        3 * expert_flops[0],
    )
    returned0 = exchange(result0, 0)
    for bit in bits[3:]:
        held1 = doubled(held1, bit)

    returned0, top_send, held1 = fence((returned0, top_send, held1))
    top_received = exchange(top_send, 1)
    results = forward(1, [h0, returned0, gates0, slot_cols[0]], True, unpack(held1))
    send1, q1, k1, v1, o1, h1, x1_1, x2_1, gates1, y0, apart0, *params1 = results
    send1, top_received, y0 = fence((send1, top_received, y0))
    received1 = exchange(send1, 1)
    far_y0 = across(y0, to_first)
    received1, far_y0 = fence((received1, far_y0))

    hidden_out = lambda layer: ((sizes[layer], hidden_units), BF16)
    dx1_send, act1, dgate1, dup1 = call(
        functools.partial(expert_pull_kernel, block_rows(1), strides[1], spares[1]),
        [((sizes[1], width), BF16), hidden_out(1), hidden_out(1), hidden_out(1)],
        [received1, top_received, *experts1],
        "layer1_experts",
        5 * expert_flops[1],
    )
    dx1_send, act1, dgate1, dup1 = fence((dx1_send, act1, dgate1, dup1))
    dx1_back = exchange(dx1_send, 1)
    lines = received1.reshape(group, strides[1], width)[:, capacity].astype(F32)
    gate_slots = lines[:, :LANES] + lines[:, LANES : 2 * LANES]
    gate_slots = gate_slots[:, : strides[1]].reshape(sizes[1], 1)
    scaled = (received1.astype(F32) * gate_slots).astype(BF16)
    scaled_top = (top_received.astype(F32) * gate_slots).astype(BF16)
    gate1 = pulled((scaled, dgate1))
    far_gate1 = to_owner(gate1, 1)
    (result1,) = call(
        functools.partial(down_kernel, block_rows(1)),
        [((sizes[1], width), BF16)],
        [act1, experts1[2]],
        "layer1_down",
        expert_flops[1],
    )
    up1, down1 = pulled((scaled, dup1)), pulled((act1, scaled_top))
    dx1_back, result1, gate1, up1, down1, far_gate1 = fence(
        (dx1_back, result1, gate1, up1, down1, far_gate1)
    )

    returned1 = exchange(result1, 1)
    results = backward(
        1,
        [dx1_back, top_block, gates1, pick_cols[1], slot_cols[1], y0, h1, q1, k1, v1]
        + [*tables, *params1, gates0, slot_rows[0]],
        True,
    )
    results, returned1 = fence((results, returned1))
    grad1, dq1, dk1, dv1, branch1, dz1, dgain1, dr0_send, low1 = results
    dr0 = exchange(dr0_send, 0)
    far_up1 = to_owner(tie(up1, dr0_send), 1)
    (y1,) = call(
        functools.partial(finish_kernel, (strides[1], capacity, chunks[1], split, 3)),
        [((count, width), BF16)],
        [scalars, h1, returned1, gates1, slot_cols[1]],
        "layer1_out",
        2 * move_flops[1],
        scalars=(0,),
    )
    blocks1 = paired(*by_core(x1_1, x2_1, o1, dq1, dk1, dv1, branch1, dz1, dgain1))
    dr0, blocks1, y1, far_up1 = fence((dr0, blocks1, y1, far_up1))

    dx0_send, act0, dgate0, dup0 = call(
        functools.partial(expert_pull_kernel, block_rows(0), strides[0], 0),
        [((sizes[0], width), BF16), hidden_out(0), hidden_out(0), hidden_out(0)],
        [received0, dr0, *experts0],
        "layer0_experts_pull",
        5 * expert_flops[0],
    )
    dx0_send, act0, dgate0, dup0 = fence((dx0_send, act0, dgate0, dup0))
    dx0_back = exchange(dx0_send, 0)
    gate0 = pulled((received0, dgate0))
    far_gate0 = to_owner(gate0, 0)
    up0, down0 = pulled((received0, dup0)), pulled((act0, dr0))
    far_down1 = to_owner(tie(down1, dx0_send), 1)
    dx0_back, gate0, up0, down0, far_gate0, far_down1 = fence(
        (dx0_back, gate0, up0, down0, far_gate0, far_down1)
    )

    moved1 = spread(tie(blocks1, dx0_back))
    far_up0 = to_owner(up0, 0)
    results = backward(
        0,
        [dx0_back, low1, gates0, pick_cols[0], slot_cols[0], apart0, token_block, h0, q0, k0, v0]
        + [*tables, *params0],
        False,
    )
    results, moved1, far_up0 = fence((results, moved1, far_up0))
    grad0, dq0, dk0, dv0, branch0, dz0, dgain0 = results

    keep, give = by_core(x1_0, x2_0, o0, dq0, dk0, dv0, branch0, dz0, dgain0)
    far_low = across(jnp.where(section == 0, tie(low1, grad0), grad0.astype(BF16)))
    far_down0 = to_owner(tie(down0, grad0), 0)
    far_y1 = across(tie(y1, grad0), to_second)
    blocks0 = paired(keep, give)
    moved0 = spread(blocks0)
    sums1 = summed(tie(moved1, blocks0))
    far_sums1 = across(sums1, to_second)
    expert_out = (
        joined(gate0, far_gate0, tie(gate1, blocks0), far_gate1),
        joined(up0, far_up0, tie(up1, blocks0), far_up1),
        joined(down0, far_down0, down1, far_down1),
    )
    input_grads = by_micro(grad0, far_low, grad1, far_low)
    layer_out = by_micro(y0, far_y0, y1, far_y1)
    moved0, input_grads, far_sums1, ready = fence((moved0, input_grads, far_sums1, expert_out[:2]))
    expert_out = (*ready, expert_out[2])
    sums0 = summed(moved0)
    total = jnp.where(section == 0, sums0 + across(sums0, to_first), sums1 + far_sums1)
    return (
        layer_out,
        input_grads,
        total[:shard_rows][None],
        total[shard_rows + 1, :gain_shard][None],
        total[shard_rows, :route_shard][None],
        *expert_out,
    )


def solution(mesh):
    in_specs = (
        P(None, "dp", None, None),
        P(None, "dp", None),
        P("section", None, "dp", None, None),
        P(None, "dp", None, None),
        P("section", "dp", None),
        P("section", "dp"),
        P("section", "dp"),
        P("section", "dp", None, None),
        P("section", "dp", None, None),
        P("section", "dp", None, None),
    )
    out_specs = (
        P("section", None, "dp", None, None),
        P("section", None, "dp", None, None),
        P("section", "dp", None),
        P("section", "dp"),
        P("section", "dp"),
        P("section", "dp", None, None),
        P("section", "dp", None, None),
        P("section", "dp", None, None),
    )
    return jax.shard_map(
        per_device, mesh=mesh, in_specs=in_specs, out_specs=out_specs, check_vma=False
    )
```

```python
import functools
import math

import jax
import jax.numpy as jnp
from jax import lax
from jax.experimental import pallas as pl
from jax.experimental.pallas import tpu as pltpu
from jax.sharding import PartitionSpec as P

HEADS = 6
NORM_EPSILON = 1e-05
LANES = 128
F32 = jnp.float32
BF16 = jnp.bfloat16
I32 = jnp.int32
VMEM_LIMIT = 56 * 1024 * 1024


def dot(left, right, left_dim=1, right_dim=0):
    return lax.dot_general(
        left, right, (((left_dim,), (right_dim,)), ((), ())), preferred_element_type=F32
    )


def places(shape, dim):
    return lax.broadcasted_iota(I32, shape, dim)


def tie(value, *others):
    return lax.optimization_barrier((value, others))[0]


def round_up(value, step):
    return -(-value // step) * step


def call(body, outs, args, name, flops, scratch=(), scalars=()):
    shapes = [jax.ShapeDtypeStruct(shape, dtype) for shape, dtype in outs]
    moved = sum(math.prod(a.shape) * a.dtype.itemsize for a in list(args) + shapes)
    return pl.pallas_call(
        body,
        out_shape=shapes,
        in_specs=[
            pl.BlockSpec(memory_space=pltpu.SMEM if index in scalars else pltpu.VMEM)
            for index in range(len(args))
        ],
        out_specs=[pl.BlockSpec(memory_space=pltpu.VMEM) for _ in shapes],
        scratch_shapes=list(scratch),
        compiler_params=pltpu.CompilerParams(vmem_limit_bytes=VMEM_LIMIT),
        cost_estimate=pl.CostEstimate(flops=flops, bytes_accessed=moved, transcendentals=0),
        name=name,
    )(*args)


def norm_parts(values):
    inverse = lax.rsqrt(jnp.mean(values * values, axis=-1, keepdims=True) + NORM_EPSILON)
    return values * inverse, inverse


def norm_pull(grad_out, normed, inverse, gain):
    grad_gain = jnp.sum(grad_out * normed, axis=0, keepdims=True)
    grad_normed = grad_out * gain
    inner = jnp.mean(grad_normed * normed, axis=-1, keepdims=True)
    return inverse * (grad_normed - normed * inner), grad_gain


def swap_halves(values, half):
    low = places((1, LANES), 1) % (2 * half) < half
    return jnp.where(
        low, pltpu.roll(values, LANES - half, 1), pltpu.roll(values, half, 1)
    )


def wide_tables(cos_ref, sin_ref):
    half = cos_ref.shape[1]
    cosine = jnp.concatenate([cos_ref[...]] * (LANES // half), axis=1)
    sine = jnp.concatenate([sin_ref[...]] * (LANES // half), axis=1)
    return cosine, jnp.where(places((1, LANES), 1) % (2 * half) < half, -sine, sine)


def head_lanes(values, head, width):
    lane = places((1, LANES), 1)
    return jnp.where((lane >= head * width) & (lane < (head + 1) * width), values, 0.0)


def staged(jobs, *stages):
    values = {}
    for step in range(len(jobs) + len(stages) - 1):
        for late, stage in enumerate(stages):
            index = step - late
            if 0 <= index < len(jobs):
                values[index] = stage(*jobs[index], *values.get(index, ()))
    return [values[index] for index in range(len(jobs))]


def attend(queries, keys, values, seg_col, seg_row, width, tile):
    count = queries[0].shape[0]
    heads = LANES // width
    turned = [jnp.transpose(v.astype(F32)).astype(BF16) for v in values]
    jobs = [
        (block, head, at)
        for block in range(len(queries))
        for head in range(heads)
        for at in range(0, count, tile)
    ]

    def scores(block, head, at):
        own = head_lanes(keys[block].astype(F32), head, width).astype(BF16)
        return (dot(own, queries[block][at : at + tile], 1, 1),)

    def terms(block, head, at, score):
        score = jnp.where(seg_col == seg_row[:, at : at + tile], score, -1e30)
        term = jnp.exp(score - jnp.max(score, axis=0, keepdims=True))
        return ((term * (1.0 / jnp.sum(term, axis=0, keepdims=True))).astype(BF16),)

    def mixed(block, head, at, weights):
        return dot(turned[block][head * width : (head + 1) * width], weights)

    parts = staged(jobs, scores, terms, mixed)
    each = count // tile
    outs = []
    for block in range(len(queries)):
        rows = []
        for head in range(heads):
            first = (block * heads + head) * each
            rows.append(jnp.concatenate(parts[first : first + each], axis=1))
        outs.append(jnp.transpose(jnp.concatenate(rows, axis=0)))
    return outs


def attend_pull(queries, keys, values, grads, seg_col, seg_row, width, tile):
    count = queries[0].shape[0]
    heads = LANES // width
    turned = [jnp.transpose(k.astype(F32)).astype(BF16) for k in keys]
    jobs = [
        (block, head, at)
        for block in range(len(queries))
        for head in range(heads)
        for at in range(0, count, tile)
    ]

    def scores(block, head, at):
        own_keys = head_lanes(keys[block].astype(F32), head, width).astype(BF16)
        own_values = head_lanes(values[block].astype(F32), head, width).astype(BF16)
        return (
            dot(own_keys, queries[block][at : at + tile], 1, 1),
            dot(own_values, grads[block][at : at + tile], 1, 1),
        )

    def terms(block, head, at, score, pulled):
        score = jnp.where(seg_col == seg_row[:, at : at + tile], score, -1e30)
        term = jnp.exp(score - jnp.max(score, axis=0, keepdims=True))
        weights = term * (1.0 / jnp.sum(term, axis=0, keepdims=True))
        inner = jnp.sum(weights * pulled, axis=0, keepdims=True)
        return weights.astype(BF16), (weights * (pulled - inner)).astype(BF16)

    def mixed(block, head, at, weights, grad_scores):
        return (
            dot(turned[block][head * width : (head + 1) * width], grad_scores),
            dot(grad_scores, queries[block][at : at + tile]),
            dot(weights, grads[block][at : at + tile]),
        )

    parts = staged(jobs, scores, terms, mixed)
    each = count // tile
    outs = []
    for block in range(len(queries)):
        rows, grad_keys, grad_values = [], 0.0, 0.0
        for head in range(heads):
            first = (block * heads + head) * each
            own = parts[first : first + each]
            rows.append(jnp.concatenate([part[0] for part in own], axis=1))
            grad_keys = grad_keys + head_lanes(sum(part[1] for part in own), head, width)
            grad_values = grad_values + head_lanes(sum(part[2] for part in own), head, width)
        outs.append((jnp.transpose(jnp.concatenate(rows, axis=0)), grad_keys, grad_values))
    return outs


def one_hot(hits):
    return jnp.where(hits, 1.0, 0.0).astype(BF16)


def scatter_rows(out_ref, split, stride, slot_rows, loads, extra_ref=None, extra_at=0):
    blocks = out_ref.shape[0] // stride
    count = slot_rows.shape[1]
    first, second = slot_rows[0:1], slot_rows[1:2]

    def hits(slots, block):
        return (slots - block // split * stride) == places((stride, count), 0)

    def write(step, carry):
        pair = (2 * step, 2 * step + 1)
        if len(loads) == 1:
            chosen = one_hot(
                jnp.concatenate([hits(first, b) | hits(second, b) for b in pair], axis=0)
            )
            rows = dot(chosen, loads[0])
        else:
            rows = dot(
                one_hot(jnp.concatenate([hits(first, b) for b in pair], axis=0)), loads[0]
            ) + dot(one_hot(jnp.concatenate([hits(second, b) for b in pair], axis=0)), loads[1])
        if extra_ref is not None:
            line = places((stride, 1), 0)
            rows = jnp.concatenate(
                [
                    jnp.where(
                        line == extra_at,
                        extra_ref[pl.ds(b, 1), :],
                        rows[i * stride : (i + 1) * stride],
                    )
                    for i, b in enumerate(pair)
                ],
                axis=0,
            )
        at = step * 2 * stride if blocks <= 16 else pl.multiple_of(step * 2 * stride, 16)
        out_ref[pl.ds(at, 2 * stride), :] = rows.astype(BF16)
        return carry

    if blocks <= 16:
        for step in range(blocks // 2):
            write(step, 0)
    else:
        lax.fori_loop(0, blocks // 2, write, 0)


def slot_line(total, group, split, stride, rows, capacity):
    row = places((1, total), 1)
    at = row % rows
    return jnp.where(at < capacity, row // rows // split * stride + at, -1)


def gather_rows(slots, line, rows_ref, chunk):
    total = 0.0
    for at in range(0, rows_ref.shape[0], chunk):
        part = line[:, at : at + chunk]
        hits = slots[0] == part
        for more in slots[1:]:
            hits = hits | (more == part)
        total = total + dot(one_hot(hits), rows_ref[at : at + chunk, :])
    return total


def tables_kernel(strides, experts, scalars, *refs):
    own_ref, far_ref, seg_ref, *outs = refs
    count = seg_ref.shape[1]
    first = scalars[0] == 0
    after = one_hot(places((count, count), 0) < places((count, count), 1))
    seg_col = outs.pop()
    seg_col[...] = jnp.transpose(jnp.broadcast_to(seg_ref[...], (8, count)).astype(F32))[
        :, 0:1
    ].astype(I32)
    for layer, stride in enumerate(strides):
        pick_cols, pick_rows, slot_cols, slot_rows = outs[4 * layer : 4 * layer + 4]
        own = first if layer == 0 else jnp.logical_not(first)
        rows = jnp.where(own, own_ref[...], far_ref[...])
        pick_rows[...] = rows
        marks = [rows[k : k + 1, :] == places((experts, count), 0) for k in range(2)]
        ranks = dot(one_hot(marks[0] | marks[1]), after)
        wanted = []
        for k in range(2):
            rank = jnp.sum(jnp.where(marks[k], ranks, 0.0), axis=0, keepdims=True)
            wanted.append(rows[k : k + 1, :] * stride + rank.astype(I32))
            slot_rows[k : k + 1, :] = wanted[k]
        lines = [rows[0:1, :], rows[1:2, :], *wanted]
        lines = jnp.concatenate([line.astype(F32) for line in lines] * 2, axis=0)
        cols = jnp.transpose(lines).astype(I32)
        pick_cols[...] = cols[:, 0:2]
        slot_cols[...] = cols[:, 2:4]


def scatter_kernel(stride, split, slot_rows_ref, load_ref, out_ref):
    scatter_rows(out_ref, split, stride, slot_rows_ref[...], [load_ref[...]])


def unpack_rows(core, own_ref, other_ref, shard_rows, wide_ref, route_ref, gains_ref):
    pairs, rows, width = own_ref.shape
    group = 2 * pairs
    small = rows - shard_rows
    lines = []
    for i in range(group):
        own = core == i % 2
        wide_ref[i * shard_rows : (i + 1) * shard_rows, :] = jnp.where(
            own, own_ref[i // 2, :shard_rows, :], other_ref[i // 2, :shard_rows, :]
        )
        lines.append(
            jnp.where(
                own,
                own_ref[i // 2, shard_rows:, :].astype(F32),
                other_ref[i // 2, shard_rows:, :].astype(F32),
            )
        )
    lines = jnp.concatenate(lines, axis=0).astype(BF16)
    experts = route_ref.shape[1]
    each = width // group
    row, line = places((width, 1), 0), places((1, group * small), 1)
    spread = dot(one_hot(line == row // each * small), lines)
    lane = places((1, width), 1)
    spread = jnp.where(lane // experts == row % each, spread, 0.0).astype(BF16)
    fold = one_hot(places((width, 1), 0) % experts == places((1, experts), 1))
    route_ref[...] = dot(spread, fold).astype(BF16)
    each = 2 * width // group
    lane = places((1, 2 * width), 1)
    spread = dot(lines, one_hot(places((width, 1), 0) == lane % each))
    line = places((group * small, 1), 0)
    spread = jnp.where(line == lane // each * small + 1, spread, 0.0)
    gains = jnp.sum(spread, axis=0, keepdims=True)
    gains_ref[0:1, :] = gains[:, :width]
    gains_ref[1:2, :] = gains[:, width:]


def own_sums(core, x1, x2, o, dq, dk, dv, branch, dz, dgain, keep, give, wide):
    width, experts = x1.shape[1], dz.shape[1]
    pairs, rows, _ = keep.shape
    group = 2 * pairs
    shard_rows = 4 * width // group
    small = rows - shard_rows
    x1_turned = jnp.transpose(x1.astype(F32)).astype(BF16)
    for i, grads in enumerate((dq, dk, dv)):
        wide[i * width : (i + 1) * width, :] = dot(x1_turned, grads).astype(BF16)
    wide[3 * width :, :] = dot(jnp.transpose(o.astype(F32)).astype(BF16), branch).astype(BF16)
    route = dot(jnp.transpose(x2.astype(F32)).astype(BF16), dz).astype(BF16)
    each = width // group
    row, lane = places((width, 1), 0), places((1, width), 1)
    spread = dot(route, one_hot(places((experts, 1), 0) == lane % experts))
    spread = jnp.where(lane // experts == row % each, spread, 0.0).astype(BF16)
    line = places((group * small, 1), 0)
    lines = dot(one_hot(line == places((1, width), 1) // each * small), spread)
    each = 2 * width // group
    lane = places((1, 2 * width), 1)
    gains = jnp.concatenate([dgain[0:1, :], dgain[1:2, :]], axis=1)
    held = jnp.where(line == lane // each * small + 1, gains, 0.0).astype(BF16)
    lines = lines + dot(held, one_hot(places((1, width), 1) == places((2 * width, 1), 0) % each))
    for out, side in ((keep, core), (give, 1 - core)):
        for i in range(pairs):
            at = pl.multiple_of((2 * i + side) * shard_rows, 16)
            out[i, :shard_rows, :] = wide[pl.ds(at, shard_rows), :]
            out[i, shard_rows:, :] = jnp.where(
                side == 0,
                lines[2 * i * small : (2 * i + 1) * small],
                lines[(2 * i + 1) * small : (2 * i + 2) * small],
            ).astype(BF16)


def sums_kernel(scalars, *refs):
    *values, dgain, keep, give, wide = refs
    own_sums(scalars[1], *(ref[...] for ref in values), dgain, keep, give, wide)


def forward_kernel(cfg, combine, packed, scalars, *refs):
    stride, spare, chunk, capacity, strides, head_width, tile, split, shard_rows = cfg
    refs = list(refs)
    take = lambda number: [refs.pop(0) for _ in range(number)]
    if combine:
        hidden_in, returned, gates_in, slots_in = take(4)
    else:
        (tokens_ref,) = take(1)
    cos_ref, sin_ref, seg_col, seg_row = take(4)
    params = take(2 if packed else 3)
    pick_cols, pick_rows, slot_cols, slot_rows = take(4)
    send, q_out, k_out, v_out, o_out, h_out, x1_out, x2_out, gates_out = take(9)
    if combine:
        y_out, apart_out = take(2)
    if packed:
        wide, wr, gains = take(3)
        unpack_rows(scalars[1], *params, shard_rows, wide, wr, gains)
    else:
        wide, wr, gains = params
    (extra_ref,) = take(1)
    group = send.shape[0] // stride

    if combine:
        line = slot_line(returned.shape[0], group, split, strides[0], strides[0], capacity)
        first = gather_rows([slots_in[:, 0:1]], line, returned, chunk)
        second = gather_rows([slots_in[:, 1:2]], line, returned, chunk)
        whole = hidden_in[...] + gates_in[:, 0:1] * first + gates_in[:, 1:2] * second
        apart_out[...] = first - second
        leaving = whole.astype(BF16)
        y_out[...] = leaving
        entering = leaving.astype(F32)
    else:
        entering = tokens_ref[...].astype(F32)

    half = head_width // 2
    width = entering.shape[1]
    cosine, sine = wide_tables(cos_ref, sin_ref)
    normed, _ = norm_parts(entering)
    x1 = (normed * gains[0:1, :]).astype(BF16)
    x1_out[...] = x1
    q_all, k_all, v_all = (dot(x1, wide[i * width : (i + 1) * width, :]) for i in range(3))
    scale = 1.0 / math.sqrt(head_width)
    queries, keys, values = [], [], []
    for at in range(0, width, LANES):
        lanes = slice(at, at + LANES)
        q, k, v = q_all[:, lanes], k_all[:, lanes], v_all[:, lanes]
        q = (q * cosine + swap_halves(q, half) * sine).astype(BF16).astype(F32) * scale
        queries.append(q.astype(BF16))
        keys.append((k * cosine + swap_halves(k, half) * sine).astype(BF16))
        values.append(v.astype(BF16))
    for out, parts in ((q_out, queries), (k_out, keys), (v_out, values)):
        out[...] = jnp.concatenate(parts, axis=1)
    mixed = attend(queries, keys, values, seg_col[...], seg_row[...], head_width, tile)
    mixed = jnp.concatenate([part.astype(BF16) for part in mixed], axis=1)
    o_out[...] = mixed
    hidden = entering + dot(mixed, wide[3 * width :, :])
    h_out[...] = hidden
    normed, _ = norm_parts(hidden)
    x2 = (normed * gains[1:2, :]).astype(BF16)
    x2_out[...] = x2
    logits = dot(x2, wr[...])
    signs = [
        jnp.where(pick_cols[:, k : k + 1] == places(logits.shape, 1), logits, 0.0) for k in range(2)
    ]
    gap = jnp.sum(signs[0] - signs[1], axis=1, keepdims=True)
    gates_out[:, 0:1] = jax.nn.sigmoid(gap)
    gates_out[:, 1:2] = jax.nn.sigmoid(-gap)
    if spare:
        logits_row = dot(wr[...], x2, 0, 1)
        signs = [
            jnp.where(pick_rows[k : k + 1, :] == places(logits_row.shape, 0), logits_row, 0.0)
            for k in range(2)
        ]
        gap_row = jnp.sum(signs[0] - signs[1], axis=0, keepdims=True)
        high, low = 0.0, 0.0
        members = places((group, 1), 0) // split
        for k, gate in enumerate((jax.nn.sigmoid(gap_row), jax.nn.sigmoid(-gap_row))):
            rank = slot_cols[:, k : k + 1] - pick_cols[:, k : k + 1] * stride
            line = one_hot(rank == places((x2.shape[0], LANES), 1))
            held = jnp.where(members == pick_rows[k : k + 1, :], gate, 0.0)
            top = held.astype(BF16)
            rest = (held - top.astype(F32)).astype(BF16)
            high = high + dot(top, line)
            low = low + dot(rest, line)
        extra_ref[:, 0:LANES] = high
        extra_ref[:, LANES : 2 * LANES] = low
        extra_ref[:, 2 * LANES :] = jnp.zeros_like(extra_ref[:, 2 * LANES :])
        scatter_rows(send, split, stride, slot_rows[...], [x2], extra_ref, spare)
    else:
        scatter_rows(send, split, stride, slot_rows[...], [x2])


def row_tiles(total, rows):
    return [(at,) for at in range(0, total, rows)]


def expert_kernel(rows, x_ref, gate_ref, up_ref, down_ref, out_ref):
    def grown(at):
        x = x_ref[at : at + rows, :]
        return dot(x, gate_ref[...]), dot(x, up_ref[...])

    def folded(at, gate, up):
        return ((gate * jax.nn.sigmoid(gate) * up).astype(BF16),)

    def out(at, hidden):
        out_ref[at : at + rows, :] = dot(hidden, down_ref[...]).astype(BF16)
        return ()

    staged(row_tiles(x_ref.shape[0], rows), grown, folded, out)


def expert_pull_kernel(
    rows, stride, spare, x_ref, gate_ref, up_ref, g_ref, down_ref, dx_ref, act_ref, dgate_ref, dup_ref
):
    def grown(at):
        x = x_ref[at : at + rows, :]
        gate, up = dot(x, gate_ref[...]), dot(x, up_ref[...])
        return gate, up, dot(g_ref[at : at + rows, :], down_ref[...], 1, 1)

    def folded(at, gate, up, grad):
        sigmoid = jax.nn.sigmoid(gate)
        silu = gate * sigmoid
        act = (silu * up).astype(BF16)
        dup = (grad * silu).astype(BF16)
        dgate = (grad * up * (sigmoid + silu * (1.0 - sigmoid))).astype(BF16)
        for ref, value in ((act_ref, act), (dup_ref, dup), (dgate_ref, dgate)):
            ref[at : at + rows, :] = value
        inner = jnp.sum(grad * act.astype(F32), axis=1, keepdims=True) if spare else None
        return dgate, dup, inner

    def out(at, dgate, dup, inner):
        dx = dot(dgate, gate_ref[...], 1, 1) + dot(dup, up_ref[...], 1, 1)
        if spare:
            line = places((stride, 1), 0)
            eye = places((stride, LANES), 0) == places((stride, LANES), 1)
            blocks = []
            for top in range(0, rows, stride):
                row = jnp.sum(
                    jnp.where(eye, inner[top : top + stride], 0.0), axis=0, keepdims=True
                )
                high = row.astype(BF16).astype(F32)
                extra = jnp.concatenate(
                    [high, row - high, jnp.zeros((1, dx.shape[1] - 2 * LANES), F32)], axis=1
                )
                blocks.append(jnp.where(line == spare, extra, dx[top : top + stride]))
            dx = jnp.concatenate(blocks, axis=0)
        dx_ref[at : at + rows, :] = dx.astype(BF16)
        return ()

    staged(row_tiles(x_ref.shape[0], rows), grown, folded, out)


def down_kernel(rows, stride, out_stride, act_ref, down_ref, out_ref):
    to = 0
    for (at,) in row_tiles(act_ref.shape[0], rows):
        result = dot(act_ref[at : at + rows, :], down_ref[...])
        kept = [result[top : top + out_stride] for top in range(0, rows, stride)]
        kept = jnp.concatenate(kept, axis=0).astype(BF16)
        out_ref[to : to + kept.shape[0], :] = kept
        to += kept.shape[0]


def finish_kernel(cfg, hidden, returned, gates, slots, out_ref):
    stride, rows, capacity, chunk, split = cfg
    total = returned.shape[0]
    line = slot_line(total, total // rows, split, stride, rows, capacity)
    first = gather_rows([slots[:, 0:1]], line, returned, chunk)
    second = gather_rows([slots[:, 1:2]], line, returned, chunk)
    out_ref[...] = (hidden[...] + gates[:, 0:1] * first + gates[:, 1:2] * second).astype(BF16)


def backward_kernel(cfg, top, closing, *refs):
    stride, spare, chunk, capacity, next_stride, head_width, tile, split = cfg
    refs = list(refs)
    take = lambda number: [refs.pop(0) for _ in range(number)]
    if closing:
        scalars, o_ref = take(2)
    returned, grad_top, gates, pick_cols, slot_cols = take(5)
    apart = None if top else take(1)[0]
    enter_ref, hidden_ref, q_ref, k_ref, v_ref, cos_ref, sin_ref, seg_col, seg_row = take(9)
    wide, wr, gains = take(3)
    if not closing:
        next_gates, next_slots = take(2)
    grad_out, low_out = take(2)
    if closing:
        keep, give, dgain_out, wide_sums = take(4)
    else:
        dq_out, dk_out, dv_out, branch_out, dz_out, dgain_out, send = take(7)

    group = returned.shape[0] // stride
    line = slot_line(returned.shape[0], group, split, stride, stride, capacity)
    width = wide.shape[1]
    grad_y = grad_top[...].astype(F32)
    c1, c2 = gates[:, 0:1], gates[:, 1:2]
    if top:
        parts = [
            gather_rows([slot_cols[:, k : k + 1]], line, returned, chunk) for k in range(2)
        ]
        dx2 = c1 * parts[0] + c2 * parts[1]
        lines = one_hot(
            places((group, returned.shape[0]), 1)
            == places((group, returned.shape[0]), 0) * stride + spare
        )
        extra = dot(lines, returned[...]).astype(BF16)
        inner = []
        for k in range(2):
            pick = pick_cols[:, k : k + 1]
            held = dot(one_hot(pick == places((1, group), 1) // split), extra)
            held = held[:, 0:LANES] + held[:, LANES : 2 * LANES]
            rank = slot_cols[:, k : k + 1] - pick * stride
            inner.append(
                jnp.sum(
                    jnp.where(rank == places(held.shape, 1), held, 0.0), axis=1, keepdims=True
                )
            )
        apart_grad = inner[0] - inner[1]
    else:
        dx2 = gather_rows([slot_cols[:, 0:1], slot_cols[:, 1:2]], line, returned, chunk)
        apart_grad = jnp.sum(grad_y * apart[...], axis=1, keepdims=True)
    grad_gap = apart_grad * c1 * c2
    ids = places((grad_y.shape[0], wr.shape[1]), 1)
    dz = (
        jnp.where(pick_cols[:, 0:1] == ids, grad_gap, 0.0)
        - jnp.where(pick_cols[:, 1:2] == ids, grad_gap, 0.0)
    ).astype(BF16)
    if not closing:
        dz_out[...] = dz
    dx2 = dx2 + dot(dz, wr[...], 1, 1)
    normed, inverse = norm_parts(hidden_ref[...])
    x2 = (normed * gains[1:2, :]).astype(BF16)
    middle, grad_gain = norm_pull(dx2, normed, inverse, gains[1:2, :])
    dgain_out[1:2, :] = grad_gain
    grad_hidden = grad_y + middle
    branch = grad_hidden.astype(BF16)
    if not closing:
        branch_out[...] = branch
    grad_mixed = dot(branch, wide[3 * width :, :], 1, 1).astype(BF16)

    half = head_width // 2
    cosine, sine = wide_tables(cos_ref, sin_ref)
    scale = 1.0 / math.sqrt(head_width)
    blocks = [slice(at, at + LANES) for at in range(0, width, LANES)]
    pulled = attend_pull(
        *([ref[:, lanes] for lanes in blocks] for ref in (q_ref, k_ref, v_ref)),
        [grad_mixed[:, lanes] for lanes in blocks],
        seg_col[...],
        seg_row[...],
        head_width,
        tile,
    )
    turned = [[], [], []]
    for dq, dk, dv in pulled:
        dq = dq * scale
        turned[0].append((dq * cosine - swap_halves(dq, half) * sine).astype(BF16))
        turned[1].append((dk * cosine - swap_halves(dk, half) * sine).astype(BF16))
        turned[2].append(dv.astype(BF16))
    dq, dk, dv = (jnp.concatenate(parts, axis=1) for parts in turned)
    dx1 = (
        dot(dq, wide[:width, :], 1, 1)
        + dot(dk, wide[width : 2 * width, :], 1, 1)
        + dot(dv, wide[2 * width : 3 * width, :], 1, 1)
    )
    normed, inverse = norm_parts(enter_ref[...].astype(F32))
    lower, grad_gain = norm_pull(dx1, normed, inverse, gains[0:1, :])
    dgain_out[0:1, :] = grad_gain
    grad_enter = grad_hidden + lower
    grad_out[...] = grad_enter
    rounded = grad_enter.astype(BF16)
    low_out[...] = rounded
    if closing:
        x1 = (normed * gains[0:1, :]).astype(BF16)
        own_sums(
            scalars[1], x1, x2, o_ref[...], dq, dk, dv, branch, dz, dgain_out, keep, give, wide_sums
        )
    else:
        dq_out[...], dk_out[...], dv_out[...] = dq, dk, dv
        loads = [(next_gates[:, k : k + 1] * rounded.astype(F32)).astype(BF16) for k in range(2)]
        scatter_rows(send, split, next_stride, next_slots[...], loads)


def per_device(
    tokens, segments, routes, grad_top, w_attn, norm_gains, w_route, w_gate, w_up, w_down
):
    section = lax.axis_index("section")
    place = lax.axis_index("dp")
    group = lax.axis_size("dp")
    half = group // 2
    micro_count, rows_local, length, width = tokens.shape
    count = rows_local * length
    shard_rows = w_attn.shape[1]
    route_shard, gain_shard = w_route.shape[1], norm_gains.shape[1]
    experts = route_shard * group // width
    split = group // experts
    capacity = 9 * count // (4 * experts)
    head_width = width // HEADS
    half_width = head_width // 2
    strides = (round_up(capacity, 8), round_up(capacity + 1, 8))
    spares = (0, capacity)
    sizes = tuple(group * stride for stride in strides)
    chunks = tuple(min(size, 16 * stride) for size, stride in zip(sizes, strides))
    tile = min(512, count)
    aligned = shard_rows % 16 == 0
    hidden_units = w_gate.shape[-1]

    fence = lax.optimization_barrier
    to_second, to_first = ((0, 1),), ((1, 0),)

    def across(array, pairs=((0, 1), (1, 0))):
        return lax.ppermute(array, "section", list(pairs))

    def round_dp(array, bit):
        return lax.ppermute(array, "dp", [(i, i ^ bit) for i in range(group)])

    scalars = jnp.stack([section, place % 2]).astype(I32)

    small_rows = 8

    def wide_row(row):
        return jnp.pad(row, ((0, 0), (0, width - row.shape[1])))

    own_pack = jnp.concatenate(
        [
            w_attn[0],
            wide_row(w_route),
            wide_row(norm_gains),
            jnp.zeros((small_rows - 2, width), BF16),
        ]
    )
    far_pack = across(own_pack)
    packs = (
        jnp.where(section == 0, own_pack, far_pack),
        jnp.where(section == 0, far_pack, own_pack),
    )

    def doubled(held, bit):
        return merged(held, round_dp(held, bit), bit)

    def merged(held, other, bit):
        high = (place // bit) % 2 == 1
        return jnp.where(
            high, jnp.stack([other, held], axis=1), jnp.stack([held, other], axis=1)
        ).reshape(-1, *held.shape[1:])

    bits = [group >> step for step in range(1, group.bit_length())]

    def unpack(held):
        other = round_dp(held, 1)
        if aligned:
            return [held, other]
        full = merged(held, other, 1)
        route = full[:, shard_rows, :route_shard].reshape(width, experts)
        gain = full[:, shard_rows + 1, :gain_shard].reshape(2, width).astype(F32)
        return [full[:, :shard_rows].reshape(4 * width, width), route, gain]

    def exchange(rows):
        blocks = rows.reshape(group, -1, width)
        moved = lax.all_to_all(blocks, "dp", split_axis=0, concat_axis=0, tiled=True)
        return moved.reshape(rows.shape)

    def to_owner(array, layer):
        return across(array.astype(BF16), ((1 - layer, layer),))

    own_experts = (w_gate[0, 0], w_up[0, 0], w_down[0, 0])

    def own_rows(array):
        return lax.dynamic_index_in_dim(array, section, 0, keepdims=False).reshape(count, width)

    own_routes = lax.dynamic_index_in_dim(routes[0], section, 0, keepdims=False)
    far_routes = lax.dynamic_index_in_dim(routes[0], 1 - section, 0, keepdims=False)
    own_routes, far_routes = own_routes.reshape(count, 2).T, far_routes.reshape(count, 2).T
    far_routes = across(tie(far_routes, far_pack))
    offset = jnp.arange(rows_local, dtype=I32)[:, None] * length
    segment = (lax.dynamic_index_in_dim(segments, section, 0, keepdims=False) + offset).reshape(count)
    firsts = jnp.sum((segment[:, None] > segment[None, :]).astype(I32), axis=1)
    offsets = (jnp.arange(count, dtype=I32) - firsts).astype(F32)
    freqs = jnp.exp(
        jnp.arange(half_width, dtype=F32) * (-2.0 * math.log(10000.0) / head_width)
    )
    angles = offsets[:, None] * freqs
    seg_row = segment[None, :]
    tables_out = [((count, 2), I32), ((2, count), I32)] * 4 + [((count, 1), I32)]
    *tables, seg_col = call(
        functools.partial(tables_kernel, strides, experts),
        tables_out,
        [scalars, own_routes, far_routes, seg_row],
        "tables",
        2 * 2 * count * count * experts,
        scalars=(0,),
    )
    pick_cols, pick_rows, slot_cols, slot_rows = (tables[i::4] for i in range(4))

    tokens_flops = 2 * count * width
    attn_flops = tokens_flops * (4 * width + 2 * count * (LANES // head_width) * 2)
    move_flops = [tokens_flops * size for size in sizes]
    expert_flops = [2 * size * width * hidden_units for size in sizes]

    def block_rows(layer):
        blocks = 1
        while 2 * blocks * strides[layer] <= 384 and group % (2 * blocks) == 0:
            blocks *= 2
        return blocks * strides[layer]

    def forward(layer, lead, combine, params):
        outs = [((sizes[layer], width), BF16)]
        outs += [((count, width), BF16)] * 4
        outs += [((count, width), F32), ((count, width), BF16), ((count, width), BF16)]
        outs += [((count, 2), F32)]
        if combine:
            outs += [((count, width), BF16), ((count, width), F32)]
        if aligned:
            outs += [((4 * width, width), BF16), ((width, experts), BF16), ((2, width), F32)]
        cfg = (strides[layer], spares[layer], chunks[0], capacity, strides, head_width, tile)
        cfg += (split, shard_rows)
        results = call(
            functools.partial(forward_kernel, cfg, combine, aligned),
            outs,
            [scalars, *lead, cosine, sine, seg_col, seg_row, *params]
            + [pick_cols[layer], pick_rows[layer], slot_cols[layer], slot_rows[layer]],
            f"layer{layer}_forward",
            attn_flops + move_flops[layer] * (3 if combine else 1),
            scratch=[pltpu.VMEM((group, width), F32)],
            scalars=(0,),
        )
        return results if aligned else [*results, *params]

    def backward(layer, args):
        top, closing = layer == 1, layer == 0 and aligned
        rows, line = ((count, width), BF16), ((2, width), F32)
        outs = [((count, width), F32), rows]
        scratch = []
        if closing:
            outs += [((half, shard_rows + small_rows, width), BF16)] * 2
            scratch = [pltpu.VMEM((2, width), F32), pltpu.VMEM((4 * width, width), BF16)]
        else:
            outs += [rows] * 4 + [((count, experts), BF16), line, ((sizes[0], width), BF16)]
        cfg = (strides[layer], spares[layer], chunks[layer], capacity, strides[0], head_width, tile)
        return call(
            functools.partial(backward_kernel, cfg + (split,), top, closing),
            outs,
            args,
            f"layer{layer}_backward",
            3 * attn_flops + move_flops[layer] * (4 if top else 1),
            scratch=scratch,
            scalars=(0,) if closing else (),
        )

    def pulled(rows):
        return jnp.einsum("nd,nf->df", *rows, preferred_element_type=F32)

    def by_core(x1, x2, o, dq, dk, dv, branch, dz, dgain):
        if aligned:
            block = ((half, shard_rows + small_rows, width), BF16)
            return call(
                sums_kernel,
                [block, block],
                [scalars, x1, x2, o, dq, dk, dv, branch, dz, dgain],
                "own_sums",
                4 * tokens_flops * width,
                scratch=[pltpu.VMEM((4 * width, width), BF16)],
                scalars=(0,),
            )
        matrix = jnp.concatenate(
            [pulled((x1, dq)), pulled((x1, dk)), pulled((x1, dv)), pulled((o, branch))], axis=0
        )
        route = pulled((x2, dz)).reshape(group, 1, route_shard)
        gain = dgain.reshape(group, 1, gain_shard)
        blocks = jnp.concatenate(
            [
                matrix.reshape(group, shard_rows, width),
                jnp.pad(route, ((0, 0), (0, 0), (0, width - route_shard))),
                jnp.pad(gain, ((0, 0), (0, 0), (0, width - gain_shard))),
                jnp.zeros((group, small_rows - 2, width), F32),
            ],
            axis=1,
        ).astype(BF16)
        pairs = blocks.reshape(half, 2, *blocks.shape[1:])
        return (
            lax.dynamic_index_in_dim(pairs, place % 2, 1, keepdims=False),
            lax.dynamic_index_in_dim(pairs, 1 - place % 2, 1, keepdims=False),
        )

    def paired(keep, give):
        return added(keep, round_dp(give, 1))

    def spread(blocks):
        sets = [[2 * chip + c for chip in range(half)] for c in range(2)]
        return lax.all_to_all(
            blocks, "dp", split_axis=0, concat_axis=0, tiled=True, axis_index_groups=sets
        )

    def halved(blocks, bit):
        pairs = blocks.reshape(-1, 2, *blocks.shape[1:])
        own = (place // 2 // bit) % 2
        keep = lax.dynamic_index_in_dim(pairs, own, 1, keepdims=False)
        give = lax.dynamic_index_in_dim(pairs, 1 - own, 1, keepdims=False)
        return keep, round_dp(give, 2 * bit)

    def added(keep, got):
        return (keep.astype(F32) + got.astype(F32)).astype(BF16)

    def summed(moved):
        return jnp.sum(moved.astype(F32), axis=0)

    def by_micro(first, far_first, second, far_second):
        return jnp.where(
            section == 0,
            jnp.stack([first, far_first.astype(first.dtype)]),
            jnp.stack([far_second.astype(second.dtype), second]),
        ).reshape(1, micro_count, rows_local, length, width)

    def joined(first, far_first, second, far_second):
        whole = jnp.where(
            section == 0, first + far_first.astype(F32), second + far_second.astype(F32)
        )
        return whole[None, None]

    def hosted(index, far):
        own = own_experts[index]
        return jnp.where(section == 0, own, far), jnp.where(section == 0, far, own)

    other = round_dp(packs[0][None], bits[0])
    other, slot_rows = fence((other, slot_rows))
    gathered = merged(packs[0][None], other, bits[0])
    other = round_dp(gathered, bits[1])
    tokens, grad_top = tie((tokens, grad_top), gathered)
    token_rows, top_rows = own_rows(tokens), own_rows(grad_top)
    (top_send,) = call(
        functools.partial(scatter_kernel, strides[1], split),
        [((sizes[1], width), BF16)],
        [slot_rows[1], top_rows],
        "top_send",
        move_flops[1],
    )
    other, top_send = fence((other, top_send))
    gathered = merged(gathered, other, bits[1])
    other = round_dp(gathered, bits[2])
    angles = tie(angles, gathered)
    cosine, sine = jnp.cos(angles), jnp.sin(angles)
    held1 = packs[1][None]
    other1 = round_dp(tie(held1, gathered), bits[0])
    other, cosine, sine, other1 = fence((other, cosine, sine, other1))
    far_gate = across(tie(own_experts[0], far_pack))
    top_received = exchange(tie(top_send, other, far_gate))
    gathered = merged(gathered, other, bits[2])
    for bit in bits[3:-1]:
        gathered = doubled(gathered, bit)

    far_up = across(tie(own_experts[1], gathered))
    results = forward(0, [token_rows], False, unpack(gathered))
    send0, q0, k0, v0, o0, h0, x1_0, x2_0, gates0, *params0 = results
    send0, far_up, top_received = fence((send0, far_up, top_received))
    received0 = exchange(send0)
    held1 = merged(held1, tie(other1, send0), bits[0])
    other1 = round_dp(held1, bits[1])
    far_down = across(tie(own_experts[2], send0))
    gates_up_down = [hosted(i, far) for i, far in enumerate((far_gate, far_up, far_down))]
    experts0, experts1 = zip(*gates_up_down)
    received0, experts0, experts1, other1 = fence((received0, experts0, experts1, other1))
    held1 = merged(held1, other1, bits[1])
    (result0,) = call(
        functools.partial(expert_kernel, block_rows(0)),
        [((sizes[0], width), BF16)],
        [received0, *experts0],
        "layer0_experts",
        3 * expert_flops[0],
    )
    result0, held1 = fence((result0, held1))
    for bit in bits[2:-1]:
        held1 = doubled(held1, bit)
    params1 = unpack(held1)
    returned0 = exchange(result0)

    returned0, params1 = fence((returned0, params1))
    results = forward(1, [h0, returned0, gates0, slot_cols[0]], True, params1)
    send1, q1, k1, v1, o1, h1, x1_1, x2_1, gates1, y0, apart0, *params1 = results
    send1, y0 = fence((send1, y0))
    received1 = exchange(send1)
    far_y0 = across(y0, to_first)
    received1, far_y0 = fence((received1, far_y0))

    hidden_out = lambda layer: ((sizes[layer], hidden_units), BF16)
    dx1_send, act1, dgate1, dup1 = call(
        functools.partial(expert_pull_kernel, block_rows(1), strides[1], spares[1]),
        [((sizes[1], width), BF16), hidden_out(1), hidden_out(1), hidden_out(1)],
        [received1, *experts1[:2], top_received, experts1[2]],
        "layer1_experts",
        5 * expert_flops[1],
    )
    dx1_send, act1, dgate1, dup1 = fence((dx1_send, act1, dgate1, dup1))
    dx1_back = exchange(dx1_send)
    lines = received1.reshape(group, strides[1], width)[:, capacity].astype(F32)
    gate_slots = lines[:, :LANES] + lines[:, LANES : 2 * LANES]
    gate_slots = gate_slots[:, : strides[1]].reshape(sizes[1], 1)
    scaled = (received1.astype(F32) * gate_slots).astype(BF16)
    scaled_top = (top_received.astype(F32) * gate_slots).astype(BF16)
    gate1 = pulled((scaled, dgate1))
    far_gate1 = to_owner(gate1, 1)
    (result1,) = call(
        functools.partial(down_kernel, block_rows(1), strides[1], strides[0]),
        [((sizes[0], width), BF16)],
        [act1, experts1[2]],
        "layer1_down",
        expert_flops[1],
    )
    up1, down1 = pulled((scaled, dup1)), pulled((act1, scaled_top))
    dx1_back, result1, gate1, up1, down1, far_gate1 = fence(
        (dx1_back, result1, gate1, up1, down1, far_gate1)
    )

    returned1 = exchange(result1)
    results = backward(
        1,
        [dx1_back, top_rows, gates1, pick_cols[1], slot_cols[1], y0, h1, q1, k1, v1]
        + [cosine, sine, seg_col, seg_row, *params1, gates0, slot_rows[0]],
    )
    results, returned1 = fence((results, returned1))
    grad1, low1, dq1, dk1, dv1, branch1, dz1, dgain1, dr0_send = results
    dr0 = exchange(dr0_send)
    far_up1 = to_owner(tie(up1, dr0_send), 1)
    blocks1 = paired(*by_core(x1_1, x2_1, o1, dq1, dk1, dv1, branch1, dz1, dgain1))
    chip_bits = [1 << step for step in range(half.bit_length() - 1)]
    keep1, got1 = halved(blocks1, chip_bits[0])
    (y1,) = call(
        functools.partial(finish_kernel, (strides[1], strides[0], capacity, chunks[0], split)),
        [((count, width), BF16)],
        [h1, returned1, gates1, slot_cols[1]],
        "layer1_out",
        2 * move_flops[1],
    )
    dr0, y1, far_up1 = fence((dr0, y1, far_up1))

    dx0_send, act0, dgate0, dup0 = call(
        functools.partial(expert_pull_kernel, block_rows(0), strides[0], 0),
        [((sizes[0], width), BF16), hidden_out(0), hidden_out(0), hidden_out(0)],
        [received0, *experts0[:2], dr0, experts0[2]],
        "layer0_experts_pull",
        5 * expert_flops[0],
    )
    dx0_send, act0, dgate0, dup0 = fence((dx0_send, act0, dgate0, dup0))
    dx0_back = exchange(dx0_send)
    gate0 = pulled((received0, dgate0))
    far_gate0 = to_owner(gate0, 0)
    up0, down0 = pulled((received0, dup0)), pulled((act0, dr0))
    far_down1 = to_owner(tie(down1, dx0_send), 1)
    low_up0, low_down0 = up0.astype(BF16), down0.astype(BF16)
    keep1, got1 = tie((keep1, got1), dx0_send)
    for bit in chip_bits[1:-1]:
        keep1, got1 = halved(added(keep1, got1), bit)
    dx0_back, gate0, up0, down0, low_up0, low_down0, keep1, got1 = fence(
        (dx0_back, gate0, up0, down0, low_up0, low_down0, keep1, got1)
    )

    closing = [scalars, o0] if aligned else []
    results = backward(
        0,
        closing
        + [dx0_back, low1, gates0, pick_cols[0], slot_cols[0], apart0, token_rows, h0, q0, k0, v0]
        + [cosine, sine, seg_col, seg_row, *params0]
        + ([] if aligned else [gates0, slot_rows[0]]),
    )
    far_up0 = to_owner(low_up0, 0)
    results, far_gate0, far_down1 = fence((results, far_gate0, far_down1))
    if aligned:
        grad0, low0, keep, give = results
    else:
        grad0, low0, dq0, dk0, dv0, branch0, dz0, dgain0, _ = results
        keep, give = by_core(x1_0, x2_0, o0, dq0, dk0, dv0, branch0, dz0, dgain0)

    low_up0, low_down0 = tie((low_up0, low_down0), grad0)
    far_up0 = to_owner(low_up0, 0)
    far_down0 = to_owner(low_down0, 0)
    blocks0 = paired(keep, give)
    moved0 = spread(blocks0)
    low0, low1, y0, y1, keep1, got1 = tie((low0, low1, y0, y1, keep1, got1), blocks0)
    far_y1 = across(y1, to_second)
    far_low = across(jnp.where(section == 0, low1, low0))
    keep1, got1 = halved(added(keep1, got1), chip_bits[-1])
    sums1 = keep1[0].astype(F32) + got1[0].astype(F32)
    gate0, up0, down0, gate1, up1, down1 = tie((gate0, up0, down0, gate1, up1, down1), blocks0)
    gate_out = joined(gate0, far_gate0, gate1, far_gate1)
    up_out = joined(up0, far_up0, up1, far_up1)
    down_own = jnp.where(section == 0, down0, down1 + far_down1.astype(F32))
    moved0, gate_out, up_out, down_own = fence((moved0, gate_out, up_out, down_own))
    sums0 = summed(moved0)
    far_sums0 = across(sums0, to_first)
    far_low, far_y1, sums1, far_down0 = tie((far_low, far_y1, sums1, far_down0), sums0)
    far_sums1 = across(sums1, to_second)
    input_grads = by_micro(grad0, far_low, grad1, far_low)
    layer_out = by_micro(y0, far_y0, y1, far_y1)
    down_out = (down_own + far_down0.astype(F32))[None, None]
    total = jnp.where(section == 0, sums0 + far_sums0, sums1 + far_sums1)
    return (
        layer_out,
        input_grads,
        total[:shard_rows][None],
        total[shard_rows + 1, :gain_shard][None],
        total[shard_rows, :route_shard][None],
        gate_out,
        up_out,
        down_out,
    )


def solution(mesh):
    in_specs = (
        P(None, "dp", None, None),
        P(None, "dp", None),
        P("section", None, "dp", None, None),
        P(None, "dp", None, None),
        P("section", "dp", None),
        P("section", "dp"),
        P("section", "dp"),
        P("section", "dp", None, None),
        P("section", "dp", None, None),
        P("section", "dp", None, None),
    )
    out_specs = (
        P("section", None, "dp", None, None),
        P("section", None, "dp", None, None),
        P("section", "dp", None),
        P("section", "dp"),
        P("section", "dp"),
        P("section", "dp", None, None),
        P("section", "dp", None, None),
        P("section", "dp", None, None),
    )
    return jax.shard_map(
        per_device, mesh=mesh, in_specs=in_specs, out_specs=out_specs, check_vma=False
    )
```

```python
import functools
import math

import jax
import jax.numpy as jnp
from jax import lax
from jax.experimental import pallas as pl
from jax.experimental.pallas import tpu as pltpu
from jax.sharding import PartitionSpec as P

HEADS = 6
NORM_EPSILON = 1e-05
LANES = 128
F32 = jnp.float32
BF16 = jnp.bfloat16
I32 = jnp.int32
VMEM_LIMIT = 56 * 1024 * 1024


def dot(left, right, left_dim=1, right_dim=0):
    return lax.dot_general(
        left, right, (((left_dim,), (right_dim,)), ((), ())), preferred_element_type=F32
    )


def places(shape, dim):
    return lax.broadcasted_iota(I32, shape, dim)


def tie(value, *others):
    return lax.optimization_barrier((value, others))[0]


def round_up(value, step):
    return -(-value // step) * step


def call(body, outs, args, name, flops, scratch=(), scalars=()):
    shapes = [jax.ShapeDtypeStruct(shape, dtype) for shape, dtype in outs]
    moved = sum(math.prod(a.shape) * a.dtype.itemsize for a in list(args) + shapes)
    return pl.pallas_call(
        body,
        out_shape=shapes,
        in_specs=[
            pl.BlockSpec(memory_space=pltpu.SMEM if index in scalars else pltpu.VMEM)
            for index in range(len(args))
        ],
        out_specs=[pl.BlockSpec(memory_space=pltpu.VMEM) for _ in shapes],
        scratch_shapes=list(scratch),
        compiler_params=pltpu.CompilerParams(vmem_limit_bytes=VMEM_LIMIT),
        cost_estimate=pl.CostEstimate(flops=flops, bytes_accessed=moved, transcendentals=0),
        name=name,
    )(*args)


def norm_parts(values):
    inverse = lax.rsqrt(jnp.mean(values * values, axis=-1, keepdims=True) + NORM_EPSILON)
    return values * inverse, inverse


def norm_pull(grad_out, normed, inverse, gain):
    grad_gain = jnp.sum(grad_out * normed, axis=0, keepdims=True)
    grad_normed = grad_out * gain
    inner = jnp.mean(grad_normed * normed, axis=-1, keepdims=True)
    return inverse * (grad_normed - normed * inner), grad_gain


def swap_halves(values, half):
    low = places((1, LANES), 1) % (2 * half) < half
    return jnp.where(
        low, pltpu.roll(values, LANES - half, 1), pltpu.roll(values, half, 1)
    )


def wide_tables(cos_ref, sin_ref):
    half = cos_ref.shape[1]
    cosine = jnp.concatenate([cos_ref[...]] * (LANES // half), axis=1)
    sine = jnp.concatenate([sin_ref[...]] * (LANES // half), axis=1)
    return cosine, jnp.where(places((1, LANES), 1) % (2 * half) < half, -sine, sine)


def head_lanes(values, head, width):
    lane = places((1, LANES), 1)
    return jnp.where((lane >= head * width) & (lane < (head + 1) * width), values, 0.0)


def staged(jobs, *stages):
    values = {}
    for step in range(len(jobs) + len(stages) - 1):
        for late, stage in enumerate(stages):
            index = step - late
            if 0 <= index < len(jobs):
                values[index] = stage(*jobs[index], *values.get(index, ()))
    return [values[index] for index in range(len(jobs))]


def attend(queries, keys, values, seg_col, seg_row, width, tile):
    count = queries[0].shape[0]
    heads = LANES // width
    turned = [jnp.transpose(v.astype(F32)).astype(BF16) for v in values]
    jobs = [
        (block, head, at)
        for block in range(len(queries))
        for head in range(heads)
        for at in range(0, count, tile)
    ]

    def scores(block, head, at):
        own = head_lanes(keys[block].astype(F32), head, width).astype(BF16)
        return (dot(own, queries[block][at : at + tile], 1, 1),)

    def terms(block, head, at, score):
        score = jnp.where(seg_col == seg_row[:, at : at + tile], score, -1e30)
        term = jnp.exp(score - jnp.max(score, axis=0, keepdims=True))
        return ((term * (1.0 / jnp.sum(term, axis=0, keepdims=True))).astype(BF16),)

    def mixed(block, head, at, weights):
        return dot(turned[block][head * width : (head + 1) * width], weights)

    parts = staged(jobs, scores, terms, mixed)
    each = count // tile
    outs = []
    for block in range(len(queries)):
        rows = []
        for head in range(heads):
            first = (block * heads + head) * each
            rows.append(jnp.concatenate(parts[first : first + each], axis=1))
        outs.append(jnp.transpose(jnp.concatenate(rows, axis=0)))
    return outs


def attend_pull(queries, keys, values, grads, seg_col, seg_row, width, tile):
    count = queries[0].shape[0]
    heads = LANES // width
    turned = [jnp.transpose(k.astype(F32)).astype(BF16) for k in keys]
    jobs = [
        (block, head, at)
        for block in range(len(queries))
        for head in range(heads)
        for at in range(0, count, tile)
    ]

    def scores(block, head, at):
        own_keys = head_lanes(keys[block].astype(F32), head, width).astype(BF16)
        own_values = head_lanes(values[block].astype(F32), head, width).astype(BF16)
        return (
            dot(own_keys, queries[block][at : at + tile], 1, 1),
            dot(own_values, grads[block][at : at + tile], 1, 1),
        )

    def terms(block, head, at, score, pulled):
        score = jnp.where(seg_col == seg_row[:, at : at + tile], score, -1e30)
        term = jnp.exp(score - jnp.max(score, axis=0, keepdims=True))
        weights = term * (1.0 / jnp.sum(term, axis=0, keepdims=True))
        inner = jnp.sum(weights * pulled, axis=0, keepdims=True)
        return weights.astype(BF16), (weights * (pulled - inner)).astype(BF16)

    def mixed(block, head, at, weights, grad_scores):
        return (
            dot(turned[block][head * width : (head + 1) * width], grad_scores),
            dot(grad_scores, queries[block][at : at + tile]),
            dot(weights, grads[block][at : at + tile]),
        )

    parts = staged(jobs, scores, terms, mixed)
    each = count // tile
    outs = []
    for block in range(len(queries)):
        rows, grad_keys, grad_values = [], 0.0, 0.0
        for head in range(heads):
            first = (block * heads + head) * each
            own = parts[first : first + each]
            rows.append(jnp.concatenate([part[0] for part in own], axis=1))
            grad_keys = grad_keys + head_lanes(sum(part[1] for part in own), head, width)
            grad_values = grad_values + head_lanes(sum(part[2] for part in own), head, width)
        outs.append((jnp.transpose(jnp.concatenate(rows, axis=0)), grad_keys, grad_values))
    return outs


def one_hot(hits):
    return jnp.where(hits, 1.0, 0.0).astype(BF16)


def scatter_rows(out_ref, split, stride, slot_rows, loads, extra_ref=None, extra_at=0):
    blocks = out_ref.shape[0] // stride
    count = slot_rows.shape[1]
    first, second = slot_rows[0:1], slot_rows[1:2]

    def hits(slots, block):
        return (slots - block // split * stride) == places((stride, count), 0)

    def write(step, carry):
        pair = (2 * step, 2 * step + 1)
        if len(loads) == 1:
            chosen = one_hot(
                jnp.concatenate([hits(first, b) | hits(second, b) for b in pair], axis=0)
            )
            rows = dot(chosen, loads[0])
        else:
            rows = dot(
                one_hot(jnp.concatenate([hits(first, b) for b in pair], axis=0)), loads[0]
            ) + dot(one_hot(jnp.concatenate([hits(second, b) for b in pair], axis=0)), loads[1])
        if extra_ref is not None:
            line = places((stride, 1), 0)
            rows = jnp.concatenate(
                [
                    jnp.where(
                        line == extra_at,
                        extra_ref[pl.ds(b, 1), :],
                        rows[i * stride : (i + 1) * stride],
                    )
                    for i, b in enumerate(pair)
                ],
                axis=0,
            )
        at = step * 2 * stride if blocks <= 16 else pl.multiple_of(step * 2 * stride, 16)
        out_ref[pl.ds(at, 2 * stride), :] = rows.astype(BF16)
        return carry

    if blocks <= 16:
        for step in range(blocks // 2):
            write(step, 0)
    else:
        lax.fori_loop(0, blocks // 2, write, 0)


def slot_line(total, group, split, stride, rows, capacity):
    row = places((1, total), 1)
    at = row % rows
    return jnp.where(at < capacity, row // rows // split * stride + at, -1)


def gather_rows(slots, line, rows_ref, chunk):
    total = 0.0
    for at in range(0, rows_ref.shape[0], chunk):
        part = line[:, at : at + chunk]
        hits = slots[0] == part
        for more in slots[1:]:
            hits = hits | (more == part)
        total = total + dot(one_hot(hits), rows_ref[at : at + chunk, :])
    return total


def tables_kernel(strides, experts, scalars, *refs):
    own_ref, far_ref, seg_ref, *outs = refs
    count = seg_ref.shape[1]
    first = scalars[0] == 0
    after = one_hot(places((count, count), 0) < places((count, count), 1))
    seg_col = outs.pop()
    seg_col[...] = jnp.transpose(jnp.broadcast_to(seg_ref[...], (8, count)).astype(F32))[
        :, 0:1
    ].astype(I32)
    for layer, stride in enumerate(strides):
        pick_cols, pick_rows, slot_cols, slot_rows = outs[4 * layer : 4 * layer + 4]
        own = first if layer == 0 else jnp.logical_not(first)
        rows = jnp.where(own, own_ref[...], far_ref[...])
        pick_rows[...] = rows
        marks = [rows[k : k + 1, :] == places((experts, count), 0) for k in range(2)]
        ranks = dot(one_hot(marks[0] | marks[1]), after)
        wanted = []
        for k in range(2):
            rank = jnp.sum(jnp.where(marks[k], ranks, 0.0), axis=0, keepdims=True)
            wanted.append(rows[k : k + 1, :] * stride + rank.astype(I32))
            slot_rows[k : k + 1, :] = wanted[k]
        lines = [rows[0:1, :], rows[1:2, :], *wanted]
        lines = jnp.concatenate([line.astype(F32) for line in lines] * 2, axis=0)
        cols = jnp.transpose(lines).astype(I32)
        pick_cols[...] = cols[:, 0:2]
        slot_cols[...] = cols[:, 2:4]


def scatter_kernel(stride, split, slot_rows_ref, load_ref, out_ref):
    scatter_rows(out_ref, split, stride, slot_rows_ref[...], [load_ref[...]])


def unpack_rows(core, own_ref, other_ref, shard_rows, wide_ref, route_ref, gains_ref):
    pairs, rows, width = own_ref.shape
    group = 2 * pairs
    small = rows - shard_rows
    lines = []
    for i in range(group):
        own = core == i % 2
        wide_ref[i * shard_rows : (i + 1) * shard_rows, :] = jnp.where(
            own, own_ref[i // 2, :shard_rows, :], other_ref[i // 2, :shard_rows, :]
        )
        lines.append(
            jnp.where(
                own,
                own_ref[i // 2, shard_rows:, :].astype(F32),
                other_ref[i // 2, shard_rows:, :].astype(F32),
            )
        )
    lines = jnp.concatenate(lines, axis=0).astype(BF16)
    experts = route_ref.shape[1]
    each = width // group
    row, line = places((width, 1), 0), places((1, group * small), 1)
    spread = dot(one_hot(line == row // each * small), lines)
    lane = places((1, width), 1)
    spread = jnp.where(lane // experts == row % each, spread, 0.0).astype(BF16)
    fold = one_hot(places((width, 1), 0) % experts == places((1, experts), 1))
    route_ref[...] = dot(spread, fold).astype(BF16)
    each = 2 * width // group
    lane = places((1, 2 * width), 1)
    spread = dot(lines, one_hot(places((width, 1), 0) == lane % each))
    line = places((group * small, 1), 0)
    spread = jnp.where(line == lane // each * small + 1, spread, 0.0)
    gains = jnp.sum(spread, axis=0, keepdims=True)
    gains_ref[0:1, :] = gains[:, :width]
    gains_ref[1:2, :] = gains[:, width:]


def own_sums(core, x1, x2, o, dq, dk, dv, branch, dz, dgain, keep, give, wide):
    width, experts = x1.shape[1], dz.shape[1]
    pairs, rows, _ = keep.shape
    group = 2 * pairs
    shard_rows = 4 * width // group
    small = rows - shard_rows
    x1_turned = jnp.transpose(x1.astype(F32)).astype(BF16)
    for i, grads in enumerate((dq, dk, dv)):
        wide[i * width : (i + 1) * width, :] = dot(x1_turned, grads).astype(BF16)
    wide[3 * width :, :] = dot(jnp.transpose(o.astype(F32)).astype(BF16), branch).astype(BF16)
    route = dot(jnp.transpose(x2.astype(F32)).astype(BF16), dz).astype(BF16)
    each = width // group
    row, lane = places((width, 1), 0), places((1, width), 1)
    spread = dot(route, one_hot(places((experts, 1), 0) == lane % experts))
    spread = jnp.where(lane // experts == row % each, spread, 0.0).astype(BF16)
    line = places((group * small, 1), 0)
    lines = dot(one_hot(line == places((1, width), 1) // each * small), spread)
    each = 2 * width // group
    lane = places((1, 2 * width), 1)
    gains = jnp.concatenate([dgain[0:1, :], dgain[1:2, :]], axis=1)
    held = jnp.where(line == lane // each * small + 1, gains, 0.0).astype(BF16)
    lines = lines + dot(held, one_hot(places((1, width), 1) == places((2 * width, 1), 0) % each))
    for out, side in ((keep, core), (give, 1 - core)):
        for i in range(pairs):
            at = pl.multiple_of((2 * i + side) * shard_rows, 16)
            out[i, :shard_rows, :] = wide[pl.ds(at, shard_rows), :]
            out[i, shard_rows:, :] = jnp.where(
                side == 0,
                lines[2 * i * small : (2 * i + 1) * small],
                lines[(2 * i + 1) * small : (2 * i + 2) * small],
            ).astype(BF16)


def sums_kernel(scalars, *refs):
    *values, dgain, keep, give, wide = refs
    own_sums(scalars[1], *(ref[...] for ref in values), dgain, keep, give, wide)


def forward_kernel(cfg, combine, packed, scalars, *refs):
    stride, spare, chunk, capacity, strides, head_width, tile, split, shard_rows = cfg
    refs = list(refs)
    take = lambda number: [refs.pop(0) for _ in range(number)]
    if combine:
        hidden_in, returned, gates_in, slots_in = take(4)
    else:
        (tokens_ref,) = take(1)
    cos_ref, sin_ref, seg_col, seg_row = take(4)
    params = take(2 if packed else 3)
    pick_cols, pick_rows, slot_cols, slot_rows = take(4)
    send, q_out, k_out, v_out, o_out, h_out, x1_out, x2_out, gates_out = take(9)
    if combine:
        y_out, apart_out = take(2)
    if packed:
        wide, wr, gains = take(3)
        unpack_rows(scalars[1], *params, shard_rows, wide, wr, gains)
    else:
        wide, wr, gains = params
    (extra_ref,) = take(1)
    group = send.shape[0] // stride

    if combine:
        line = slot_line(returned.shape[0], group, split, strides[0], strides[0], capacity)
        first = gather_rows([slots_in[:, 0:1]], line, returned, chunk)
        second = gather_rows([slots_in[:, 1:2]], line, returned, chunk)
        whole = hidden_in[...] + gates_in[:, 0:1] * first + gates_in[:, 1:2] * second
        apart_out[...] = first - second
        leaving = whole.astype(BF16)
        y_out[...] = leaving
        entering = leaving.astype(F32)
    else:
        entering = tokens_ref[...].astype(F32)

    half = head_width // 2
    width = entering.shape[1]
    cosine, sine = wide_tables(cos_ref, sin_ref)
    normed, _ = norm_parts(entering)
    x1 = (normed * gains[0:1, :]).astype(BF16)
    x1_out[...] = x1
    q_all, k_all, v_all = (dot(x1, wide[i * width : (i + 1) * width, :]) for i in range(3))
    scale = 1.0 / math.sqrt(head_width)
    queries, keys, values = [], [], []
    for at in range(0, width, LANES):
        lanes = slice(at, at + LANES)
        q, k, v = q_all[:, lanes], k_all[:, lanes], v_all[:, lanes]
        q = (q * cosine + swap_halves(q, half) * sine).astype(BF16).astype(F32) * scale
        queries.append(q.astype(BF16))
        keys.append((k * cosine + swap_halves(k, half) * sine).astype(BF16))
        values.append(v.astype(BF16))
    for out, parts in ((q_out, queries), (k_out, keys), (v_out, values)):
        out[...] = jnp.concatenate(parts, axis=1)
    mixed = attend(queries, keys, values, seg_col[...], seg_row[...], head_width, tile)
    mixed = jnp.concatenate([part.astype(BF16) for part in mixed], axis=1)
    o_out[...] = mixed
    hidden = entering + dot(mixed, wide[3 * width :, :])
    h_out[...] = hidden
    normed, _ = norm_parts(hidden)
    x2 = (normed * gains[1:2, :]).astype(BF16)
    x2_out[...] = x2
    logits = dot(x2, wr[...])
    signs = [
        jnp.where(pick_cols[:, k : k + 1] == places(logits.shape, 1), logits, 0.0) for k in range(2)
    ]
    gap = jnp.sum(signs[0] - signs[1], axis=1, keepdims=True)
    gates_out[:, 0:1] = jax.nn.sigmoid(gap)
    gates_out[:, 1:2] = jax.nn.sigmoid(-gap)
    if spare:
        logits_row = dot(wr[...], x2, 0, 1)
        signs = [
            jnp.where(pick_rows[k : k + 1, :] == places(logits_row.shape, 0), logits_row, 0.0)
            for k in range(2)
        ]
        gap_row = jnp.sum(signs[0] - signs[1], axis=0, keepdims=True)
        high, low = 0.0, 0.0
        members = places((group, 1), 0) // split
        for k, gate in enumerate((jax.nn.sigmoid(gap_row), jax.nn.sigmoid(-gap_row))):
            rank = slot_cols[:, k : k + 1] - pick_cols[:, k : k + 1] * stride
            line = one_hot(rank == places((x2.shape[0], LANES), 1))
            held = jnp.where(members == pick_rows[k : k + 1, :], gate, 0.0)
            top = held.astype(BF16)
            rest = (held - top.astype(F32)).astype(BF16)
            high = high + dot(top, line)
            low = low + dot(rest, line)
        extra_ref[:, 0:LANES] = high
        extra_ref[:, LANES : 2 * LANES] = low
        extra_ref[:, 2 * LANES :] = jnp.zeros_like(extra_ref[:, 2 * LANES :])
        scatter_rows(send, split, stride, slot_rows[...], [x2], extra_ref, spare)
    else:
        scatter_rows(send, split, stride, slot_rows[...], [x2])


def row_tiles(total, rows):
    return [(at,) for at in range(0, total, rows)]


def expert_kernel(rows, x_ref, gate_ref, up_ref, down_ref, out_ref):
    def grown(at):
        x = x_ref[at : at + rows, :]
        return dot(x, gate_ref[...]), dot(x, up_ref[...])

    def folded(at, gate, up):
        return ((gate * jax.nn.sigmoid(gate) * up).astype(BF16),)

    def out(at, hidden):
        out_ref[at : at + rows, :] = dot(hidden, down_ref[...]).astype(BF16)
        return ()

    staged(row_tiles(x_ref.shape[0], rows), grown, folded, out)


def expert_pull_kernel(
    rows, stride, spare, x_ref, gate_ref, up_ref, g_ref, down_ref, dx_ref, act_ref, dgate_ref, dup_ref
):
    def grown(at):
        x = x_ref[at : at + rows, :]
        gate, up = dot(x, gate_ref[...]), dot(x, up_ref[...])
        return gate, up, dot(g_ref[at : at + rows, :], down_ref[...], 1, 1)

    def folded(at, gate, up, grad):
        sigmoid = jax.nn.sigmoid(gate)
        silu = gate * sigmoid
        act = (silu * up).astype(BF16)
        dup = (grad * silu).astype(BF16)
        dgate = (grad * up * (sigmoid + silu * (1.0 - sigmoid))).astype(BF16)
        for ref, value in ((act_ref, act), (dup_ref, dup), (dgate_ref, dgate)):
            ref[at : at + rows, :] = value
        inner = jnp.sum(grad * act.astype(F32), axis=1, keepdims=True) if spare else None
        return dgate, dup, inner

    def out(at, dgate, dup, inner):
        dx = dot(dgate, gate_ref[...], 1, 1) + dot(dup, up_ref[...], 1, 1)
        if spare:
            line = places((stride, 1), 0)
            eye = places((stride, LANES), 0) == places((stride, LANES), 1)
            blocks = []
            for top in range(0, rows, stride):
                row = jnp.sum(
                    jnp.where(eye, inner[top : top + stride], 0.0), axis=0, keepdims=True
                )
                high = row.astype(BF16).astype(F32)
                extra = jnp.concatenate(
                    [high, row - high, jnp.zeros((1, dx.shape[1] - 2 * LANES), F32)], axis=1
                )
                blocks.append(jnp.where(line == spare, extra, dx[top : top + stride]))
            dx = jnp.concatenate(blocks, axis=0)
        dx_ref[at : at + rows, :] = dx.astype(BF16)
        return ()

    staged(row_tiles(x_ref.shape[0], rows), grown, folded, out)


def down_kernel(rows, stride, out_stride, act_ref, down_ref, out_ref):
    to = 0
    for (at,) in row_tiles(act_ref.shape[0], rows):
        result = dot(act_ref[at : at + rows, :], down_ref[...])
        kept = [result[top : top + out_stride] for top in range(0, rows, stride)]
        kept = jnp.concatenate(kept, axis=0).astype(BF16)
        out_ref[to : to + kept.shape[0], :] = kept
        to += kept.shape[0]


def finish_kernel(cfg, hidden, returned, gates, slots, out_ref):
    stride, rows, capacity, chunk, split = cfg
    total = returned.shape[0]
    line = slot_line(total, total // rows, split, stride, rows, capacity)
    first = gather_rows([slots[:, 0:1]], line, returned, chunk)
    second = gather_rows([slots[:, 1:2]], line, returned, chunk)
    out_ref[...] = (hidden[...] + gates[:, 0:1] * first + gates[:, 1:2] * second).astype(BF16)


def backward_kernel(cfg, top, closing, *refs):
    stride, spare, chunk, capacity, next_stride, head_width, tile, split = cfg
    refs = list(refs)
    take = lambda number: [refs.pop(0) for _ in range(number)]
    if closing:
        scalars, o_ref = take(2)
    returned, grad_top, gates, pick_cols, slot_cols = take(5)
    apart = None if top else take(1)[0]
    enter_ref, hidden_ref, q_ref, k_ref, v_ref, cos_ref, sin_ref, seg_col, seg_row = take(9)
    wide, wr, gains = take(3)
    if not closing:
        next_gates, next_slots = take(2)
    grad_out, low_out = take(2)
    if closing:
        keep, give, dgain_out, wide_sums = take(4)
    else:
        dq_out, dk_out, dv_out, branch_out, dz_out, dgain_out, send = take(7)

    group = returned.shape[0] // stride
    line = slot_line(returned.shape[0], group, split, stride, stride, capacity)
    width = wide.shape[1]
    grad_y = grad_top[...].astype(F32)
    c1, c2 = gates[:, 0:1], gates[:, 1:2]
    if top:
        parts = [
            gather_rows([slot_cols[:, k : k + 1]], line, returned, chunk) for k in range(2)
        ]
        dx2 = c1 * parts[0] + c2 * parts[1]
        lines = one_hot(
            places((group, returned.shape[0]), 1)
            == places((group, returned.shape[0]), 0) * stride + spare
        )
        extra = dot(lines, returned[...]).astype(BF16)
        inner = []
        for k in range(2):
            pick = pick_cols[:, k : k + 1]
            held = dot(one_hot(pick == places((1, group), 1) // split), extra)
            held = held[:, 0:LANES] + held[:, LANES : 2 * LANES]
            rank = slot_cols[:, k : k + 1] - pick * stride
            inner.append(
                jnp.sum(
                    jnp.where(rank == places(held.shape, 1), held, 0.0), axis=1, keepdims=True
                )
            )
        apart_grad = inner[0] - inner[1]
    else:
        dx2 = gather_rows([slot_cols[:, 0:1], slot_cols[:, 1:2]], line, returned, chunk)
        apart_grad = jnp.sum(grad_y * apart[...], axis=1, keepdims=True)
    grad_gap = apart_grad * c1 * c2
    ids = places((grad_y.shape[0], wr.shape[1]), 1)
    dz = (
        jnp.where(pick_cols[:, 0:1] == ids, grad_gap, 0.0)
        - jnp.where(pick_cols[:, 1:2] == ids, grad_gap, 0.0)
    ).astype(BF16)
    if not closing:
        dz_out[...] = dz
    dx2 = dx2 + dot(dz, wr[...], 1, 1)
    normed, inverse = norm_parts(hidden_ref[...])
    x2 = (normed * gains[1:2, :]).astype(BF16)
    middle, grad_gain = norm_pull(dx2, normed, inverse, gains[1:2, :])
    dgain_out[1:2, :] = grad_gain
    grad_hidden = grad_y + middle
    branch = grad_hidden.astype(BF16)
    if not closing:
        branch_out[...] = branch
    grad_mixed = dot(branch, wide[3 * width :, :], 1, 1).astype(BF16)

    half = head_width // 2
    cosine, sine = wide_tables(cos_ref, sin_ref)
    scale = 1.0 / math.sqrt(head_width)
    blocks = [slice(at, at + LANES) for at in range(0, width, LANES)]
    pulled = attend_pull(
        *([ref[:, lanes] for lanes in blocks] for ref in (q_ref, k_ref, v_ref)),
        [grad_mixed[:, lanes] for lanes in blocks],
        seg_col[...],
        seg_row[...],
        head_width,
        tile,
    )
    turned = [[], [], []]
    for dq, dk, dv in pulled:
        dq = dq * scale
        turned[0].append((dq * cosine - swap_halves(dq, half) * sine).astype(BF16))
        turned[1].append((dk * cosine - swap_halves(dk, half) * sine).astype(BF16))
        turned[2].append(dv.astype(BF16))
    dq, dk, dv = (jnp.concatenate(parts, axis=1) for parts in turned)
    dx1 = (
        dot(dq, wide[:width, :], 1, 1)
        + dot(dk, wide[width : 2 * width, :], 1, 1)
        + dot(dv, wide[2 * width : 3 * width, :], 1, 1)
    )
    normed, inverse = norm_parts(enter_ref[...].astype(F32))
    lower, grad_gain = norm_pull(dx1, normed, inverse, gains[0:1, :])
    dgain_out[0:1, :] = grad_gain
    grad_enter = grad_hidden + lower
    grad_out[...] = grad_enter
    rounded = grad_enter.astype(BF16)
    low_out[...] = rounded
    if closing:
        x1 = (normed * gains[0:1, :]).astype(BF16)
        own_sums(
            scalars[1], x1, x2, o_ref[...], dq, dk, dv, branch, dz, dgain_out, keep, give, wide_sums
        )
    else:
        dq_out[...], dk_out[...], dv_out[...] = dq, dk, dv
        loads = [(next_gates[:, k : k + 1] * rounded.astype(F32)).astype(BF16) for k in range(2)]
        scatter_rows(send, split, next_stride, next_slots[...], loads)


def per_device(
    tokens, segments, routes, grad_top, w_attn, norm_gains, w_route, w_gate, w_up, w_down
):
    section = lax.axis_index("section")
    place = lax.axis_index("dp")
    group = lax.axis_size("dp")
    half = group // 2
    micro_count, rows_local, length, width = tokens.shape
    count = rows_local * length
    shard_rows = w_attn.shape[1]
    route_shard, gain_shard = w_route.shape[1], norm_gains.shape[1]
    experts = route_shard * group // width
    split = group // experts
    capacity = 9 * count // (4 * experts)
    head_width = width // HEADS
    half_width = head_width // 2
    strides = (round_up(capacity, 8), round_up(capacity + 1, 8))
    spares = (0, capacity)
    sizes = tuple(group * stride for stride in strides)
    chunks = tuple(min(size, 16 * stride) for size, stride in zip(sizes, strides))
    tile = min(512, count)
    aligned = shard_rows % 16 == 0
    hidden_units = w_gate.shape[-1]

    fence = lax.optimization_barrier
    to_second, to_first = ((0, 1),), ((1, 0),)

    def across(array, pairs=((0, 1), (1, 0))):
        return lax.ppermute(array, "section", list(pairs))

    def round_dp(array, bit):
        return lax.ppermute(array, "dp", [(i, i ^ bit) for i in range(group)])

    scalars = jnp.stack([section, place % 2]).astype(I32)

    small_rows = 8

    def wide_row(row):
        return jnp.pad(row, ((0, 0), (0, width - row.shape[1])))

    own_pack = jnp.concatenate(
        [
            w_attn[0],
            wide_row(w_route),
            wide_row(norm_gains),
            jnp.zeros((small_rows - 2, width), BF16),
        ]
    )
    far_pack = across(own_pack)
    packs = (
        jnp.where(section == 0, own_pack, far_pack),
        jnp.where(section == 0, far_pack, own_pack),
    )

    def doubled(held, bit):
        return merged(held, round_dp(held, bit), bit)

    def merged(held, other, bit):
        high = (place // bit) % 2 == 1
        return jnp.where(
            high, jnp.stack([other, held], axis=1), jnp.stack([held, other], axis=1)
        ).reshape(-1, *held.shape[1:])

    bits = [group >> step for step in range(1, group.bit_length())]

    def unpack(held):
        other = round_dp(held, 1)
        if aligned:
            return [held, other]
        full = merged(held, other, 1)
        route = full[:, shard_rows, :route_shard].reshape(width, experts)
        gain = full[:, shard_rows + 1, :gain_shard].reshape(2, width).astype(F32)
        return [full[:, :shard_rows].reshape(4 * width, width), route, gain]

    def exchange(rows):
        blocks = rows.reshape(group, -1, width)
        moved = lax.all_to_all(blocks, "dp", split_axis=0, concat_axis=0, tiled=True)
        return moved.reshape(rows.shape)

    def to_owner(array, layer):
        return across(array.astype(BF16), ((1 - layer, layer),))

    own_experts = (w_gate[0, 0], w_up[0, 0], w_down[0, 0])

    def own_rows(array):
        return lax.dynamic_index_in_dim(array, section, 0, keepdims=False).reshape(count, width)

    own_routes = lax.dynamic_index_in_dim(routes[0], section, 0, keepdims=False)
    far_routes = lax.dynamic_index_in_dim(routes[0], 1 - section, 0, keepdims=False)
    own_routes, far_routes = own_routes.reshape(count, 2).T, far_routes.reshape(count, 2).T
    far_routes = across(tie(far_routes, far_pack))
    offset = jnp.arange(rows_local, dtype=I32)[:, None] * length
    segment = (lax.dynamic_index_in_dim(segments, section, 0, keepdims=False) + offset).reshape(count)
    firsts = jnp.sum((segment[:, None] > segment[None, :]).astype(I32), axis=1)
    offsets = (jnp.arange(count, dtype=I32) - firsts).astype(F32)
    freqs = jnp.exp(
        jnp.arange(half_width, dtype=F32) * (-2.0 * math.log(10000.0) / head_width)
    )
    angles = offsets[:, None] * freqs
    seg_row = segment[None, :]
    tables_out = [((count, 2), I32), ((2, count), I32)] * 4 + [((count, 1), I32)]
    *tables, seg_col = call(
        functools.partial(tables_kernel, strides, experts),
        tables_out,
        [scalars, own_routes, far_routes, seg_row],
        "tables",
        2 * 2 * count * count * experts,
        scalars=(0,),
    )
    pick_cols, pick_rows, slot_cols, slot_rows = (tables[i::4] for i in range(4))

    tokens_flops = 2 * count * width
    attn_flops = tokens_flops * (4 * width + 2 * count * (LANES // head_width) * 2)
    move_flops = [tokens_flops * size for size in sizes]
    expert_flops = [2 * size * width * hidden_units for size in sizes]

    def block_rows(layer):
        blocks = 1
        while 2 * blocks * strides[layer] <= 384 and group % (2 * blocks) == 0:
            blocks *= 2
        return blocks * strides[layer]

    def forward(layer, lead, combine, params):
        outs = [((sizes[layer], width), BF16)]
        outs += [((count, width), BF16)] * 4
        outs += [((count, width), F32), ((count, width), BF16), ((count, width), BF16)]
        outs += [((count, 2), F32)]
        if combine:
            outs += [((count, width), BF16), ((count, width), F32)]
        if aligned:
            outs += [((4 * width, width), BF16), ((width, experts), BF16), ((2, width), F32)]
        cfg = (strides[layer], spares[layer], chunks[0], capacity, strides, head_width, tile)
        cfg += (split, shard_rows)
        results = call(
            functools.partial(forward_kernel, cfg, combine, aligned),
            outs,
            [scalars, *lead, cosine, sine, seg_col, seg_row, *params]
            + [pick_cols[layer], pick_rows[layer], slot_cols[layer], slot_rows[layer]],
            f"layer{layer}_forward",
            attn_flops + move_flops[layer] * (3 if combine else 1),
            scratch=[pltpu.VMEM((group, width), F32)],
            scalars=(0,),
        )
        return results if aligned else [*results, *params]

    def backward(layer, args):
        top, closing = layer == 1, layer == 0 and aligned
        rows, line = ((count, width), BF16), ((2, width), F32)
        outs = [((count, width), F32), rows]
        scratch = []
        if closing:
            outs += [((half, shard_rows + small_rows, width), BF16)] * 2
            scratch = [pltpu.VMEM((2, width), F32), pltpu.VMEM((4 * width, width), BF16)]
        else:
            outs += [rows] * 4 + [((count, experts), BF16), line, ((sizes[0], width), BF16)]
        cfg = (strides[layer], spares[layer], chunks[layer], capacity, strides[0], head_width, tile)
        return call(
            functools.partial(backward_kernel, cfg + (split,), top, closing),
            outs,
            args,
            f"layer{layer}_backward",
            3 * attn_flops + move_flops[layer] * (4 if top else 1),
            scratch=scratch,
            scalars=(0,) if closing else (),
        )

    def pulled(rows):
        return jnp.einsum("nd,nf->df", *rows, preferred_element_type=F32)

    def by_core(x1, x2, o, dq, dk, dv, branch, dz, dgain):
        if aligned:
            block = ((half, shard_rows + small_rows, width), BF16)
            return call(
                sums_kernel,
                [block, block],
                [scalars, x1, x2, o, dq, dk, dv, branch, dz, dgain],
                "own_sums",
                4 * tokens_flops * width,
                scratch=[pltpu.VMEM((4 * width, width), BF16)],
                scalars=(0,),
            )
        matrix = jnp.concatenate(
            [pulled((x1, dq)), pulled((x1, dk)), pulled((x1, dv)), pulled((o, branch))], axis=0
        )
        route = pulled((x2, dz)).reshape(group, 1, route_shard)
        gain = dgain.reshape(group, 1, gain_shard)
        blocks = jnp.concatenate(
            [
                matrix.reshape(group, shard_rows, width),
                jnp.pad(route, ((0, 0), (0, 0), (0, width - route_shard))),
                jnp.pad(gain, ((0, 0), (0, 0), (0, width - gain_shard))),
                jnp.zeros((group, small_rows - 2, width), F32),
            ],
            axis=1,
        ).astype(BF16)
        pairs = blocks.reshape(half, 2, *blocks.shape[1:])
        return (
            lax.dynamic_index_in_dim(pairs, place % 2, 1, keepdims=False),
            lax.dynamic_index_in_dim(pairs, 1 - place % 2, 1, keepdims=False),
        )

    def paired(keep, give):
        return added(keep, round_dp(give, 1))

    def spread(blocks):
        sets = [[2 * chip + c for chip in range(half)] for c in range(2)]
        return lax.all_to_all(
            blocks, "dp", split_axis=0, concat_axis=0, tiled=True, axis_index_groups=sets
        )

    def halved(blocks, bit):
        pairs = blocks.reshape(-1, 2, *blocks.shape[1:])
        own = (place // 2 // bit) % 2
        keep = lax.dynamic_index_in_dim(pairs, own, 1, keepdims=False)
        give = lax.dynamic_index_in_dim(pairs, 1 - own, 1, keepdims=False)
        return keep, round_dp(give, 2 * bit)

    def added(keep, got):
        return (keep.astype(F32) + got.astype(F32)).astype(BF16)

    def summed(moved):
        return jnp.sum(moved.astype(F32), axis=0)

    def by_micro(first, far_first, second, far_second):
        return jnp.where(
            section == 0,
            jnp.stack([first, far_first.astype(first.dtype)]),
            jnp.stack([far_second.astype(second.dtype), second]),
        ).reshape(1, micro_count, rows_local, length, width)

    def joined(first, far_first, second, far_second):
        whole = jnp.where(
            section == 0, first + far_first.astype(F32), second + far_second.astype(F32)
        )
        return whole[None, None]

    def hosted(index, far):
        own = own_experts[index]
        return jnp.where(section == 0, own, far), jnp.where(section == 0, far, own)

    other = round_dp(packs[0][None], bits[0])
    other, slot_rows = fence((other, slot_rows))
    gathered = merged(packs[0][None], other, bits[0])
    other = round_dp(gathered, bits[1])
    tokens, grad_top = tie((tokens, grad_top), gathered)
    token_rows, top_rows = own_rows(tokens), own_rows(grad_top)
    (top_send,) = call(
        functools.partial(scatter_kernel, strides[1], split),
        [((sizes[1], width), BF16)],
        [slot_rows[1], top_rows],
        "top_send",
        move_flops[1],
    )
    other, top_send = fence((other, top_send))
    gathered = merged(gathered, other, bits[1])
    other = round_dp(gathered, bits[2])
    angles = tie(angles, gathered)
    cosine, sine = jnp.cos(angles), jnp.sin(angles)
    held1 = packs[1][None]
    other1 = round_dp(tie(held1, gathered), bits[0])
    other, cosine, sine, other1 = fence((other, cosine, sine, other1))
    far_gate = across(tie(own_experts[0], far_pack))
    top_received = exchange(tie(top_send, other, far_gate))
    gathered = merged(gathered, other, bits[2])
    for bit in bits[3:-1]:
        gathered = doubled(gathered, bit)

    far_up = across(tie(own_experts[1], gathered))
    results = forward(0, [token_rows], False, unpack(gathered))
    send0, q0, k0, v0, o0, h0, x1_0, x2_0, gates0, *params0 = results
    send0, far_up, top_received = fence((send0, far_up, top_received))
    received0 = exchange(send0)
    held1 = merged(held1, tie(other1, send0), bits[0])
    other1 = round_dp(held1, bits[1])
    far_down = across(tie(own_experts[2], send0))
    gates_up_down = [hosted(i, far) for i, far in enumerate((far_gate, far_up, far_down))]
    experts0, experts1 = zip(*gates_up_down)
    received0, experts0, experts1, other1 = fence((received0, experts0, experts1, other1))
    held1 = merged(held1, other1, bits[1])
    (result0,) = call(
        functools.partial(expert_kernel, block_rows(0)),
        [((sizes[0], width), BF16)],
        [received0, *experts0],
        "layer0_experts",
        3 * expert_flops[0],
    )
    result0, held1 = fence((result0, held1))
    for bit in bits[2:-1]:
        held1 = doubled(held1, bit)
    params1 = unpack(held1)
    returned0 = exchange(result0)

    returned0, params1 = fence((returned0, params1))
    results = forward(1, [h0, returned0, gates0, slot_cols[0]], True, params1)
    send1, q1, k1, v1, o1, h1, x1_1, x2_1, gates1, y0, apart0, *params1 = results
    send1, y0 = fence((send1, y0))
    received1 = exchange(send1)
    far_y0 = across(y0, to_first)
    received1, far_y0 = fence((received1, far_y0))

    hidden_out = lambda layer: ((sizes[layer], hidden_units), BF16)
    dx1_send, act1, dgate1, dup1 = call(
        functools.partial(expert_pull_kernel, block_rows(1), strides[1], spares[1]),
        [((sizes[1], width), BF16), hidden_out(1), hidden_out(1), hidden_out(1)],
        [received1, *experts1[:2], top_received, experts1[2]],
        "layer1_experts",
        5 * expert_flops[1],
    )
    dx1_send, act1, dgate1, dup1 = fence((dx1_send, act1, dgate1, dup1))
    dx1_back = exchange(dx1_send)
    lines = received1.reshape(group, strides[1], width)[:, capacity].astype(F32)
    gate_slots = lines[:, :LANES] + lines[:, LANES : 2 * LANES]
    gate_slots = gate_slots[:, : strides[1]].reshape(sizes[1], 1)
    scaled = (received1.astype(F32) * gate_slots).astype(BF16)
    scaled_top = (top_received.astype(F32) * gate_slots).astype(BF16)
    gate1 = pulled((scaled, dgate1))
    far_gate1 = to_owner(gate1, 1)
    (result1,) = call(
        functools.partial(down_kernel, block_rows(1), strides[1], strides[0]),
        [((sizes[0], width), BF16)],
        [act1, experts1[2]],
        "layer1_down",
        expert_flops[1],
    )
    up1, down1 = pulled((scaled, dup1)), pulled((act1, scaled_top))
    low_up1, low_down1 = up1.astype(BF16), down1.astype(BF16)
    dx1_back, result1, gate1, up1, down1, low_up1, low_down1, far_gate1 = fence(
        (dx1_back, result1, gate1, up1, down1, low_up1, low_down1, far_gate1)
    )

    returned1 = exchange(result1)
    results = backward(
        1,
        [dx1_back, top_rows, gates1, pick_cols[1], slot_cols[1], y0, h1, q1, k1, v1]
        + [cosine, sine, seg_col, seg_row, *params1, gates0, slot_rows[0]],
    )
    results, returned1 = fence((results, returned1))
    grad1, low1, dq1, dk1, dv1, branch1, dz1, dgain1, dr0_send = results
    dr0 = exchange(dr0_send)
    far_up1 = to_owner(tie(low_up1, dr0_send), 1)
    blocks1 = paired(*by_core(x1_1, x2_1, o1, dq1, dk1, dv1, branch1, dz1, dgain1))
    chip_bits = [1 << step for step in range(half.bit_length() - 1)]
    keep1, got1 = halved(blocks1, chip_bits[0])
    (y1,) = call(
        functools.partial(finish_kernel, (strides[1], strides[0], capacity, chunks[0], split)),
        [((count, width), BF16)],
        [h1, returned1, gates1, slot_cols[1]],
        "layer1_out",
        2 * move_flops[1],
    )
    dr0, y1 = fence((dr0, y1))

    dx0_send, act0, dgate0, dup0 = call(
        functools.partial(expert_pull_kernel, block_rows(0), strides[0], 0),
        [((sizes[0], width), BF16), hidden_out(0), hidden_out(0), hidden_out(0)],
        [received0, *experts0[:2], dr0, experts0[2]],
        "layer0_experts_pull",
        5 * expert_flops[0],
    )
    dx0_send, act0, dgate0, dup0, far_up1, keep1, got1 = fence(
        (dx0_send, act0, dgate0, dup0, far_up1, keep1, got1)
    )
    dx0_back = exchange(dx0_send)
    gate0 = pulled((received0, dgate0))
    far_gate0 = to_owner(gate0, 0)
    up0, down0 = pulled((received0, dup0)), pulled((act0, dr0))
    far_down1 = to_owner(tie(low_down1, gate0), 1)
    far_y1 = across(tie(y1, gate0), to_second)
    low_up0, low_down0 = up0.astype(BF16), down0.astype(BF16)
    keep1, got1 = tie((keep1, got1), dx0_send)
    for bit in chip_bits[1:-1]:
        keep1, got1 = halved(added(keep1, got1), bit)
    dx0_back, gate0, up0, down0, low_up0, low_down0, keep1, got1 = fence(
        (dx0_back, gate0, up0, down0, low_up0, low_down0, keep1, got1)
    )

    closing = [scalars, o0] if aligned else []
    results = backward(
        0,
        closing
        + [dx0_back, low1, gates0, pick_cols[0], slot_cols[0], apart0, token_rows, h0, q0, k0, v0]
        + [cosine, sine, seg_col, seg_row, *params0]
        + ([] if aligned else [gates0, slot_rows[0]]),
    )
    far_up0 = to_owner(low_up0, 0)
    far_up0 = to_owner(low_up0, 0)
    results, far_gate0, far_up0, far_down1, far_y1 = fence(
        (results, far_gate0, far_up0, far_down1, far_y1)
    )
    if aligned:
        grad0, low0, keep, give = results
    else:
        grad0, low0, dq0, dk0, dv0, branch0, dz0, dgain0, _ = results
        keep, give = by_core(x1_0, x2_0, o0, dq0, dk0, dv0, branch0, dz0, dgain0)

    far_down0 = to_owner(tie(low_down0, grad0), 0)
    blocks0 = paired(keep, give)
    moved0 = spread(blocks0)
    low0, low1, y0, y1, keep1, got1 = tie((low0, low1, y0, y1, keep1, got1), blocks0)
    far_low = across(jnp.where(section == 0, low1, low0))
    keep1, got1 = halved(added(keep1, got1), chip_bits[-1])
    gate0, up0, down0, gate1, up1, down1 = tie((gate0, up0, down0, gate1, up1, down1), blocks0)
    gate_out = joined(gate0, far_gate0, gate1, far_gate1)
    up_out = joined(up0, far_up0, up1, far_up1)
    down_out = joined(down0, far_down0, down1, far_down1)
    layer_out = by_micro(y0, far_y0, y1, far_y1)
    moved0, gate_out, up_out, down_out, layer_out = fence(
        (moved0, gate_out, up_out, down_out, layer_out)
    )
    sums0 = summed(moved0)
    far_sums0 = across(sums0, to_first)
    far_low, keep1, got1 = tie((far_low, keep1, got1), sums0)
    sums1 = keep1[0].astype(F32) + got1[0].astype(F32)
    far_sums1 = across(sums1, to_second)
    input_grads = by_micro(grad0, far_low, grad1, far_low)
    total = jnp.where(section == 0, sums0 + far_sums0, sums1 + far_sums1)
    return (
        layer_out,
        input_grads,
        total[:shard_rows][None],
        total[shard_rows + 1, :gain_shard][None],
        total[shard_rows, :route_shard][None],
        gate_out,
        up_out,
        down_out,
    )


def solution(mesh):
    in_specs = (
        P(None, "dp", None, None),
        P(None, "dp", None),
        P("section", None, "dp", None, None),
        P(None, "dp", None, None),
        P("section", "dp", None),
        P("section", "dp"),
        P("section", "dp"),
        P("section", "dp", None, None),
        P("section", "dp", None, None),
        P("section", "dp", None, None),
    )
    out_specs = (
        P("section", None, "dp", None, None),
        P("section", None, "dp", None, None),
        P("section", "dp", None),
        P("section", "dp"),
        P("section", "dp"),
        P("section", "dp", None, None),
        P("section", "dp", None, None),
        P("section", "dp", None, None),
    )
    return jax.shard_map(
        per_device, mesh=mesh, in_specs=in_specs, out_specs=out_specs, check_vma=False
    )
```

```python
import functools
import math

import jax
import jax.numpy as jnp
from jax import lax
from jax.experimental import pallas as pl
from jax.experimental.pallas import tpu as pltpu
from jax.sharding import PartitionSpec as P

HEADS = 6
NORM_EPSILON = 1e-05
LANES = 128
F32 = jnp.float32
BF16 = jnp.bfloat16
I32 = jnp.int32
VMEM_LIMIT = 56 * 1024 * 1024


def dot(left, right, left_dim=1, right_dim=0):
    return lax.dot_general(
        left, right, (((left_dim,), (right_dim,)), ((), ())), preferred_element_type=F32
    )


def places(shape, dim):
    return lax.broadcasted_iota(I32, shape, dim)


def tie(value, *others):
    return lax.optimization_barrier((value, others))[0]


def round_up(value, step):
    return -(-value // step) * step


def call(body, outs, args, name, flops, scratch=(), scalars=(), limit=VMEM_LIMIT):
    shapes = [jax.ShapeDtypeStruct(shape, dtype) for shape, dtype in outs]
    moved = sum(math.prod(a.shape) * a.dtype.itemsize for a in list(args) + shapes)
    return pl.pallas_call(
        body,
        out_shape=shapes,
        in_specs=[
            pl.BlockSpec(memory_space=pltpu.SMEM if index in scalars else pltpu.VMEM)
            for index in range(len(args))
        ],
        out_specs=[pl.BlockSpec(memory_space=pltpu.VMEM) for _ in shapes],
        scratch_shapes=list(scratch),
        compiler_params=pltpu.CompilerParams(vmem_limit_bytes=limit),
        cost_estimate=pl.CostEstimate(flops=flops, bytes_accessed=moved, transcendentals=0),
        name=name,
    )(*args)


def norm_parts(values):
    inverse = lax.rsqrt(jnp.mean(values * values, axis=-1, keepdims=True) + NORM_EPSILON)
    return values * inverse, inverse


def norm_pull(grad_out, normed, inverse, gain):
    grad_gain = jnp.sum(grad_out * normed, axis=0, keepdims=True)
    grad_normed = grad_out * gain
    inner = jnp.mean(grad_normed * normed, axis=-1, keepdims=True)
    return inverse * (grad_normed - normed * inner), grad_gain


def swap_halves(values, half):
    low = places((1, LANES), 1) % (2 * half) < half
    return jnp.where(
        low, pltpu.roll(values, LANES - half, 1), pltpu.roll(values, half, 1)
    )


def wide_tables(cos_ref, sin_ref):
    half = cos_ref.shape[1]
    cosine = jnp.concatenate([cos_ref[...]] * (LANES // half), axis=1)
    sine = jnp.concatenate([sin_ref[...]] * (LANES // half), axis=1)
    return cosine, jnp.where(places((1, LANES), 1) % (2 * half) < half, -sine, sine)


def head_lanes(values, head, width):
    lane = places((1, LANES), 1)
    return jnp.where((lane >= head * width) & (lane < (head + 1) * width), values, 0.0)


def staged(jobs, *stages):
    values = {}
    for step in range(len(jobs) + len(stages) - 1):
        for late, stage in enumerate(stages):
            index = step - late
            if 0 <= index < len(jobs):
                values[index] = stage(*jobs[index], *values.get(index, ()))
    return [values[index] for index in range(len(jobs))]


def attend(queries, keys, values, seg_col, seg_row, width, tile):
    count = queries[0].shape[0]
    heads = LANES // width
    turned = [jnp.transpose(v.astype(F32)).astype(BF16) for v in values]
    jobs = [
        (block, head, at)
        for block in range(len(queries))
        for head in range(heads)
        for at in range(0, count, tile)
    ]

    def scores(block, head, at):
        own = head_lanes(keys[block].astype(F32), head, width).astype(BF16)
        return (dot(own, queries[block][at : at + tile], 1, 1),)

    def terms(block, head, at, score):
        score = jnp.where(seg_col == seg_row[:, at : at + tile], score, -1e30)
        term = jnp.exp(score - jnp.max(score, axis=0, keepdims=True))
        return ((term * (1.0 / jnp.sum(term, axis=0, keepdims=True))).astype(BF16),)

    def mixed(block, head, at, weights):
        return dot(turned[block][head * width : (head + 1) * width], weights)

    parts = staged(jobs, scores, terms, mixed)
    each = count // tile
    outs = []
    for block in range(len(queries)):
        rows = []
        for head in range(heads):
            first = (block * heads + head) * each
            rows.append(jnp.concatenate(parts[first : first + each], axis=1))
        outs.append(jnp.transpose(jnp.concatenate(rows, axis=0)))
    return outs


def attend_pull(queries, keys, values, grads, seg_col, seg_row, width, tile):
    count = queries[0].shape[0]
    heads = LANES // width
    turned = [jnp.transpose(k.astype(F32)).astype(BF16) for k in keys]
    jobs = [
        (block, head, at)
        for block in range(len(queries))
        for head in range(heads)
        for at in range(0, count, tile)
    ]

    def scores(block, head, at):
        own_keys = head_lanes(keys[block].astype(F32), head, width).astype(BF16)
        own_values = head_lanes(values[block].astype(F32), head, width).astype(BF16)
        return (
            dot(own_keys, queries[block][at : at + tile], 1, 1),
            dot(own_values, grads[block][at : at + tile], 1, 1),
        )

    def terms(block, head, at, score, pulled):
        score = jnp.where(seg_col == seg_row[:, at : at + tile], score, -1e30)
        term = jnp.exp(score - jnp.max(score, axis=0, keepdims=True))
        weights = term * (1.0 / jnp.sum(term, axis=0, keepdims=True))
        inner = jnp.sum(weights * pulled, axis=0, keepdims=True)
        return weights.astype(BF16), (weights * (pulled - inner)).astype(BF16)

    def mixed(block, head, at, weights, grad_scores):
        return (
            dot(turned[block][head * width : (head + 1) * width], grad_scores),
            dot(grad_scores, queries[block][at : at + tile]),
            dot(weights, grads[block][at : at + tile]),
        )

    parts = staged(jobs, scores, terms, mixed)
    each = count // tile
    outs = []
    for block in range(len(queries)):
        rows, grad_keys, grad_values = [], 0.0, 0.0
        for head in range(heads):
            first = (block * heads + head) * each
            own = parts[first : first + each]
            rows.append(jnp.concatenate([part[0] for part in own], axis=1))
            grad_keys = grad_keys + head_lanes(sum(part[1] for part in own), head, width)
            grad_values = grad_values + head_lanes(sum(part[2] for part in own), head, width)
        outs.append((jnp.transpose(jnp.concatenate(rows, axis=0)), grad_keys, grad_values))
    return outs


def one_hot(hits):
    return jnp.where(hits, 1.0, 0.0).astype(BF16)


def scatter_rows(out_ref, split, stride, rows, slot_rows, loads, extra_ref=None, extra_at=0):
    blocks = out_ref.shape[0] // rows
    count = slot_rows.shape[1]
    first, second = slot_rows[0:1], slot_rows[1:2]

    def hits(slots, block):
        return (slots - block // split * stride) == places((rows, count), 0)

    def write(step, carry):
        pair = (2 * step, 2 * step + 1)
        if len(loads) == 1:
            chosen = one_hot(
                jnp.concatenate([hits(first, b) | hits(second, b) for b in pair], axis=0)
            )
            lines = dot(chosen, loads[0])
        else:
            lines = dot(
                one_hot(jnp.concatenate([hits(first, b) for b in pair], axis=0)), loads[0]
            ) + dot(one_hot(jnp.concatenate([hits(second, b) for b in pair], axis=0)), loads[1])
        if extra_ref is not None:
            line = places((rows, 1), 0)
            lines = jnp.concatenate(
                [
                    jnp.where(
                        line == extra_at,
                        extra_ref[pl.ds(b, 1), :],
                        lines[i * rows : (i + 1) * rows],
                    )
                    for i, b in enumerate(pair)
                ],
                axis=0,
            )
        at = step * 2 * rows if blocks <= 16 else pl.multiple_of(step * 2 * rows, 16)
        out_ref[pl.ds(at, 2 * rows), :] = lines.astype(BF16)
        return carry

    if blocks <= 16:
        for step in range(blocks // 2):
            write(step, 0)
    else:
        lax.fori_loop(0, blocks // 2, write, 0)


def slot_line(total, group, split, stride, rows, capacity):
    row = places((1, total), 1)
    at = row % rows
    return jnp.where(at < capacity, row // rows // split * stride + at, -1)


def gather_rows(slots, line, rows_ref, chunk):
    total = 0.0
    for at in range(0, rows_ref.shape[0], chunk):
        part = line[:, at : at + chunk]
        hits = slots[0] == part
        for more in slots[1:]:
            hits = hits | (more == part)
        total = total + dot(one_hot(hits), rows_ref[at : at + chunk, :])
    return total


def tables_kernel(strides, experts, scalars, *refs):
    own_ref, far_ref, seg_ref, *outs = refs
    count = seg_ref.shape[1]
    first = scalars[0] == 0
    after = one_hot(places((count, count), 0) < places((count, count), 1))
    seg_col = outs.pop()
    seg_col[...] = jnp.transpose(jnp.broadcast_to(seg_ref[...], (8, count)).astype(F32))[
        :, 0:1
    ].astype(I32)
    for layer, stride in enumerate(strides):
        pick_cols, pick_rows, slot_cols, slot_rows = outs[4 * layer : 4 * layer + 4]
        own = first if layer == 0 else jnp.logical_not(first)
        rows = jnp.where(own, own_ref[...], far_ref[...])
        pick_rows[...] = rows
        marks = [rows[k : k + 1, :] == places((experts, count), 0) for k in range(2)]
        ranks = dot(one_hot(marks[0] | marks[1]), after)
        wanted = []
        for k in range(2):
            rank = jnp.sum(jnp.where(marks[k], ranks, 0.0), axis=0, keepdims=True)
            wanted.append(rows[k : k + 1, :] * stride + rank.astype(I32))
            slot_rows[k : k + 1, :] = wanted[k]
        lines = [rows[0:1, :], rows[1:2, :], *wanted]
        lines = jnp.concatenate([line.astype(F32) for line in lines] * 2, axis=0)
        cols = jnp.transpose(lines).astype(I32)
        pick_cols[...] = cols[:, 0:2]
        slot_cols[...] = cols[:, 2:4]


def scatter_kernel(
    stride, split, spare, pick_cols, pick_rows, slot_cols, slot_rows, load_ref, out_ref, extra_ref
):
    group, count = extra_ref.shape[0], load_ref.shape[0]
    members = places((group, 1), 0) // split
    extra_ref[...] = jnp.zeros_like(extra_ref)
    for k in range(2):
        rank = slot_cols[:, k : k + 1] - pick_cols[:, k : k + 1] * stride
        line = one_hot(rank == places((count, LANES), 1))
        other = pick_rows[1 - k : 2 - k, :].astype(F32)
        held = jnp.where(members == pick_rows[k : k + 1, :], other, 0.0).astype(BF16)
        extra_ref[:, 0:LANES] += dot(held, line)
    scatter_rows(
        out_ref, split, stride, stride, slot_rows[...], [load_ref[...]], extra_ref, spare
    )


def unpack_rows(core, own_ref, other_ref, shard_rows, wide_ref, route_ref, gains_ref):
    pairs, rows, width = own_ref.shape
    group = 2 * pairs
    small = rows - shard_rows
    lines = []
    for i in range(group):
        own = core == i % 2
        wide_ref[i * shard_rows : (i + 1) * shard_rows, :] = jnp.where(
            own, own_ref[i // 2, :shard_rows, :], other_ref[i // 2, :shard_rows, :]
        )
        lines.append(
            jnp.where(
                own,
                own_ref[i // 2, shard_rows:, :].astype(F32),
                other_ref[i // 2, shard_rows:, :].astype(F32),
            )
        )
    lines = jnp.concatenate(lines, axis=0).astype(BF16)
    experts = route_ref.shape[1]
    each = width // group
    row, line = places((width, 1), 0), places((1, group * small), 1)
    spread = dot(one_hot(line == row // each * small), lines)
    lane = places((1, width), 1)
    spread = jnp.where(lane // experts == row % each, spread, 0.0).astype(BF16)
    fold = one_hot(places((width, 1), 0) % experts == places((1, experts), 1))
    route_ref[...] = dot(spread, fold).astype(BF16)
    each = 2 * width // group
    lane = places((1, 2 * width), 1)
    spread = dot(lines, one_hot(places((width, 1), 0) == lane % each))
    line = places((group * small, 1), 0)
    spread = jnp.where(line == lane // each * small + 1, spread, 0.0)
    gains = jnp.sum(spread, axis=0, keepdims=True)
    gains_ref[0:1, :] = gains[:, :width]
    gains_ref[1:2, :] = gains[:, width:]


def own_sums(core, x1, x2, o, dq, dk, dv, branch, dz, dgain, keep, give, wide):
    width, experts = x1.shape[1], dz.shape[1]
    pairs, rows, _ = keep.shape
    group = 2 * pairs
    shard_rows = 4 * width // group
    small = rows - shard_rows
    x1_turned = jnp.transpose(x1.astype(F32)).astype(BF16)
    for i, grads in enumerate((dq, dk, dv)):
        wide[i * width : (i + 1) * width, :] = dot(x1_turned, grads).astype(BF16)
    wide[3 * width :, :] = dot(jnp.transpose(o.astype(F32)).astype(BF16), branch).astype(BF16)
    route = dot(jnp.transpose(x2.astype(F32)).astype(BF16), dz).astype(BF16)
    each = width // group
    row, lane = places((width, 1), 0), places((1, width), 1)
    spread = dot(route, one_hot(places((experts, 1), 0) == lane % experts))
    spread = jnp.where(lane // experts == row % each, spread, 0.0).astype(BF16)
    line = places((group * small, 1), 0)
    lines = dot(one_hot(line == places((1, width), 1) // each * small), spread)
    each = 2 * width // group
    lane = places((1, 2 * width), 1)
    gains = jnp.concatenate([dgain[0:1, :], dgain[1:2, :]], axis=1)
    held = jnp.where(line == lane // each * small + 1, gains, 0.0).astype(BF16)
    lines = lines + dot(held, one_hot(places((1, width), 1) == places((2 * width, 1), 0) % each))
    for out, side in ((keep, core), (give, 1 - core)):
        for i in range(pairs):
            at = pl.multiple_of((2 * i + side) * shard_rows, 16)
            out[i, :shard_rows, :] = wide[pl.ds(at, shard_rows), :]
            out[i, shard_rows:, :] = jnp.where(
                side == 0,
                lines[2 * i * small : (2 * i + 1) * small],
                lines[(2 * i + 1) * small : (2 * i + 2) * small],
            ).astype(BF16)


def sums_kernel(scalars, *refs):
    *values, dgain, keep, give, wide = refs
    own_sums(scalars[1], *(ref[...] for ref in values), dgain, keep, give, wide)


def forward_kernel(cfg, combine, packed, scalars, *refs):
    stride, chunk, capacity, rows, head_width, tile, split, shard_rows = cfg
    refs = list(refs)
    take = lambda number: [refs.pop(0) for _ in range(number)]
    if combine:
        hidden_in, returned, gates_in, slots_in = take(4)
    else:
        (tokens_ref,) = take(1)
    cos_ref, sin_ref, seg_col, seg_row = take(4)
    params = take(2 if packed else 3)
    pick_cols, pick_rows, slot_cols, slot_rows = take(4)
    send, q_out, k_out, v_out, o_out, h_out, x1_out, x2_out, gates_out = take(9)
    if combine:
        y_out, apart_out = take(2)
    if packed:
        wide, wr, gains = take(3)
        unpack_rows(scalars[1], *params, shard_rows, wide, wr, gains)
    else:
        wide, wr, gains = params
    group = send.shape[0] // rows

    if combine:
        line = slot_line(returned.shape[0], group, split, rows, rows, capacity)
        first = gather_rows([slots_in[:, 0:1]], line, returned, chunk)
        second = gather_rows([slots_in[:, 1:2]], line, returned, chunk)
        whole = hidden_in[...] + gates_in[:, 0:1] * first + gates_in[:, 1:2] * second
        apart_out[...] = first - second
        leaving = whole.astype(BF16)
        y_out[...] = leaving
        entering = leaving.astype(F32)
    else:
        entering = tokens_ref[...].astype(F32)

    half = head_width // 2
    width = entering.shape[1]
    cosine, sine = wide_tables(cos_ref, sin_ref)
    normed, _ = norm_parts(entering)
    x1 = (normed * gains[0:1, :]).astype(BF16)
    x1_out[...] = x1
    q_all, k_all, v_all = (dot(x1, wide[i * width : (i + 1) * width, :]) for i in range(3))
    scale = 1.0 / math.sqrt(head_width)
    queries, keys, values = [], [], []
    for at in range(0, width, LANES):
        lanes = slice(at, at + LANES)
        q, k, v = q_all[:, lanes], k_all[:, lanes], v_all[:, lanes]
        q = (q * cosine + swap_halves(q, half) * sine).astype(BF16).astype(F32) * scale
        queries.append(q.astype(BF16))
        keys.append((k * cosine + swap_halves(k, half) * sine).astype(BF16))
        values.append(v.astype(BF16))
    for out, parts in ((q_out, queries), (k_out, keys), (v_out, values)):
        out[...] = jnp.concatenate(parts, axis=1)
    mixed = attend(queries, keys, values, seg_col[...], seg_row[...], head_width, tile)
    mixed = jnp.concatenate([part.astype(BF16) for part in mixed], axis=1)
    o_out[...] = mixed
    hidden = entering + dot(mixed, wide[3 * width :, :])
    h_out[...] = hidden
    normed, _ = norm_parts(hidden)
    x2 = (normed * gains[1:2, :]).astype(BF16)
    x2_out[...] = x2
    logits = dot(x2, wr[...])
    signs = [
        jnp.where(pick_cols[:, k : k + 1] == places(logits.shape, 1), logits, 0.0) for k in range(2)
    ]
    gap = jnp.sum(signs[0] - signs[1], axis=1, keepdims=True)
    gates_out[:, 0:1] = jax.nn.sigmoid(gap)
    gates_out[:, 1:2] = jax.nn.sigmoid(-gap)
    scatter_rows(send, split, stride, rows, slot_rows[...], [x2])


def row_tiles(total, rows):
    return [(at,) for at in range(0, total, rows)]


def expert_kernel(rows, x_ref, gate_ref, up_ref, down_ref, out_ref):
    def grown(at):
        x = x_ref[at : at + rows, :]
        return dot(x, gate_ref[...]), dot(x, up_ref[...])

    def folded(at, gate, up):
        return ((gate * jax.nn.sigmoid(gate) * up).astype(BF16),)

    def out(at, hidden):
        out_ref[at : at + rows, :] = dot(hidden, down_ref[...]).astype(BF16)
        return ()

    staged(row_tiles(x_ref.shape[0], rows), grown, folded, out)


def expert_pull_kernel(
    rows, stride, out_stride, spare, x_ref, gate_ref, up_ref, g_ref, down_ref, dx_ref, act_ref, dgate_ref, dup_ref
):
    def spaced(at):
        return at // stride * out_stride

    def grown(at):
        x = x_ref[at : at + rows, :]
        gate, up = dot(x, gate_ref[...]), dot(x, up_ref[...])
        g = g_ref[spaced(at) : spaced(at + rows), :]
        if stride != out_stride:
            g = g.astype(F32)
            kept = [g[top : top + stride] for top in range(0, g.shape[0], out_stride)]
            g = jnp.concatenate(kept, axis=0).astype(BF16)
        return gate, up, dot(g, down_ref[...], 1, 1)

    def folded(at, gate, up, grad):
        sigmoid = jax.nn.sigmoid(gate)
        silu = gate * sigmoid
        act = (silu * up).astype(BF16)
        dup = (grad * silu).astype(BF16)
        dgate = (grad * up * (sigmoid + silu * (1.0 - sigmoid))).astype(BF16)
        for ref, value in ((act_ref, act), (dup_ref, dup), (dgate_ref, dgate)):
            ref[at : at + rows, :] = value
        inner = jnp.sum(grad * act.astype(F32), axis=1, keepdims=True) if spare else None
        return dgate, dup, inner

    def out(at, dgate, dup, inner):
        dx = dot(dgate, gate_ref[...], 1, 1) + dot(dup, up_ref[...], 1, 1)
        if spare:
            eye = places((stride, LANES), 0) == places((stride, LANES), 1)
            width = dx.shape[1]
            line = places((out_stride, 1), 0)
            blocks = []
            for top in range(0, rows, stride):
                row = jnp.sum(
                    jnp.where(eye, inner[top : top + stride], 0.0), axis=0, keepdims=True
                )
                high = row.astype(BF16).astype(F32)
                extra = jnp.concatenate(
                    [high, row - high, jnp.zeros((1, width - 2 * LANES), F32)], axis=1
                )
                block = dx[top : top + stride]
                if stride != out_stride:
                    pad = jnp.zeros((out_stride - stride, width), F32)
                    block = jnp.concatenate([block, pad], axis=0)
                blocks.append(jnp.where(line == spare, extra, block))
            dx = jnp.concatenate(blocks, axis=0)
        dx_ref[spaced(at) : spaced(at + rows), :] = dx.astype(BF16)
        return ()

    staged(row_tiles(x_ref.shape[0], rows), grown, folded, out)


def down_kernel(rows, act_ref, down_ref, out_ref):
    for (at,) in row_tiles(act_ref.shape[0], rows):
        out_ref[at : at + rows, :] = dot(act_ref[at : at + rows, :], down_ref[...]).astype(BF16)


def finish_kernel(cfg, hidden, returned, gates, slots, out_ref):
    stride, rows, capacity, chunk, split = cfg
    total = returned.shape[0]
    line = slot_line(total, total // rows, split, stride, rows, capacity)
    first = gather_rows([slots[:, 0:1]], line, returned, chunk)
    second = gather_rows([slots[:, 1:2]], line, returned, chunk)
    out_ref[...] = (hidden[...] + gates[:, 0:1] * first + gates[:, 1:2] * second).astype(BF16)


def backward_kernel(cfg, top, closing, *refs):
    stride, spare, chunk, capacity, next_stride, head_width, tile, split = cfg
    refs = list(refs)
    take = lambda number: [refs.pop(0) for _ in range(number)]
    if closing:
        scalars, o_ref = take(2)
    returned, grad_top, gates, pick_cols, slot_cols = take(5)
    apart = None if top else take(1)[0]
    enter_ref, hidden_ref, q_ref, k_ref, v_ref, cos_ref, sin_ref, seg_col, seg_row = take(9)
    wide, wr, gains = take(3)
    if not closing:
        next_gates, next_slots = take(2)
    grad_out, low_out = take(2)
    if closing:
        keep, give, dgain_out, wide_sums = take(4)
    else:
        dq_out, dk_out, dv_out, branch_out, dz_out, dgain_out, send = take(7)

    group = returned.shape[0] // stride
    line = slot_line(returned.shape[0], group, split, stride, stride, capacity)
    width = wide.shape[1]
    grad_y = grad_top[...].astype(F32)
    c1, c2 = gates[:, 0:1], gates[:, 1:2]
    if top:
        parts = [
            gather_rows([slot_cols[:, k : k + 1]], line, returned, chunk) for k in range(2)
        ]
        dx2 = c1 * parts[0] + c2 * parts[1]
        lines = one_hot(
            places((group, returned.shape[0]), 1)
            == places((group, returned.shape[0]), 0) * stride + spare
        )
        extra = dot(lines, returned[...]).astype(BF16)
        inner = []
        for k in range(2):
            pick = pick_cols[:, k : k + 1]
            held = dot(one_hot(pick == places((1, group), 1) // split), extra)
            held = held[:, 0:LANES] + held[:, LANES : 2 * LANES]
            rank = slot_cols[:, k : k + 1] - pick * stride
            inner.append(
                jnp.sum(
                    jnp.where(rank == places(held.shape, 1), held, 0.0), axis=1, keepdims=True
                )
            )
        apart_grad = inner[0] - inner[1]
    else:
        dx2 = gather_rows([slot_cols[:, 0:1], slot_cols[:, 1:2]], line, returned, chunk)
        apart_grad = jnp.sum(grad_y * apart[...], axis=1, keepdims=True)
    grad_gap = apart_grad * c1 * c2
    ids = places((grad_y.shape[0], wr.shape[1]), 1)
    dz = (
        jnp.where(pick_cols[:, 0:1] == ids, grad_gap, 0.0)
        - jnp.where(pick_cols[:, 1:2] == ids, grad_gap, 0.0)
    ).astype(BF16)
    if not closing:
        dz_out[...] = dz
    dx2 = dx2 + dot(dz, wr[...], 1, 1)
    normed, inverse = norm_parts(hidden_ref[...])
    x2 = (normed * gains[1:2, :]).astype(BF16)
    middle, grad_gain = norm_pull(dx2, normed, inverse, gains[1:2, :])
    dgain_out[1:2, :] = grad_gain
    grad_hidden = grad_y + middle
    branch = grad_hidden.astype(BF16)
    if not closing:
        branch_out[...] = branch
    grad_mixed = dot(branch, wide[3 * width :, :], 1, 1).astype(BF16)

    half = head_width // 2
    cosine, sine = wide_tables(cos_ref, sin_ref)
    scale = 1.0 / math.sqrt(head_width)
    blocks = [slice(at, at + LANES) for at in range(0, width, LANES)]
    pulled = attend_pull(
        *([ref[:, lanes] for lanes in blocks] for ref in (q_ref, k_ref, v_ref)),
        [grad_mixed[:, lanes] for lanes in blocks],
        seg_col[...],
        seg_row[...],
        head_width,
        tile,
    )
    turned = [[], [], []]
    for dq, dk, dv in pulled:
        dq = dq * scale
        turned[0].append((dq * cosine - swap_halves(dq, half) * sine).astype(BF16))
        turned[1].append((dk * cosine - swap_halves(dk, half) * sine).astype(BF16))
        turned[2].append(dv.astype(BF16))
    dq, dk, dv = (jnp.concatenate(parts, axis=1) for parts in turned)
    dx1 = (
        dot(dq, wide[:width, :], 1, 1)
        + dot(dk, wide[width : 2 * width, :], 1, 1)
        + dot(dv, wide[2 * width : 3 * width, :], 1, 1)
    )
    normed, inverse = norm_parts(enter_ref[...].astype(F32))
    lower, grad_gain = norm_pull(dx1, normed, inverse, gains[0:1, :])
    dgain_out[0:1, :] = grad_gain
    grad_enter = grad_hidden + lower
    grad_out[...] = grad_enter
    rounded = grad_enter.astype(BF16)
    low_out[...] = rounded
    if closing:
        x1 = (normed * gains[0:1, :]).astype(BF16)
        own_sums(
            scalars[1], x1, x2, o_ref[...], dq, dk, dv, branch, dz, dgain_out, keep, give, wide_sums
        )
    else:
        dq_out[...], dk_out[...], dv_out[...] = dq, dk, dv
        loads = [(next_gates[:, k : k + 1] * rounded.astype(F32)).astype(BF16) for k in range(2)]
        scatter_rows(send, split, next_stride, next_stride, next_slots[...], loads)


def per_device(
    tokens, segments, routes, grad_top, w_attn, norm_gains, w_route, w_gate, w_up, w_down
):
    section = lax.axis_index("section")
    place = lax.axis_index("dp")
    group = lax.axis_size("dp")
    half = group // 2
    micro_count, rows_local, length, width = tokens.shape
    count = rows_local * length
    shard_rows = w_attn.shape[1]
    route_shard, gain_shard = w_route.shape[1], norm_gains.shape[1]
    experts = route_shard * group // width
    split = group // experts
    capacity = 9 * count // (4 * experts)
    head_width = width // HEADS
    half_width = head_width // 2
    strides = (round_up(capacity, 8), round_up(capacity + 1, 8))
    spares = (0, capacity)
    sizes = tuple(group * stride for stride in strides)
    chunks = tuple(min(size, 16 * stride) for size, stride in zip(sizes, strides))
    tile = min(512, count)
    aligned = shard_rows % 16 == 0
    hidden_units = w_gate.shape[-1]

    fence = lax.optimization_barrier
    to_second, to_first = ((0, 1),), ((1, 0),)

    def across(array, pairs=((0, 1), (1, 0))):
        return lax.ppermute(array, "section", list(pairs))

    def round_dp(array, bit):
        return lax.ppermute(array, "dp", [(i, i ^ bit) for i in range(group)])

    scalars = jnp.stack([section, place % 2]).astype(I32)

    small_rows = 8

    def wide_row(row):
        return jnp.pad(row, ((0, 0), (0, width - row.shape[1])))

    own_pack = jnp.concatenate(
        [
            w_attn[0],
            wide_row(w_route),
            wide_row(norm_gains),
            jnp.zeros((small_rows - 2, width), BF16),
        ]
    )
    far_pack = across(own_pack)
    packs = (
        jnp.where(section == 0, own_pack, far_pack),
        jnp.where(section == 0, far_pack, own_pack),
    )

    def doubled(held, bit):
        return merged(held, round_dp(held, bit), bit)

    def merged(held, other, bit):
        high = (place // bit) % 2 == 1
        return jnp.where(
            high, jnp.stack([other, held], axis=1), jnp.stack([held, other], axis=1)
        ).reshape(-1, *held.shape[1:])

    bits = [group >> step for step in range(1, group.bit_length())]

    def unpack(held):
        other = round_dp(held, 1)
        if aligned:
            return [held, other]
        full = merged(held, other, 1)
        route = full[:, shard_rows, :route_shard].reshape(width, experts)
        gain = full[:, shard_rows + 1, :gain_shard].reshape(2, width).astype(F32)
        return [full[:, :shard_rows].reshape(4 * width, width), route, gain]

    def exchange(rows):
        blocks = rows.reshape(group, -1, width)
        moved = lax.all_to_all(blocks, "dp", split_axis=0, concat_axis=0, tiled=True)
        return moved.reshape(rows.shape)

    def to_owner(array, layer):
        return across(array.astype(BF16), ((1 - layer, layer),))

    own_experts = (w_gate[0, 0], w_up[0, 0], w_down[0, 0])

    def own_rows(array):
        return lax.dynamic_index_in_dim(array, section, 0, keepdims=False).reshape(count, width)

    own_routes = lax.dynamic_index_in_dim(routes[0], section, 0, keepdims=False)
    far_routes = lax.dynamic_index_in_dim(routes[0], 1 - section, 0, keepdims=False)
    own_routes, far_routes = own_routes.reshape(count, 2).T, far_routes.reshape(count, 2).T
    far_routes = across(tie(far_routes, far_pack))
    offset = jnp.arange(rows_local, dtype=I32)[:, None] * length
    segment = (lax.dynamic_index_in_dim(segments, section, 0, keepdims=False) + offset).reshape(count)
    firsts = jnp.sum((segment[:, None] > segment[None, :]).astype(I32), axis=1)
    offsets = (jnp.arange(count, dtype=I32) - firsts).astype(F32)
    freqs = jnp.exp(
        jnp.arange(half_width, dtype=F32) * (-2.0 * math.log(10000.0) / head_width)
    )
    angles = offsets[:, None] * freqs
    seg_row = segment[None, :]
    tables_out = [((count, 2), I32), ((2, count), I32)] * 4 + [((count, 1), I32)]
    *tables, seg_col = call(
        functools.partial(tables_kernel, strides, experts),
        tables_out,
        [scalars, own_routes, far_routes, seg_row],
        "tables",
        2 * 2 * count * count * experts,
        scalars=(0,),
    )
    pick_cols, pick_rows, slot_cols, slot_rows = (tables[i::4] for i in range(4))

    tokens_flops = 2 * count * width
    attn_flops = tokens_flops * (4 * width + 2 * count * (LANES // head_width) * 2)
    move_flops = [tokens_flops * size for size in sizes]
    expert_flops = [2 * size * width * hidden_units for size in sizes]

    blocks = 1
    while 2 * blocks * strides[0] <= 320 and group % (2 * blocks) == 0:
        blocks *= 2
    tile_rows = blocks * strides[0]

    def forward(layer, lead, combine, params):
        outs = [((sizes[0], width), BF16)]
        outs += [((count, width), BF16)] * 4
        outs += [((count, width), F32), ((count, width), BF16), ((count, width), BF16)]
        outs += [((count, 2), F32)]
        if combine:
            outs += [((count, width), BF16), ((count, width), F32)]
        if aligned:
            outs += [((4 * width, width), BF16), ((width, experts), BF16), ((2, width), F32)]
        cfg = (strides[layer], chunks[0], capacity, strides[0], head_width, tile)
        cfg += (split, shard_rows)
        results = call(
            functools.partial(forward_kernel, cfg, combine, aligned),
            outs,
            [scalars, *lead, cosine, sine, seg_col, seg_row, *params]
            + [pick_cols[layer], pick_rows[layer], slot_cols[layer], slot_rows[layer]],
            f"layer{layer}_forward",
            attn_flops + move_flops[layer] * (3 if combine else 1),
            scalars=(0,),
        )
        return results if aligned else [*results, *params]

    def backward(layer, args):
        top, closing = layer == 1, layer == 0 and aligned
        rows, line = ((count, width), BF16), ((2, width), F32)
        outs = [((count, width), F32), rows]
        scratch = []
        if closing:
            outs += [((half, shard_rows + small_rows, width), BF16)] * 2
            scratch = [pltpu.VMEM((2, width), F32), pltpu.VMEM((4 * width, width), BF16)]
        else:
            outs += [rows] * 4 + [((count, experts), BF16), line, ((sizes[0], width), BF16)]
        cfg = (strides[layer], spares[layer], chunks[layer], capacity, strides[0], head_width, tile)
        return call(
            functools.partial(backward_kernel, cfg + (split,), top, closing),
            outs,
            args,
            f"layer{layer}_backward",
            3 * attn_flops + move_flops[layer] * (4 if top else 1),
            scratch=scratch,
            scalars=(0,) if closing else (),
        )

    def pulled(rows):
        return jnp.einsum("nd,nf->df", *rows, preferred_element_type=F32)

    def by_core(x1, x2, o, dq, dk, dv, branch, dz, dgain):
        if aligned:
            block = ((half, shard_rows + small_rows, width), BF16)
            return call(
                sums_kernel,
                [block, block],
                [scalars, x1, x2, o, dq, dk, dv, branch, dz, dgain],
                "own_sums",
                4 * tokens_flops * width,
                scratch=[pltpu.VMEM((4 * width, width), BF16)],
                scalars=(0,),
            )
        matrix = jnp.concatenate(
            [pulled((x1, dq)), pulled((x1, dk)), pulled((x1, dv)), pulled((o, branch))], axis=0
        )
        route = pulled((x2, dz)).reshape(group, 1, route_shard)
        gain = dgain.reshape(group, 1, gain_shard)
        blocks = jnp.concatenate(
            [
                matrix.reshape(group, shard_rows, width),
                jnp.pad(route, ((0, 0), (0, 0), (0, width - route_shard))),
                jnp.pad(gain, ((0, 0), (0, 0), (0, width - gain_shard))),
                jnp.zeros((group, small_rows - 2, width), F32),
            ],
            axis=1,
        ).astype(BF16)
        pairs = blocks.reshape(half, 2, *blocks.shape[1:])
        return (
            lax.dynamic_index_in_dim(pairs, place % 2, 1, keepdims=False),
            lax.dynamic_index_in_dim(pairs, 1 - place % 2, 1, keepdims=False),
        )

    def paired(keep, give):
        return added(keep, round_dp(give, 1))

    def spread(blocks):
        sets = [[2 * chip + c for chip in range(half)] for c in range(2)]
        return lax.all_to_all(
            blocks, "dp", split_axis=0, concat_axis=0, tiled=True, axis_index_groups=sets
        )

    def halved(blocks, bit):
        pairs = blocks.reshape(-1, 2, *blocks.shape[1:])
        own = (place // 2 // bit) % 2
        keep = lax.dynamic_index_in_dim(pairs, own, 1, keepdims=False)
        give = lax.dynamic_index_in_dim(pairs, 1 - own, 1, keepdims=False)
        return keep, round_dp(give, 2 * bit)

    def added(keep, got):
        return (keep.astype(F32) + got.astype(F32)).astype(BF16)

    def summed(moved):
        return jnp.sum(moved.astype(F32), axis=0)

    def by_micro(first, far_first, second, far_second):
        return jnp.where(
            section == 0,
            jnp.stack([first, far_first.astype(first.dtype)]),
            jnp.stack([far_second.astype(second.dtype), second]),
        ).reshape(1, micro_count, rows_local, length, width)

    def joined(first, far_first, second, far_second):
        whole = jnp.where(
            section == 0, first + far_first.astype(F32), second + far_second.astype(F32)
        )
        return whole[None, None]

    def hosted(index, far):
        own = own_experts[index]
        return jnp.where(section == 0, own, far), jnp.where(section == 0, far, own)

    other = round_dp(packs[0][None], bits[0])
    other, slot_rows = fence((other, slot_rows))
    gathered = merged(packs[0][None], other, bits[0])
    other = round_dp(gathered, bits[1])
    tokens, grad_top = tie((tokens, grad_top), gathered)
    token_rows, top_rows = own_rows(tokens), own_rows(grad_top)
    (top_send,) = call(
        functools.partial(scatter_kernel, strides[1], split, capacity),
        [((sizes[1], width), BF16)],
        [pick_cols[1], pick_rows[1], slot_cols[1], slot_rows[1], top_rows],
        "top_send",
        move_flops[1],
        scratch=[pltpu.VMEM((group, width), F32)],
    )
    other, top_send = fence((other, top_send))
    gathered = merged(gathered, other, bits[1])
    other = round_dp(gathered, bits[2])
    angles = tie(angles, gathered)
    cosine, sine = jnp.cos(angles), jnp.sin(angles)
    held1 = packs[1][None]
    other1 = round_dp(tie(held1, gathered), bits[0])
    other, cosine, sine, other1 = fence((other, cosine, sine, other1))
    far_gate = across(tie(own_experts[0], far_pack))
    top_received = exchange(tie(top_send, other, far_gate))
    gathered = merged(gathered, other, bits[2])
    for bit in bits[3:-1]:
        gathered = doubled(gathered, bit)

    far_up = across(tie(own_experts[1], gathered))
    results = forward(0, [token_rows], False, unpack(gathered))
    send0, q0, k0, v0, o0, h0, x1_0, x2_0, gates0, *params0 = results
    send0, far_up, top_received = fence((send0, far_up, top_received))
    received0 = exchange(send0)
    held1 = merged(held1, tie(other1, send0), bits[0])
    other1 = round_dp(held1, bits[1])
    far_down = across(tie(own_experts[2], send0))
    gates_up_down = [hosted(i, far) for i, far in enumerate((far_gate, far_up, far_down))]
    experts0, experts1 = zip(*gates_up_down)
    received0, experts0, experts1 = fence((received0, experts0, experts1))
    (result0,) = call(
        functools.partial(expert_kernel, tile_rows),
        [((sizes[0], width), BF16)],
        [received0, *experts0],
        "layer0_experts",
        3 * expert_flops[0],
        limit=20 << 20,
    )
    result0, other1 = fence((result0, other1))
    held1 = merged(held1, other1, bits[1])
    for bit in bits[2:-1]:
        held1 = doubled(held1, bit)
    params1 = unpack(held1)
    returned0 = exchange(result0)

    returned0, params1 = fence((returned0, params1))
    results = forward(1, [h0, returned0, gates0, slot_cols[0]], True, params1)
    send1, q1, k1, v1, o1, h1, x1_1, x2_1, gates1, y0, apart0, *params1 = results
    send1, y0 = fence((send1, y0))
    received1 = exchange(send1)
    far_y0 = across(y0, to_first)
    received1, far_y0 = fence((received1, far_y0))

    hidden_out = [((sizes[0], hidden_units), BF16)] * 3
    dx1_send, act1, dgate1, dup1 = call(
        functools.partial(expert_pull_kernel, tile_rows, strides[0], strides[1], capacity),
        [((sizes[1], width), BF16), *hidden_out],
        [received1, *experts1[:2], top_received, experts1[2]],
        "layer1_experts",
        5 * expert_flops[1],
    )
    dx1_send, act1, dgate1, dup1 = fence((dx1_send, act1, dgate1, dup1))
    dx1_back = exchange(dx1_send)
    top_blocks = top_received.reshape(group, strides[1], width)
    partner = top_blocks[:, capacity, : strides[0]].astype(F32).reshape(sizes[0], 1)
    logits = jnp.dot(received1, params1[1], preferred_element_type=F32)
    ids = jnp.arange(experts, dtype=I32)
    sign = (ids == place // split).astype(F32) - (ids.astype(F32) == partner).astype(F32)
    gate_slots = jax.nn.sigmoid(jnp.sum(logits * sign, axis=1, keepdims=True))
    scaled = (received1.astype(F32) * gate_slots).astype(BF16)
    top_kept = top_blocks[:, : strides[0]].reshape(sizes[0], width)
    scaled_top = (top_kept.astype(F32) * gate_slots).astype(BF16)
    gate1 = pulled((scaled, dgate1))
    far_gate1 = to_owner(gate1, 1)
    (result1,) = call(
        functools.partial(down_kernel, tile_rows),
        [((sizes[0], width), BF16)],
        [act1, experts1[2]],
        "layer1_down",
        expert_flops[1],
    )
    up1, down1 = pulled((scaled, dup1)), pulled((act1, scaled_top))
    low_up1, low_down1 = up1.astype(BF16), down1.astype(BF16)
    dx1_back, result1, gate1, up1, down1, low_up1, low_down1, far_gate1 = fence(
        (dx1_back, result1, gate1, up1, down1, low_up1, low_down1, far_gate1)
    )

    returned1 = exchange(result1)
    results = backward(
        1,
        [dx1_back, top_rows, gates1, pick_cols[1], slot_cols[1], y0, h1, q1, k1, v1]
        + [cosine, sine, seg_col, seg_row, *params1, gates0, slot_rows[0]],
    )
    results, returned1 = fence((results, returned1))
    grad1, low1, dq1, dk1, dv1, branch1, dz1, dgain1, dr0_send = results
    dr0 = exchange(dr0_send)
    far_up1 = to_owner(tie(low_up1, dr0_send), 1)
    blocks1 = paired(*by_core(x1_1, x2_1, o1, dq1, dk1, dv1, branch1, dz1, dgain1))
    chip_bits = [1 << step for step in range(half.bit_length() - 1)]
    keep1, got1 = halved(blocks1, chip_bits[0])
    (y1,) = call(
        functools.partial(finish_kernel, (strides[1], strides[0], capacity, chunks[0], split)),
        [((count, width), BF16)],
        [h1, returned1, gates1, slot_cols[1]],
        "layer1_out",
        2 * move_flops[1],
    )
    dr0, y1 = fence((dr0, y1))

    dx0_send, act0, dgate0, dup0 = call(
        functools.partial(expert_pull_kernel, tile_rows, strides[0], strides[0], 0),
        [((sizes[0], width), BF16), *hidden_out],
        [received0, *experts0[:2], dr0, experts0[2]],
        "layer0_experts_pull",
        5 * expert_flops[0],
    )
    dx0_send, act0, dgate0, dup0, far_up1, keep1, got1 = fence(
        (dx0_send, act0, dgate0, dup0, far_up1, keep1, got1)
    )
    dx0_back = exchange(dx0_send)
    gate0 = pulled((received0, dgate0))
    far_gate0 = to_owner(gate0, 0)
    up0, down0 = pulled((received0, dup0)), pulled((act0, dr0))
    far_down1 = to_owner(tie(low_down1, gate0), 1)
    far_y1 = across(tie(y1, gate0), to_second)
    low_up0, low_down0 = up0.astype(BF16), down0.astype(BF16)
    keep1, got1 = tie((keep1, got1), dx0_send)
    for bit in chip_bits[1:-1]:
        keep1, got1 = halved(added(keep1, got1), bit)
    dx0_back, gate0, up0, down0, low_up0, low_down0, keep1, got1 = fence(
        (dx0_back, gate0, up0, down0, low_up0, low_down0, keep1, got1)
    )

    closing = [scalars, o0] if aligned else []
    results = backward(
        0,
        closing
        + [dx0_back, low1, gates0, pick_cols[0], slot_cols[0], apart0, token_rows, h0, q0, k0, v0]
        + [cosine, sine, seg_col, seg_row, *params0]
        + ([] if aligned else [gates0, slot_rows[0]]),
    )
    up_rows = width // 2
    far_up0_a = to_owner(low_up0[:up_rows], 0)
    results, far_gate0, far_up0_a, far_down1, far_y1 = fence(
        (results, far_gate0, far_up0_a, far_down1, far_y1)
    )
    if aligned:
        grad0, low0, keep, give = results
    else:
        grad0, low0, dq0, dk0, dv0, branch0, dz0, dgain0, _ = results
        keep, give = by_core(x1_0, x2_0, o0, dq0, dk0, dv0, branch0, dz0, dgain0)

    far_up0_b = to_owner(tie(low_up0, grad0)[up_rows:], 0)
    far_up0 = jnp.concatenate([far_up0_a, far_up0_b])
    far_down0 = to_owner(tie(low_down0, grad0), 0)
    blocks0 = paired(keep, give)
    moved0 = spread(blocks0)
    low0, low1, y0, y1, keep1, got1 = tie((low0, low1, y0, y1, keep1, got1), blocks0)
    far_low = across(jnp.where(section == 0, low1, low0))
    keep1, got1 = halved(added(keep1, got1), chip_bits[-1])
    gate0, up0, down0, gate1, up1, down1 = tie((gate0, up0, down0, gate1, up1, down1), blocks0)
    gate_out = joined(gate0, far_gate0, gate1, far_gate1)
    up_out = joined(up0, far_up0, up1, far_up1)
    down_out = joined(down0, far_down0, down1, far_down1)
    layer_out = by_micro(y0, far_y0, y1, far_y1)
    moved0, gate_out, up_out, down_out, layer_out = fence(
        (moved0, gate_out, up_out, down_out, layer_out)
    )
    sums0 = summed(moved0)
    far_sums0 = across(sums0, to_first)
    far_low, keep1, got1 = tie((far_low, keep1, got1), sums0)
    sums1 = keep1[0].astype(F32) + got1[0].astype(F32)
    far_sums1 = across(sums1, to_second)
    input_grads = by_micro(grad0, far_low, grad1, far_low)
    total = jnp.where(section == 0, sums0 + far_sums0, sums1 + far_sums1)
    return (
        layer_out,
        input_grads,
        total[:shard_rows][None],
        total[shard_rows + 1, :gain_shard][None],
        total[shard_rows, :route_shard][None],
        gate_out,
        up_out,
        down_out,
    )


def solution(mesh):
    in_specs = (
        P(None, "dp", None, None),
        P(None, "dp", None),
        P("section", None, "dp", None, None),
        P(None, "dp", None, None),
        P("section", "dp", None),
        P("section", "dp"),
        P("section", "dp"),
        P("section", "dp", None, None),
        P("section", "dp", None, None),
        P("section", "dp", None, None),
    )
    out_specs = (
        P("section", None, "dp", None, None),
        P("section", None, "dp", None, None),
        P("section", "dp", None),
        P("section", "dp"),
        P("section", "dp"),
        P("section", "dp", None, None),
        P("section", "dp", None, None),
        P("section", "dp", None, None),
    )
    return jax.shard_map(
        per_device, mesh=mesh, in_specs=in_specs, out_specs=out_specs, check_vma=False
    )
```

```python
import functools
import math

import jax
import jax.numpy as jnp
from jax import lax
from jax.experimental import pallas as pl
from jax.experimental.pallas import tpu as pltpu
from jax.sharding import PartitionSpec as P

HEADS = 6
NORM_EPSILON = 1e-05
LANES = 128
F32 = jnp.float32
BF16 = jnp.bfloat16
I32 = jnp.int32
VMEM_LIMIT = 56 * 1024 * 1024


def dot(left, right, left_dim=1, right_dim=0):
    return lax.dot_general(
        left, right, (((left_dim,), (right_dim,)), ((), ())), preferred_element_type=F32
    )


def places(shape, dim):
    return lax.broadcasted_iota(I32, shape, dim)


def tie(value, *others):
    return lax.optimization_barrier((value, others))[0]


def round_up(value, step):
    return -(-value // step) * step


def call(body, outs, args, name, flops, scratch=(), scalars=(), limit=VMEM_LIMIT):
    shapes = [jax.ShapeDtypeStruct(shape, dtype) for shape, dtype in outs]
    moved = sum(math.prod(a.shape) * a.dtype.itemsize for a in list(args) + shapes)
    return pl.pallas_call(
        body,
        out_shape=shapes,
        in_specs=[
            pl.BlockSpec(memory_space=pltpu.SMEM if index in scalars else pltpu.VMEM)
            for index in range(len(args))
        ],
        out_specs=[pl.BlockSpec(memory_space=pltpu.VMEM) for _ in shapes],
        scratch_shapes=list(scratch),
        compiler_params=pltpu.CompilerParams(vmem_limit_bytes=limit),
        cost_estimate=pl.CostEstimate(flops=flops, bytes_accessed=moved, transcendentals=0),
        name=name,
    )(*args)


def norm_parts(values):
    inverse = lax.rsqrt(jnp.mean(values * values, axis=-1, keepdims=True) + NORM_EPSILON)
    return values * inverse, inverse


def norm_pull(grad_out, normed, inverse, gain):
    grad_gain = jnp.sum(grad_out * normed, axis=0, keepdims=True)
    grad_normed = grad_out * gain
    inner = jnp.mean(grad_normed * normed, axis=-1, keepdims=True)
    return inverse * (grad_normed - normed * inner), grad_gain


def swap_halves(values, half):
    low = places((1, LANES), 1) % (2 * half) < half
    return jnp.where(
        low, pltpu.roll(values, LANES - half, 1), pltpu.roll(values, half, 1)
    )


def wide_tables(cos_ref, sin_ref):
    half = cos_ref.shape[1]
    cosine = jnp.concatenate([cos_ref[...]] * (LANES // half), axis=1)
    sine = jnp.concatenate([sin_ref[...]] * (LANES // half), axis=1)
    return cosine, jnp.where(places((1, LANES), 1) % (2 * half) < half, -sine, sine)


def head_lanes(values, head, width):
    lane = places((1, LANES), 1)
    return jnp.where((lane >= head * width) & (lane < (head + 1) * width), values, 0.0)


def staged(jobs, *stages):
    values = {}
    for step in range(len(jobs) + len(stages) - 1):
        for late, stage in enumerate(stages):
            index = step - late
            if 0 <= index < len(jobs):
                values[index] = stage(*jobs[index], *values.get(index, ()))
    return [values[index] for index in range(len(jobs))]


def attend(queries, keys, values, seg_col, seg_row, width, tile):
    count = queries[0].shape[0]
    heads = LANES // width
    turned = [jnp.transpose(v.astype(F32)).astype(BF16) for v in values]
    jobs = [
        (block, head, at)
        for block in range(len(queries))
        for head in range(heads)
        for at in range(0, count, tile)
    ]

    def scores(block, head, at):
        own = head_lanes(keys[block].astype(F32), head, width).astype(BF16)
        return (dot(own, queries[block][at : at + tile], 1, 1),)

    def terms(block, head, at, score):
        score = jnp.where(seg_col == seg_row[:, at : at + tile], score, -1e30)
        term = jnp.exp(score - jnp.max(score, axis=0, keepdims=True))
        return ((term * (1.0 / jnp.sum(term, axis=0, keepdims=True))).astype(BF16),)

    def mixed(block, head, at, weights):
        return dot(turned[block][head * width : (head + 1) * width], weights)

    parts = staged(jobs, scores, terms, mixed)
    each = count // tile
    outs = []
    for block in range(len(queries)):
        rows = []
        for head in range(heads):
            first = (block * heads + head) * each
            rows.append(jnp.concatenate(parts[first : first + each], axis=1))
        outs.append(jnp.transpose(jnp.concatenate(rows, axis=0)))
    return outs


def attend_pull(queries, keys, values, grads, seg_col, seg_row, width, tile):
    count = queries[0].shape[0]
    heads = LANES // width
    turned = [jnp.transpose(k.astype(F32)).astype(BF16) for k in keys]
    jobs = [
        (block, head, at)
        for block in range(len(queries))
        for head in range(heads)
        for at in range(0, count, tile)
    ]

    def scores(block, head, at):
        own_keys = head_lanes(keys[block].astype(F32), head, width).astype(BF16)
        own_values = head_lanes(values[block].astype(F32), head, width).astype(BF16)
        return (
            dot(own_keys, queries[block][at : at + tile], 1, 1),
            dot(own_values, grads[block][at : at + tile], 1, 1),
        )

    def terms(block, head, at, score, pulled):
        score = jnp.where(seg_col == seg_row[:, at : at + tile], score, -1e30)
        term = jnp.exp(score - jnp.max(score, axis=0, keepdims=True))
        weights = term * (1.0 / jnp.sum(term, axis=0, keepdims=True))
        inner = jnp.sum(weights * pulled, axis=0, keepdims=True)
        return weights.astype(BF16), (weights * (pulled - inner)).astype(BF16)

    def mixed(block, head, at, weights, grad_scores):
        return (
            dot(turned[block][head * width : (head + 1) * width], grad_scores),
            dot(grad_scores, queries[block][at : at + tile]),
            dot(weights, grads[block][at : at + tile]),
        )

    parts = staged(jobs, scores, terms, mixed)
    each = count // tile
    outs = []
    for block in range(len(queries)):
        rows, grad_keys, grad_values = [], 0.0, 0.0
        for head in range(heads):
            first = (block * heads + head) * each
            own = parts[first : first + each]
            rows.append(jnp.concatenate([part[0] for part in own], axis=1))
            grad_keys = grad_keys + head_lanes(sum(part[1] for part in own), head, width)
            grad_values = grad_values + head_lanes(sum(part[2] for part in own), head, width)
        outs.append((jnp.transpose(jnp.concatenate(rows, axis=0)), grad_keys, grad_values))
    return outs


def one_hot(hits):
    return jnp.where(hits, 1.0, 0.0).astype(BF16)


def scatter_rows(out_ref, split, stride, rows, slot_rows, loads, extra_ref=None, extra_at=0):
    blocks = out_ref.shape[0] // rows
    count = slot_rows.shape[1]
    first, second = slot_rows[0:1], slot_rows[1:2]

    def hits(slots, block):
        return (slots - block // split * stride) == places((rows, count), 0)

    def write(step, carry):
        pair = (2 * step, 2 * step + 1)
        if len(loads) == 1:
            chosen = one_hot(
                jnp.concatenate([hits(first, b) | hits(second, b) for b in pair], axis=0)
            )
            lines = dot(chosen, loads[0])
        else:
            lines = dot(
                one_hot(jnp.concatenate([hits(first, b) for b in pair], axis=0)), loads[0]
            ) + dot(one_hot(jnp.concatenate([hits(second, b) for b in pair], axis=0)), loads[1])
        if extra_ref is not None:
            line = places((rows, 1), 0)
            lines = jnp.concatenate(
                [
                    jnp.where(
                        line == extra_at,
                        extra_ref[pl.ds(b, 1), :],
                        lines[i * rows : (i + 1) * rows],
                    )
                    for i, b in enumerate(pair)
                ],
                axis=0,
            )
        at = step * 2 * rows if blocks <= 16 else pl.multiple_of(step * 2 * rows, 16)
        out_ref[pl.ds(at, 2 * rows), :] = lines.astype(BF16)
        return carry

    if blocks <= 16:
        for step in range(blocks // 2):
            write(step, 0)
    else:
        lax.fori_loop(0, blocks // 2, write, 0)


def slot_line(total, group, split, stride, rows, capacity):
    row = places((1, total), 1)
    at = row % rows
    return jnp.where(at < capacity, row // rows // split * stride + at, -1)


def gather_rows(slots, line, rows_ref, chunk):
    total = 0.0
    for at in range(0, rows_ref.shape[0], chunk):
        part = line[:, at : at + chunk]
        hits = slots[0] == part
        for more in slots[1:]:
            hits = hits | (more == part)
        total = total + dot(one_hot(hits), rows_ref[at : at + chunk, :])
    return total


def tables_kernel(strides, experts, scalars, *refs):
    own_ref, far_ref, seg_ref, *outs = refs
    count = seg_ref.shape[1]
    first = scalars[0] == 0
    after = one_hot(places((count, count), 0) < places((count, count), 1))
    seg_col = outs.pop()
    seg_col[...] = jnp.transpose(jnp.broadcast_to(seg_ref[...], (8, count)).astype(F32))[
        :, 0:1
    ].astype(I32)
    for layer, stride in enumerate(strides):
        pick_cols, pick_rows, slot_cols, slot_rows = outs[4 * layer : 4 * layer + 4]
        own = first if layer == 0 else jnp.logical_not(first)
        rows = jnp.where(own, own_ref[...], far_ref[...])
        pick_rows[...] = rows
        marks = [rows[k : k + 1, :] == places((experts, count), 0) for k in range(2)]
        ranks = dot(one_hot(marks[0] | marks[1]), after)
        wanted = []
        for k in range(2):
            rank = jnp.sum(jnp.where(marks[k], ranks, 0.0), axis=0, keepdims=True)
            wanted.append(rows[k : k + 1, :] * stride + rank.astype(I32))
            slot_rows[k : k + 1, :] = wanted[k]
        lines = [rows[0:1, :], rows[1:2, :], *wanted]
        lines = jnp.concatenate([line.astype(F32) for line in lines] * 2, axis=0)
        cols = jnp.transpose(lines).astype(I32)
        pick_cols[...] = cols[:, 0:2]
        slot_cols[...] = cols[:, 2:4]


def scatter_kernel(
    stride, split, spare, pick_cols, pick_rows, slot_cols, slot_rows, load_ref, out_ref, extra_ref
):
    group, count = extra_ref.shape[0], load_ref.shape[0]
    members = places((group, 1), 0) // split
    extra_ref[...] = jnp.zeros_like(extra_ref)
    for k in range(2):
        rank = slot_cols[:, k : k + 1] - pick_cols[:, k : k + 1] * stride
        line = one_hot(rank == places((count, LANES), 1))
        other = pick_rows[1 - k : 2 - k, :].astype(F32)
        held = jnp.where(members == pick_rows[k : k + 1, :], other, 0.0).astype(BF16)
        extra_ref[:, 0:LANES] += dot(held, line)
    scatter_rows(
        out_ref, split, stride, stride, slot_rows[...], [load_ref[...]], extra_ref, spare
    )


def unpack_rows(core, own_ref, other_ref, shard_rows, wide_ref, route_ref, gains_ref):
    pairs, rows, width = own_ref.shape
    group = 2 * pairs
    small = rows - shard_rows
    lines = []
    for i in range(group):
        own = core == i % 2
        wide_ref[i * shard_rows : (i + 1) * shard_rows, :] = jnp.where(
            own, own_ref[i // 2, :shard_rows, :], other_ref[i // 2, :shard_rows, :]
        )
        lines.append(
            jnp.where(
                own,
                own_ref[i // 2, shard_rows:, :].astype(F32),
                other_ref[i // 2, shard_rows:, :].astype(F32),
            )
        )
    lines = jnp.concatenate(lines, axis=0).astype(BF16)
    experts = route_ref.shape[1]
    each = width // group
    row, line = places((width, 1), 0), places((1, group * small), 1)
    spread = dot(one_hot(line == row // each * small), lines)
    lane = places((1, width), 1)
    spread = jnp.where(lane // experts == row % each, spread, 0.0).astype(BF16)
    fold = one_hot(places((width, 1), 0) % experts == places((1, experts), 1))
    route_ref[...] = dot(spread, fold).astype(BF16)
    each = 2 * width // group
    lane = places((1, 2 * width), 1)
    spread = dot(lines, one_hot(places((width, 1), 0) == lane % each))
    line = places((group * small, 1), 0)
    spread = jnp.where(line == lane // each * small + 1, spread, 0.0)
    gains = jnp.sum(spread, axis=0, keepdims=True)
    gains_ref[0:1, :] = gains[:, :width]
    gains_ref[1:2, :] = gains[:, width:]


def own_sums(core, x1, x2, o, dq, dk, dv, branch, dz, dgain, keep, give, wide):
    width, experts = x1.shape[1], dz.shape[1]
    pairs, rows, _ = keep.shape
    group = 2 * pairs
    shard_rows = 4 * width // group
    small = rows - shard_rows
    x1_turned = jnp.transpose(x1.astype(F32)).astype(BF16)
    for i, grads in enumerate((dq, dk, dv)):
        wide[i * width : (i + 1) * width, :] = dot(x1_turned, grads).astype(BF16)
    wide[3 * width :, :] = dot(jnp.transpose(o.astype(F32)).astype(BF16), branch).astype(BF16)
    route = dot(jnp.transpose(x2.astype(F32)).astype(BF16), dz).astype(BF16)
    each = width // group
    row, lane = places((width, 1), 0), places((1, width), 1)
    spread = dot(route, one_hot(places((experts, 1), 0) == lane % experts))
    spread = jnp.where(lane // experts == row % each, spread, 0.0).astype(BF16)
    line = places((group * small, 1), 0)
    lines = dot(one_hot(line == places((1, width), 1) // each * small), spread)
    each = 2 * width // group
    lane = places((1, 2 * width), 1)
    gains = jnp.concatenate([dgain[0:1, :], dgain[1:2, :]], axis=1)
    held = jnp.where(line == lane // each * small + 1, gains, 0.0).astype(BF16)
    lines = lines + dot(held, one_hot(places((1, width), 1) == places((2 * width, 1), 0) % each))
    for out, side in ((keep, core), (give, 1 - core)):
        for i in range(pairs):
            at = pl.multiple_of((2 * i + side) * shard_rows, 16)
            out[i, :shard_rows, :] = wide[pl.ds(at, shard_rows), :]
            out[i, shard_rows:, :] = jnp.where(
                side == 0,
                lines[2 * i * small : (2 * i + 1) * small],
                lines[(2 * i + 1) * small : (2 * i + 2) * small],
            ).astype(BF16)


def sums_kernel(scalars, *refs):
    *values, dgain, keep, give, wide = refs
    own_sums(scalars[1], *(ref[...] for ref in values), dgain, keep, give, wide)


def forward_kernel(cfg, combine, packed, scalars, *refs):
    stride, chunk, capacity, rows, head_width, tile, split, shard_rows = cfg
    refs = list(refs)
    take = lambda number: [refs.pop(0) for _ in range(number)]
    if combine:
        hidden_in, returned, gates_in, slots_in = take(4)
    else:
        (tokens_ref,) = take(1)
    cos_ref, sin_ref, seg_col, seg_row = take(4)
    params = take(2 if packed else 3)
    pick_cols, pick_rows, slot_cols, slot_rows = take(4)
    send, q_out, k_out, v_out, o_out, h_out, x1_out, x2_out, gates_out = take(9)
    if combine:
        y_out, apart_out = take(2)
    if packed:
        wide, wr, gains = take(3)
        unpack_rows(scalars[1], *params, shard_rows, wide, wr, gains)
    else:
        wide, wr, gains = params
    group = send.shape[0] // rows

    if combine:
        line = slot_line(returned.shape[0], group, split, rows, rows, capacity)
        first = gather_rows([slots_in[:, 0:1]], line, returned, chunk)
        second = gather_rows([slots_in[:, 1:2]], line, returned, chunk)
        whole = hidden_in[...] + gates_in[:, 0:1] * first + gates_in[:, 1:2] * second
        apart_out[...] = first - second
        leaving = whole.astype(BF16)
        y_out[...] = leaving
        entering = leaving.astype(F32)
    else:
        entering = tokens_ref[...].astype(F32)

    half = head_width // 2
    width = entering.shape[1]
    cosine, sine = wide_tables(cos_ref, sin_ref)
    normed, _ = norm_parts(entering)
    x1 = (normed * gains[0:1, :]).astype(BF16)
    x1_out[...] = x1
    q_all, k_all, v_all = (dot(x1, wide[i * width : (i + 1) * width, :]) for i in range(3))
    scale = 1.0 / math.sqrt(head_width)
    queries, keys, values = [], [], []
    for at in range(0, width, LANES):
        lanes = slice(at, at + LANES)
        q, k, v = q_all[:, lanes], k_all[:, lanes], v_all[:, lanes]
        q = (q * cosine + swap_halves(q, half) * sine).astype(BF16).astype(F32) * scale
        queries.append(q.astype(BF16))
        keys.append((k * cosine + swap_halves(k, half) * sine).astype(BF16))
        values.append(v.astype(BF16))
    for out, parts in ((q_out, queries), (k_out, keys), (v_out, values)):
        out[...] = jnp.concatenate(parts, axis=1)
    mixed = attend(queries, keys, values, seg_col[...], seg_row[...], head_width, tile)
    mixed = jnp.concatenate([part.astype(BF16) for part in mixed], axis=1)
    o_out[...] = mixed
    hidden = entering + dot(mixed, wide[3 * width :, :])
    h_out[...] = hidden
    normed, _ = norm_parts(hidden)
    x2 = (normed * gains[1:2, :]).astype(BF16)
    x2_out[...] = x2
    logits = dot(x2, wr[...])
    signs = [
        jnp.where(pick_cols[:, k : k + 1] == places(logits.shape, 1), logits, 0.0) for k in range(2)
    ]
    gap = jnp.sum(signs[0] - signs[1], axis=1, keepdims=True)
    gates_out[:, 0:1] = jax.nn.sigmoid(gap)
    gates_out[:, 1:2] = jax.nn.sigmoid(-gap)
    scatter_rows(send, split, stride, rows, slot_rows[...], [x2])


def row_tiles(total, rows):
    return [(at,) for at in range(0, total, rows)]


def expert_kernel(rows, x_ref, gate_ref, up_ref, down_ref, out_ref):
    def grown(at):
        x = x_ref[at : at + rows, :]
        return dot(x, gate_ref[...]), dot(x, up_ref[...])

    def folded(at, gate, up):
        return ((gate * jax.nn.sigmoid(gate) * up).astype(BF16),)

    def out(at, hidden):
        out_ref[at : at + rows, :] = dot(hidden, down_ref[...]).astype(BF16)
        return ()

    staged(row_tiles(x_ref.shape[0], rows), grown, folded, out)


def expert_pull_kernel(
    rows, stride, out_stride, spare, x_ref, gate_ref, up_ref, g_ref, down_ref, dx_ref, act_ref, dgate_ref, dup_ref
):
    def spaced(at):
        return at // stride * out_stride

    def grown(at):
        x = x_ref[at : at + rows, :]
        gate, up = dot(x, gate_ref[...]), dot(x, up_ref[...])
        g = g_ref[spaced(at) : spaced(at + rows), :]
        if stride != out_stride:
            g = g.astype(F32)
            kept = [g[top : top + stride] for top in range(0, g.shape[0], out_stride)]
            g = jnp.concatenate(kept, axis=0).astype(BF16)
        return gate, up, dot(g, down_ref[...], 1, 1)

    def folded(at, gate, up, grad):
        sigmoid = jax.nn.sigmoid(gate)
        silu = gate * sigmoid
        act = (silu * up).astype(BF16)
        dup = (grad * silu).astype(BF16)
        dgate = (grad * up * (sigmoid + silu * (1.0 - sigmoid))).astype(BF16)
        for ref, value in ((act_ref, act), (dup_ref, dup), (dgate_ref, dgate)):
            ref[at : at + rows, :] = value
        inner = jnp.sum(grad * act.astype(F32), axis=1, keepdims=True) if spare else None
        return dgate, dup, inner

    def out(at, dgate, dup, inner):
        dx = dot(dgate, gate_ref[...], 1, 1) + dot(dup, up_ref[...], 1, 1)
        if spare:
            eye = places((stride, LANES), 0) == places((stride, LANES), 1)
            width = dx.shape[1]
            line = places((out_stride, 1), 0)
            blocks = []
            for top in range(0, rows, stride):
                row = jnp.sum(
                    jnp.where(eye, inner[top : top + stride], 0.0), axis=0, keepdims=True
                )
                high = row.astype(BF16).astype(F32)
                extra = jnp.concatenate(
                    [high, row - high, jnp.zeros((1, width - 2 * LANES), F32)], axis=1
                )
                block = dx[top : top + stride]
                if stride != out_stride:
                    pad = jnp.zeros((out_stride - stride, width), F32)
                    block = jnp.concatenate([block, pad], axis=0)
                blocks.append(jnp.where(line == spare, extra, block))
            dx = jnp.concatenate(blocks, axis=0)
        dx_ref[spaced(at) : spaced(at + rows), :] = dx.astype(BF16)
        return ()

    staged(row_tiles(x_ref.shape[0], rows), grown, folded, out)


def down_kernel(rows, act_ref, down_ref, out_ref):
    for (at,) in row_tiles(act_ref.shape[0], rows):
        out_ref[at : at + rows, :] = dot(act_ref[at : at + rows, :], down_ref[...]).astype(BF16)


def finish_kernel(cfg, hidden, returned, gates, slots, out_ref):
    stride, rows, capacity, chunk, split = cfg
    total = returned.shape[0]
    line = slot_line(total, total // rows, split, stride, rows, capacity)
    first = gather_rows([slots[:, 0:1]], line, returned, chunk)
    second = gather_rows([slots[:, 1:2]], line, returned, chunk)
    out_ref[...] = (hidden[...] + gates[:, 0:1] * first + gates[:, 1:2] * second).astype(BF16)


def backward_kernel(cfg, top, closing, *refs):
    stride, spare, chunk, capacity, next_stride, head_width, tile, split = cfg
    refs = list(refs)
    take = lambda number: [refs.pop(0) for _ in range(number)]
    if closing:
        scalars, o_ref = take(2)
    returned, grad_top, gates, pick_cols, slot_cols = take(5)
    apart = None if top else take(1)[0]
    enter_ref, hidden_ref, q_ref, k_ref, v_ref, cos_ref, sin_ref, seg_col, seg_row = take(9)
    wide, wr, gains = take(3)
    if not closing:
        next_gates, next_slots = take(2)
    grad_out, low_out = take(2)
    if closing:
        keep, give, dgain_out, wide_sums = take(4)
    else:
        dq_out, dk_out, dv_out, branch_out, dz_out, dgain_out, send = take(7)

    group = returned.shape[0] // stride
    line = slot_line(returned.shape[0], group, split, stride, stride, capacity)
    width = wide.shape[1]
    grad_y = grad_top[...].astype(F32)
    c1, c2 = gates[:, 0:1], gates[:, 1:2]
    if top:
        parts = [
            gather_rows([slot_cols[:, k : k + 1]], line, returned, chunk) for k in range(2)
        ]
        dx2 = c1 * parts[0] + c2 * parts[1]
        lines = one_hot(
            places((group, returned.shape[0]), 1)
            == places((group, returned.shape[0]), 0) * stride + spare
        )
        extra = dot(lines, returned[...]).astype(BF16)
        inner = []
        for k in range(2):
            pick = pick_cols[:, k : k + 1]
            held = dot(one_hot(pick == places((1, group), 1) // split), extra)
            held = held[:, 0:LANES] + held[:, LANES : 2 * LANES]
            rank = slot_cols[:, k : k + 1] - pick * stride
            inner.append(
                jnp.sum(
                    jnp.where(rank == places(held.shape, 1), held, 0.0), axis=1, keepdims=True
                )
            )
        apart_grad = inner[0] - inner[1]
    else:
        dx2 = gather_rows([slot_cols[:, 0:1], slot_cols[:, 1:2]], line, returned, chunk)
        apart_grad = jnp.sum(grad_y * apart[...], axis=1, keepdims=True)
    grad_gap = apart_grad * c1 * c2
    ids = places((grad_y.shape[0], wr.shape[1]), 1)
    dz = (
        jnp.where(pick_cols[:, 0:1] == ids, grad_gap, 0.0)
        - jnp.where(pick_cols[:, 1:2] == ids, grad_gap, 0.0)
    ).astype(BF16)
    if not closing:
        dz_out[...] = dz
    dx2 = dx2 + dot(dz, wr[...], 1, 1)
    normed, inverse = norm_parts(hidden_ref[...])
    x2 = (normed * gains[1:2, :]).astype(BF16)
    middle, grad_gain = norm_pull(dx2, normed, inverse, gains[1:2, :])
    dgain_out[1:2, :] = grad_gain
    grad_hidden = grad_y + middle
    branch = grad_hidden.astype(BF16)
    if not closing:
        branch_out[...] = branch
    grad_mixed = dot(branch, wide[3 * width :, :], 1, 1).astype(BF16)

    half = head_width // 2
    cosine, sine = wide_tables(cos_ref, sin_ref)
    scale = 1.0 / math.sqrt(head_width)
    blocks = [slice(at, at + LANES) for at in range(0, width, LANES)]
    pulled = attend_pull(
        *([ref[:, lanes] for lanes in blocks] for ref in (q_ref, k_ref, v_ref)),
        [grad_mixed[:, lanes] for lanes in blocks],
        seg_col[...],
        seg_row[...],
        head_width,
        tile,
    )
    turned = [[], [], []]
    for dq, dk, dv in pulled:
        dq = dq * scale
        turned[0].append((dq * cosine - swap_halves(dq, half) * sine).astype(BF16))
        turned[1].append((dk * cosine - swap_halves(dk, half) * sine).astype(BF16))
        turned[2].append(dv.astype(BF16))
    dq, dk, dv = (jnp.concatenate(parts, axis=1) for parts in turned)
    dx1 = (
        dot(dq, wide[:width, :], 1, 1)
        + dot(dk, wide[width : 2 * width, :], 1, 1)
        + dot(dv, wide[2 * width : 3 * width, :], 1, 1)
    )
    normed, inverse = norm_parts(enter_ref[...].astype(F32))
    lower, grad_gain = norm_pull(dx1, normed, inverse, gains[0:1, :])
    dgain_out[0:1, :] = grad_gain
    grad_enter = grad_hidden + lower
    grad_out[...] = grad_enter
    rounded = grad_enter.astype(BF16)
    low_out[...] = rounded
    if closing:
        x1 = (normed * gains[0:1, :]).astype(BF16)
        own_sums(
            scalars[1], x1, x2, o_ref[...], dq, dk, dv, branch, dz, dgain_out, keep, give, wide_sums
        )
    else:
        dq_out[...], dk_out[...], dv_out[...] = dq, dk, dv
        loads = [(next_gates[:, k : k + 1] * rounded.astype(F32)).astype(BF16) for k in range(2)]
        scatter_rows(send, split, next_stride, next_stride, next_slots[...], loads)


def per_device(
    tokens, segments, routes, grad_top, w_attn, norm_gains, w_route, w_gate, w_up, w_down
):
    section = lax.axis_index("section")
    place = lax.axis_index("dp")
    group = lax.axis_size("dp")
    half = group // 2
    micro_count, rows_local, length, width = tokens.shape
    count = rows_local * length
    shard_rows = w_attn.shape[1]
    route_shard, gain_shard = w_route.shape[1], norm_gains.shape[1]
    experts = route_shard * group // width
    split = group // experts
    capacity = 9 * count // (4 * experts)
    head_width = width // HEADS
    half_width = head_width // 2
    strides = (round_up(capacity, 8), round_up(capacity + 1, 8))
    spares = (0, capacity)
    sizes = tuple(group * stride for stride in strides)
    chunks = tuple(min(size, 16 * stride) for size, stride in zip(sizes, strides))
    tile = min(512, count)
    aligned = shard_rows % 16 == 0
    hidden_units = w_gate.shape[-1]

    fence = lax.optimization_barrier
    to_second, to_first = ((0, 1),), ((1, 0),)

    def across(array, pairs=((0, 1), (1, 0))):
        return lax.ppermute(array, "section", list(pairs))

    def round_dp(array, bit):
        return lax.ppermute(array, "dp", [(i, i ^ bit) for i in range(group)])

    scalars = jnp.stack([section, place % 2]).astype(I32)

    small_rows = 8

    def wide_row(row):
        return jnp.pad(row, ((0, 0), (0, width - row.shape[1])))

    own_pack = jnp.concatenate(
        [
            w_attn[0],
            wide_row(w_route),
            wide_row(norm_gains),
            jnp.zeros((small_rows - 2, width), BF16),
        ]
    )
    far_pack = across(own_pack)
    packs = (
        jnp.where(section == 0, own_pack, far_pack),
        jnp.where(section == 0, far_pack, own_pack),
    )

    def doubled(held, bit):
        return merged(held, round_dp(held, bit), bit)

    def merged(held, other, bit):
        high = (place // bit) % 2 == 1
        return jnp.where(
            high, jnp.stack([other, held], axis=1), jnp.stack([held, other], axis=1)
        ).reshape(-1, *held.shape[1:])

    bits = [group >> step for step in range(1, group.bit_length())]

    def unpack(held):
        other = round_dp(held, 1)
        if aligned:
            return [held, other]
        full = merged(held, other, 1)
        route = full[:, shard_rows, :route_shard].reshape(width, experts)
        gain = full[:, shard_rows + 1, :gain_shard].reshape(2, width).astype(F32)
        return [full[:, :shard_rows].reshape(4 * width, width), route, gain]

    def exchange(rows):
        blocks = rows.reshape(group, -1, width)
        moved = lax.all_to_all(blocks, "dp", split_axis=0, concat_axis=0, tiled=True)
        return moved.reshape(rows.shape)

    def to_owner(array, layer):
        return across(array.astype(BF16), ((1 - layer, layer),))

    own_experts = (w_gate[0, 0], w_up[0, 0], w_down[0, 0])

    def own_rows(array):
        return lax.dynamic_index_in_dim(array, section, 0, keepdims=False).reshape(count, width)

    own_routes = lax.dynamic_index_in_dim(routes[0], section, 0, keepdims=False)
    far_routes = lax.dynamic_index_in_dim(routes[0], 1 - section, 0, keepdims=False)
    own_routes, far_routes = own_routes.reshape(count, 2).T, far_routes.reshape(count, 2).T
    far_routes = across(tie(far_routes, far_pack))
    offset = jnp.arange(rows_local, dtype=I32)[:, None] * length
    segment = (lax.dynamic_index_in_dim(segments, section, 0, keepdims=False) + offset).reshape(count)
    firsts = jnp.sum((segment[:, None] > segment[None, :]).astype(I32), axis=1)
    offsets = (jnp.arange(count, dtype=I32) - firsts).astype(F32)
    freqs = jnp.exp(
        jnp.arange(half_width, dtype=F32) * (-2.0 * math.log(10000.0) / head_width)
    )
    angles = offsets[:, None] * freqs
    seg_row = segment[None, :]
    tables_out = [((count, 2), I32), ((2, count), I32)] * 4 + [((count, 1), I32)]
    *tables, seg_col = call(
        functools.partial(tables_kernel, strides, experts),
        tables_out,
        [scalars, own_routes, far_routes, seg_row],
        "tables",
        2 * 2 * count * count * experts,
        scalars=(0,),
    )
    pick_cols, pick_rows, slot_cols, slot_rows = (tables[i::4] for i in range(4))

    tokens_flops = 2 * count * width
    attn_flops = tokens_flops * (4 * width + 2 * count * (LANES // head_width) * 2)
    move_flops = [tokens_flops * size for size in sizes]
    expert_flops = [2 * size * width * hidden_units for size in sizes]

    blocks = 1
    while 2 * blocks * strides[0] <= 320 and group % (2 * blocks) == 0:
        blocks *= 2
    tile_rows = blocks * strides[0]

    def forward(layer, lead, combine, params):
        outs = [((sizes[0], width), BF16)]
        outs += [((count, width), BF16)] * 4
        outs += [((count, width), F32), ((count, width), BF16), ((count, width), BF16)]
        outs += [((count, 2), F32)]
        if combine:
            outs += [((count, width), BF16), ((count, width), F32)]
        if aligned:
            outs += [((4 * width, width), BF16), ((width, experts), BF16), ((2, width), F32)]
        cfg = (strides[layer], chunks[0], capacity, strides[0], head_width, tile)
        cfg += (split, shard_rows)
        results = call(
            functools.partial(forward_kernel, cfg, combine, aligned),
            outs,
            [scalars, *lead, cosine, sine, seg_col, seg_row, *params]
            + [pick_cols[layer], pick_rows[layer], slot_cols[layer], slot_rows[layer]],
            f"layer{layer}_forward",
            attn_flops + move_flops[layer] * (3 if combine else 1),
            scalars=(0,),
        )
        return results if aligned else [*results, *params]

    def backward(layer, args):
        top, closing = layer == 1, layer == 0 and aligned
        rows, line = ((count, width), BF16), ((2, width), F32)
        outs = [((count, width), F32), rows]
        scratch = []
        if closing:
            outs += [((half, shard_rows + small_rows, width), BF16)] * 2
            scratch = [pltpu.VMEM((2, width), F32), pltpu.VMEM((4 * width, width), BF16)]
        else:
            outs += [rows] * 4 + [((count, experts), BF16), line, ((sizes[0], width), BF16)]
        cfg = (strides[layer], spares[layer], chunks[layer], capacity, strides[0], head_width, tile)
        return call(
            functools.partial(backward_kernel, cfg + (split,), top, closing),
            outs,
            args,
            f"layer{layer}_backward",
            3 * attn_flops + move_flops[layer] * (4 if top else 1),
            scratch=scratch,
            scalars=(0,) if closing else (),
        )

    def pulled(rows):
        return jnp.einsum("nd,nf->df", *rows, preferred_element_type=F32)

    def by_core(x1, x2, o, dq, dk, dv, branch, dz, dgain):
        if aligned:
            block = ((half, shard_rows + small_rows, width), BF16)
            return call(
                sums_kernel,
                [block, block],
                [scalars, x1, x2, o, dq, dk, dv, branch, dz, dgain],
                "own_sums",
                4 * tokens_flops * width,
                scratch=[pltpu.VMEM((4 * width, width), BF16)],
                scalars=(0,),
            )
        matrix = jnp.concatenate(
            [pulled((x1, dq)), pulled((x1, dk)), pulled((x1, dv)), pulled((o, branch))], axis=0
        )
        route = pulled((x2, dz)).reshape(group, 1, route_shard)
        gain = dgain.reshape(group, 1, gain_shard)
        blocks = jnp.concatenate(
            [
                matrix.reshape(group, shard_rows, width),
                jnp.pad(route, ((0, 0), (0, 0), (0, width - route_shard))),
                jnp.pad(gain, ((0, 0), (0, 0), (0, width - gain_shard))),
                jnp.zeros((group, small_rows - 2, width), F32),
            ],
            axis=1,
        ).astype(BF16)
        pairs = blocks.reshape(half, 2, *blocks.shape[1:])
        return (
            lax.dynamic_index_in_dim(pairs, place % 2, 1, keepdims=False),
            lax.dynamic_index_in_dim(pairs, 1 - place % 2, 1, keepdims=False),
        )

    def paired(keep, give):
        return added(keep, round_dp(give, 1))

    def spread(blocks):
        sets = [[2 * chip + c for chip in range(half)] for c in range(2)]
        return lax.all_to_all(
            blocks, "dp", split_axis=0, concat_axis=0, tiled=True, axis_index_groups=sets
        )

    def halved(blocks, bit):
        pairs = blocks.reshape(-1, 2, *blocks.shape[1:])
        own = (place // 2 // bit) % 2
        keep = lax.dynamic_index_in_dim(pairs, own, 1, keepdims=False)
        give = lax.dynamic_index_in_dim(pairs, 1 - own, 1, keepdims=False)
        return keep, round_dp(give, 2 * bit)

    def added(keep, got):
        return (keep.astype(F32) + got.astype(F32)).astype(BF16)

    def summed(moved):
        return jnp.sum(moved.astype(F32), axis=0)

    def by_micro(first, far_first, second, far_second):
        return jnp.where(
            section == 0,
            jnp.stack([first, far_first.astype(first.dtype)]),
            jnp.stack([far_second.astype(second.dtype), second]),
        ).reshape(1, micro_count, rows_local, length, width)

    def joined(first, far_first, second, far_second):
        whole = jnp.where(
            section == 0, first + far_first.astype(F32), second + far_second.astype(F32)
        )
        return whole[None, None]

    def hosted(index, far):
        own = own_experts[index]
        return jnp.where(section == 0, own, far), jnp.where(section == 0, far, own)

    other = round_dp(packs[0][None], bits[0])
    other, slot_rows = fence((other, slot_rows))
    gathered = merged(packs[0][None], other, bits[0])
    other = round_dp(gathered, bits[1])
    tokens, grad_top = tie((tokens, grad_top), gathered)
    token_rows, top_rows = own_rows(tokens), own_rows(grad_top)
    (top_send,) = call(
        functools.partial(scatter_kernel, strides[1], split, capacity),
        [((sizes[1], width), BF16)],
        [pick_cols[1], pick_rows[1], slot_cols[1], slot_rows[1], top_rows],
        "top_send",
        move_flops[1],
        scratch=[pltpu.VMEM((group, width), F32)],
    )
    other, top_send = fence((other, top_send))
    gathered = merged(gathered, other, bits[1])
    other = round_dp(gathered, bits[2])
    angles = tie(angles, gathered)
    cosine, sine = jnp.cos(angles), jnp.sin(angles)
    held1 = packs[1][None]
    other1 = round_dp(tie(held1, gathered), bits[0])
    other, cosine, sine, other1 = fence((other, cosine, sine, other1))
    far_gate = across(tie(own_experts[0], far_pack))
    top_received = exchange(tie(top_send, other, far_gate))
    gathered = merged(gathered, other, bits[2])
    for bit in bits[3:-1]:
        gathered = doubled(gathered, bit)

    far_up = across(tie(own_experts[1], gathered))
    results = forward(0, [token_rows], False, unpack(gathered))
    send0, q0, k0, v0, o0, h0, x1_0, x2_0, gates0, *params0 = results
    send0, far_up, top_received = fence((send0, far_up, top_received))
    received0 = exchange(send0)
    held1 = merged(held1, tie(other1, send0), bits[0])
    other1 = round_dp(held1, bits[1])
    far_down = across(tie(own_experts[2], send0))
    gates_up_down = [hosted(i, far) for i, far in enumerate((far_gate, far_up, far_down))]
    experts0, experts1 = zip(*gates_up_down)
    received0, experts0, experts1 = fence((received0, experts0, experts1))
    (result0,) = call(
        functools.partial(expert_kernel, tile_rows),
        [((sizes[0], width), BF16)],
        [received0, *experts0],
        "layer0_experts",
        3 * expert_flops[0],
        limit=20 << 20,
    )
    result0, other1 = fence((result0, other1))
    held1 = merged(held1, other1, bits[1])
    for bit in bits[2:-1]:
        held1 = doubled(held1, bit)
    params1 = unpack(held1)
    returned0 = exchange(result0)

    returned0, params1 = fence((returned0, params1))
    results = forward(1, [h0, returned0, gates0, slot_cols[0]], True, params1)
    send1, q1, k1, v1, o1, h1, x1_1, x2_1, gates1, y0, apart0, *params1 = results
    send1, y0 = fence((send1, y0))
    received1 = exchange(send1)
    far_y0 = across(y0, to_first)
    received1, far_y0 = fence((received1, far_y0))

    hidden_out = [((sizes[0], hidden_units), BF16)] * 3
    dx1_send, act1, dgate1, dup1 = call(
        functools.partial(expert_pull_kernel, tile_rows, strides[0], strides[1], capacity),
        [((sizes[1], width), BF16), *hidden_out],
        [received1, *experts1[:2], top_received, experts1[2]],
        "layer1_experts",
        5 * expert_flops[1],
    )
    dx1_send, act1, dgate1, dup1 = fence((dx1_send, act1, dgate1, dup1))
    dx1_back = exchange(dx1_send)
    top_blocks = top_received.reshape(group, strides[1], width)
    partner = top_blocks[:, capacity, : strides[0]].astype(F32).reshape(sizes[0], 1)
    logits = jnp.dot(received1, params1[1], preferred_element_type=F32)
    ids = jnp.arange(experts, dtype=I32)
    sign = (ids == place // split).astype(F32) - (ids.astype(F32) == partner).astype(F32)
    gate_slots = jax.nn.sigmoid(jnp.sum(logits * sign, axis=1, keepdims=True))
    scaled = (received1.astype(F32) * gate_slots).astype(BF16)
    top_kept = top_blocks[:, : strides[0]].reshape(sizes[0], width)
    scaled_top = (top_kept.astype(F32) * gate_slots).astype(BF16)
    gate1 = pulled((scaled, dgate1))
    far_gate1 = to_owner(gate1, 1)
    (result1,) = call(
        functools.partial(down_kernel, tile_rows),
        [((sizes[0], width), BF16)],
        [act1, experts1[2]],
        "layer1_down",
        expert_flops[1],
    )
    up1, down1 = pulled((scaled, dup1)), pulled((act1, scaled_top))
    low_up1, low_down1 = up1.astype(BF16), down1.astype(BF16)
    dx1_back, result1, gate1, up1, down1, low_up1, low_down1, far_gate1 = fence(
        (dx1_back, result1, gate1, up1, down1, low_up1, low_down1, far_gate1)
    )

    returned1 = exchange(result1)
    results = backward(
        1,
        [dx1_back, top_rows, gates1, pick_cols[1], slot_cols[1], y0, h1, q1, k1, v1]
        + [cosine, sine, seg_col, seg_row, *params1, gates0, slot_rows[0]],
    )
    results, returned1 = fence((results, returned1))
    grad1, low1, dq1, dk1, dv1, branch1, dz1, dgain1, dr0_send = results
    dr0 = exchange(dr0_send)
    far_up1 = to_owner(tie(low_up1, dr0_send), 1)
    blocks1 = paired(*by_core(x1_1, x2_1, o1, dq1, dk1, dv1, branch1, dz1, dgain1))
    chip_bits = [1 << step for step in range(half.bit_length() - 1)]
    keep1, got1 = halved(blocks1, chip_bits[0])
    (y1,) = call(
        functools.partial(finish_kernel, (strides[1], strides[0], capacity, chunks[0], split)),
        [((count, width), BF16)],
        [h1, returned1, gates1, slot_cols[1]],
        "layer1_out",
        2 * move_flops[1],
    )
    dr0, y1 = fence((dr0, y1))

    dx0_send, act0, dgate0, dup0 = call(
        functools.partial(expert_pull_kernel, tile_rows, strides[0], strides[0], 0),
        [((sizes[0], width), BF16), *hidden_out],
        [received0, *experts0[:2], dr0, experts0[2]],
        "layer0_experts_pull",
        5 * expert_flops[0],
    )
    dx0_send, act0, dgate0, dup0, far_up1, keep1, got1 = fence(
        (dx0_send, act0, dgate0, dup0, far_up1, keep1, got1)
    )
    dx0_back = exchange(dx0_send)
    gate0 = pulled((received0, dgate0))
    far_gate0 = to_owner(gate0, 0)
    up0, down0 = pulled((received0, dup0)), pulled((act0, dr0))
    far_down1 = to_owner(tie(low_down1, gate0), 1)
    far_y1 = across(tie(y1, gate0), to_second)
    low_up0, low_down0 = up0.astype(BF16), down0.astype(BF16)
    low_up0 = (low_up0[: width // 2], low_up0[width // 2 :])
    keep1, got1 = tie((keep1, got1), dx0_send)
    for bit in chip_bits[1:-1]:
        keep1, got1 = halved(added(keep1, got1), bit)
    dx0_back, gate0, up0, down0, low_up0, low_down0, keep1, got1 = fence(
        (dx0_back, gate0, up0, down0, low_up0, low_down0, keep1, got1)
    )

    closing = [scalars, o0] if aligned else []
    results = backward(
        0,
        closing
        + [dx0_back, low1, gates0, pick_cols[0], slot_cols[0], apart0, token_rows, h0, q0, k0, v0]
        + [cosine, sine, seg_col, seg_row, *params0]
        + ([] if aligned else [gates0, slot_rows[0]]),
    )
    far_up0_a = to_owner(low_up0[0], 0)
    results, far_gate0, far_up0_a, far_down1, far_y1 = fence(
        (results, far_gate0, far_up0_a, far_down1, far_y1)
    )
    if aligned:
        grad0, low0, keep, give = results
    else:
        grad0, low0, dq0, dk0, dv0, branch0, dz0, dgain0, _ = results
        keep, give = by_core(x1_0, x2_0, o0, dq0, dk0, dv0, branch0, dz0, dgain0)

    far_up0_b = to_owner(tie(low_up0[1], grad0), 0)
    far_up0 = jnp.concatenate([far_up0_a, far_up0_b])
    far_down0 = to_owner(tie(low_down0, grad0), 0)
    blocks0 = paired(keep, give)
    moved0 = spread(blocks0)
    low0, low1, y0, y1, keep1, got1 = tie((low0, low1, y0, y1, keep1, got1), blocks0)
    far_low = across(jnp.where(section == 0, low1, low0))
    keep1, got1 = halved(added(keep1, got1), chip_bits[-1])
    gate0, up0, down0, gate1, up1, down1 = tie((gate0, up0, down0, gate1, up1, down1), blocks0)
    gate_out = joined(gate0, far_gate0, gate1, far_gate1)
    up_out = joined(up0, far_up0, up1, far_up1)
    down_out = joined(down0, far_down0, down1, far_down1)
    layer_out = by_micro(y0, far_y0, y1, far_y1)
    sums1 = keep1[0].astype(F32) + got1[0].astype(F32)
    moved0, gate_out, up_out, down_out, layer_out, sums1 = fence(
        (moved0, gate_out, up_out, down_out, layer_out, sums1)
    )
    sums0 = summed(moved0)
    far_sums = across(jnp.where(section == 0, sums1, sums0))
    far_low = tie(far_low, sums0)
    input_grads = by_micro(grad0, far_low, grad1, far_low)
    total = jnp.where(section == 0, sums0, sums1) + far_sums
    return (
        layer_out,
        input_grads,
        total[:shard_rows][None],
        total[shard_rows + 1, :gain_shard][None],
        total[shard_rows, :route_shard][None],
        gate_out,
        up_out,
        down_out,
    )


def solution(mesh):
    in_specs = (
        P(None, "dp", None, None),
        P(None, "dp", None),
        P("section", None, "dp", None, None),
        P(None, "dp", None, None),
        P("section", "dp", None),
        P("section", "dp"),
        P("section", "dp"),
        P("section", "dp", None, None),
        P("section", "dp", None, None),
        P("section", "dp", None, None),
    )
    out_specs = (
        P("section", None, "dp", None, None),
        P("section", None, "dp", None, None),
        P("section", "dp", None),
        P("section", "dp"),
        P("section", "dp"),
        P("section", "dp", None, None),
        P("section", "dp", None, None),
        P("section", "dp", None, None),
    )
    return jax.shard_map(
        per_device, mesh=mesh, in_specs=in_specs, out_specs=out_specs, check_vma=False
    )
```

```python
import functools
import math

import jax
import jax.numpy as jnp
from jax import lax
from jax.experimental import pallas as pl
from jax.experimental.pallas import tpu as pltpu
from jax.sharding import PartitionSpec as P

HEADS = 6
NORM_EPSILON = 1e-05
LANES = 128
F32 = jnp.float32
BF16 = jnp.bfloat16
I32 = jnp.int32
VMEM_LIMIT = 56 * 1024 * 1024


def dot(left, right, left_dim=1, right_dim=0):
    return lax.dot_general(
        left, right, (((left_dim,), (right_dim,)), ((), ())), preferred_element_type=F32
    )


def places(shape, dim):
    return lax.broadcasted_iota(I32, shape, dim)


def tie(value, *others):
    return lax.optimization_barrier((value, others))[0]


def round_up(value, step):
    return -(-value // step) * step


def call(body, outs, args, name, flops, scratch=(), scalars=(), limit=VMEM_LIMIT):
    shapes = [jax.ShapeDtypeStruct(shape, dtype) for shape, dtype in outs]
    moved = sum(math.prod(a.shape) * a.dtype.itemsize for a in list(args) + shapes)
    return pl.pallas_call(
        body,
        out_shape=shapes,
        in_specs=[
            pl.BlockSpec(memory_space=pltpu.SMEM if index in scalars else pltpu.VMEM)
            for index in range(len(args))
        ],
        out_specs=[pl.BlockSpec(memory_space=pltpu.VMEM) for _ in shapes],
        scratch_shapes=list(scratch),
        compiler_params=pltpu.CompilerParams(vmem_limit_bytes=limit),
        cost_estimate=pl.CostEstimate(flops=flops, bytes_accessed=moved, transcendentals=0),
        name=name,
    )(*args)


def norm_parts(values):
    inverse = lax.rsqrt(jnp.mean(values * values, axis=-1, keepdims=True) + NORM_EPSILON)
    return values * inverse, inverse


def norm_pull(grad_out, normed, inverse, gain):
    grad_gain = jnp.sum(grad_out * normed, axis=0, keepdims=True)
    grad_normed = grad_out * gain
    inner = jnp.mean(grad_normed * normed, axis=-1, keepdims=True)
    return inverse * (grad_normed - normed * inner), grad_gain


def swap_halves(values, half):
    low = places((1, LANES), 1) % (2 * half) < half
    return jnp.where(
        low, pltpu.roll(values, LANES - half, 1), pltpu.roll(values, half, 1)
    )


def wide_tables(cos_ref, sin_ref):
    half = cos_ref.shape[1]
    cosine = jnp.concatenate([cos_ref[...]] * (LANES // half), axis=1)
    sine = jnp.concatenate([sin_ref[...]] * (LANES // half), axis=1)
    return cosine, jnp.where(places((1, LANES), 1) % (2 * half) < half, -sine, sine)


def head_lanes(values, head, width):
    lane = places((1, LANES), 1)
    return jnp.where((lane >= head * width) & (lane < (head + 1) * width), values, 0.0)


def staged(jobs, *stages):
    values = {}
    for step in range(len(jobs) + len(stages) - 1):
        for late, stage in enumerate(stages):
            index = step - late
            if 0 <= index < len(jobs):
                values[index] = stage(*jobs[index], *values.get(index, ()))
    return [values[index] for index in range(len(jobs))]


def attend(queries, keys, values, seg_col, seg_row, width, tile):
    count = queries[0].shape[0]
    heads = LANES // width
    turned = [jnp.transpose(v.astype(F32)).astype(BF16) for v in values]
    jobs = [
        (block, head, at)
        for block in range(len(queries))
        for head in range(heads)
        for at in range(0, count, tile)
    ]

    def scores(block, head, at):
        own = head_lanes(keys[block].astype(F32), head, width).astype(BF16)
        return (dot(own, queries[block][at : at + tile], 1, 1),)

    def terms(block, head, at, score):
        score = jnp.where(seg_col == seg_row[:, at : at + tile], score, -1e30)
        term = jnp.exp(score - jnp.max(score, axis=0, keepdims=True))
        return ((term * (1.0 / jnp.sum(term, axis=0, keepdims=True))).astype(BF16),)

    def mixed(block, head, at, weights):
        return dot(turned[block][head * width : (head + 1) * width], weights)

    parts = staged(jobs, scores, terms, mixed)
    each = count // tile
    outs = []
    for block in range(len(queries)):
        rows = []
        for head in range(heads):
            first = (block * heads + head) * each
            rows.append(jnp.concatenate(parts[first : first + each], axis=1))
        outs.append(jnp.transpose(jnp.concatenate(rows, axis=0)))
    return outs


def attend_pull(queries, keys, values, grads, seg_col, seg_row, width, tile):
    count = queries[0].shape[0]
    heads = LANES // width
    turned = [jnp.transpose(k.astype(F32)).astype(BF16) for k in keys]
    jobs = [
        (block, head, at)
        for block in range(len(queries))
        for head in range(heads)
        for at in range(0, count, tile)
    ]

    def scores(block, head, at):
        own_keys = head_lanes(keys[block].astype(F32), head, width).astype(BF16)
        own_values = head_lanes(values[block].astype(F32), head, width).astype(BF16)
        return (
            dot(own_keys, queries[block][at : at + tile], 1, 1),
            dot(own_values, grads[block][at : at + tile], 1, 1),
        )

    def terms(block, head, at, score, pulled):
        score = jnp.where(seg_col == seg_row[:, at : at + tile], score, -1e30)
        term = jnp.exp(score - jnp.max(score, axis=0, keepdims=True))
        weights = term * (1.0 / jnp.sum(term, axis=0, keepdims=True))
        inner = jnp.sum(weights * pulled, axis=0, keepdims=True)
        return weights.astype(BF16), (weights * (pulled - inner)).astype(BF16)

    def mixed(block, head, at, weights, grad_scores):
        return (
            dot(turned[block][head * width : (head + 1) * width], grad_scores),
            dot(grad_scores, queries[block][at : at + tile]),
            dot(weights, grads[block][at : at + tile]),
        )

    parts = staged(jobs, scores, terms, mixed)
    each = count // tile
    outs = []
    for block in range(len(queries)):
        rows, grad_keys, grad_values = [], 0.0, 0.0
        for head in range(heads):
            first = (block * heads + head) * each
            own = parts[first : first + each]
            rows.append(jnp.concatenate([part[0] for part in own], axis=1))
            grad_keys = grad_keys + head_lanes(sum(part[1] for part in own), head, width)
            grad_values = grad_values + head_lanes(sum(part[2] for part in own), head, width)
        outs.append((jnp.transpose(jnp.concatenate(rows, axis=0)), grad_keys, grad_values))
    return outs


def one_hot(hits):
    return jnp.where(hits, 1.0, 0.0).astype(BF16)


def scatter_rows(out_ref, split, stride, rows, slot_rows, loads, extra_ref=None, extra_at=0):
    blocks = out_ref.shape[0] // rows
    count = slot_rows.shape[1]
    first, second = slot_rows[0:1], slot_rows[1:2]

    def hits(slots, block):
        return (slots - block // split * stride) == places((rows, count), 0)

    def write(step, carry):
        pair = (2 * step, 2 * step + 1)
        if len(loads) == 1:
            chosen = one_hot(
                jnp.concatenate([hits(first, b) | hits(second, b) for b in pair], axis=0)
            )
            lines = dot(chosen, loads[0])
        else:
            lines = dot(
                one_hot(jnp.concatenate([hits(first, b) for b in pair], axis=0)), loads[0]
            ) + dot(one_hot(jnp.concatenate([hits(second, b) for b in pair], axis=0)), loads[1])
        if extra_ref is not None:
            line = places((rows, 1), 0)
            lines = jnp.concatenate(
                [
                    jnp.where(
                        line == extra_at,
                        extra_ref[pl.ds(b, 1), :],
                        lines[i * rows : (i + 1) * rows],
                    )
                    for i, b in enumerate(pair)
                ],
                axis=0,
            )
        at = step * 2 * rows if blocks <= 16 else pl.multiple_of(step * 2 * rows, 16)
        out_ref[pl.ds(at, 2 * rows), :] = lines.astype(BF16)
        return carry

    if blocks <= 16:
        for step in range(blocks // 2):
            write(step, 0)
    else:
        lax.fori_loop(0, blocks // 2, write, 0)


def slot_line(total, group, split, stride, rows, capacity):
    row = places((1, total), 1)
    at = row % rows
    return jnp.where(at < capacity, row // rows // split * stride + at, -1)


def gather_rows(slots, line, rows_ref, chunk):
    total = 0.0
    for at in range(0, rows_ref.shape[0], chunk):
        part = line[:, at : at + chunk]
        hits = slots[0] == part
        for more in slots[1:]:
            hits = hits | (more == part)
        total = total + dot(one_hot(hits), rows_ref[at : at + chunk, :])
    return total


def tables_kernel(strides, experts, scalars, *refs):
    own_ref, far_ref, seg_ref, *outs = refs
    count = seg_ref.shape[1]
    first = scalars[0] == 0
    after = one_hot(places((count, count), 0) < places((count, count), 1))
    seg_col = outs.pop()
    seg_col[...] = jnp.transpose(jnp.broadcast_to(seg_ref[...], (8, count)).astype(F32))[
        :, 0:1
    ].astype(I32)
    for layer, stride in enumerate(strides):
        pick_cols, pick_rows, slot_cols, slot_rows = outs[4 * layer : 4 * layer + 4]
        own = first if layer == 0 else jnp.logical_not(first)
        rows = jnp.where(own, own_ref[...], far_ref[...])
        pick_rows[...] = rows
        marks = [rows[k : k + 1, :] == places((experts, count), 0) for k in range(2)]
        ranks = dot(one_hot(marks[0] | marks[1]), after)
        wanted = []
        for k in range(2):
            rank = jnp.sum(jnp.where(marks[k], ranks, 0.0), axis=0, keepdims=True)
            wanted.append(rows[k : k + 1, :] * stride + rank.astype(I32))
            slot_rows[k : k + 1, :] = wanted[k]
        lines = [rows[0:1, :], rows[1:2, :], *wanted]
        lines = jnp.concatenate([line.astype(F32) for line in lines] * 2, axis=0)
        cols = jnp.transpose(lines).astype(I32)
        pick_cols[...] = cols[:, 0:2]
        slot_cols[...] = cols[:, 2:4]


def scatter_kernel(
    stride, split, spare, pick_cols, pick_rows, slot_cols, slot_rows, load_ref, out_ref, extra_ref
):
    group, count = extra_ref.shape[0], load_ref.shape[0]
    members = places((group, 1), 0) // split
    extra_ref[...] = jnp.zeros_like(extra_ref)
    for k in range(2):
        rank = slot_cols[:, k : k + 1] - pick_cols[:, k : k + 1] * stride
        line = one_hot(rank == places((count, LANES), 1))
        other = pick_rows[1 - k : 2 - k, :].astype(F32)
        held = jnp.where(members == pick_rows[k : k + 1, :], other, 0.0).astype(BF16)
        extra_ref[:, 0:LANES] += dot(held, line)
    scatter_rows(
        out_ref, split, stride, stride, slot_rows[...], [load_ref[...]], extra_ref, spare
    )


def unpack_rows(core, own_ref, other_ref, shard_rows, wide_ref, route_ref, gains_ref):
    pairs, rows, width = own_ref.shape
    group = 2 * pairs
    small = rows - shard_rows
    lines = []
    for i in range(group):
        own = core == i % 2
        wide_ref[i * shard_rows : (i + 1) * shard_rows, :] = jnp.where(
            own, own_ref[i // 2, :shard_rows, :], other_ref[i // 2, :shard_rows, :]
        )
        lines.append(
            jnp.where(
                own,
                own_ref[i // 2, shard_rows:, :].astype(F32),
                other_ref[i // 2, shard_rows:, :].astype(F32),
            )
        )
    lines = jnp.concatenate(lines, axis=0).astype(BF16)
    experts = route_ref.shape[1]
    each = width // group
    row, line = places((width, 1), 0), places((1, group * small), 1)
    spread = dot(one_hot(line == row // each * small), lines)
    lane = places((1, width), 1)
    spread = jnp.where(lane // experts == row % each, spread, 0.0).astype(BF16)
    fold = one_hot(places((width, 1), 0) % experts == places((1, experts), 1))
    route_ref[...] = dot(spread, fold).astype(BF16)
    each = 2 * width // group
    lane = places((1, 2 * width), 1)
    spread = dot(lines, one_hot(places((width, 1), 0) == lane % each))
    line = places((group * small, 1), 0)
    spread = jnp.where(line == lane // each * small + 1, spread, 0.0)
    gains = jnp.sum(spread, axis=0, keepdims=True)
    gains_ref[0:1, :] = gains[:, :width]
    gains_ref[1:2, :] = gains[:, width:]


def own_sums(core, x1, x2, o, dq, dk, dv, branch, dz, dgain, keep, give, wide):
    width, experts = x1.shape[1], dz.shape[1]
    pairs, rows, _ = keep.shape
    group = 2 * pairs
    shard_rows = 4 * width // group
    small = rows - shard_rows
    x1_turned = jnp.transpose(x1.astype(F32)).astype(BF16)
    for i, grads in enumerate((dq, dk, dv)):
        wide[i * width : (i + 1) * width, :] = dot(x1_turned, grads).astype(BF16)
    wide[3 * width :, :] = dot(jnp.transpose(o.astype(F32)).astype(BF16), branch).astype(BF16)
    route = dot(jnp.transpose(x2.astype(F32)).astype(BF16), dz).astype(BF16)
    each = width // group
    row, lane = places((width, 1), 0), places((1, width), 1)
    spread = dot(route, one_hot(places((experts, 1), 0) == lane % experts))
    spread = jnp.where(lane // experts == row % each, spread, 0.0).astype(BF16)
    line = places((group * small, 1), 0)
    lines = dot(one_hot(line == places((1, width), 1) // each * small), spread)
    each = 2 * width // group
    lane = places((1, 2 * width), 1)
    gains = jnp.concatenate([dgain[0:1, :], dgain[1:2, :]], axis=1)
    held = jnp.where(line == lane // each * small + 1, gains, 0.0).astype(BF16)
    lines = lines + dot(held, one_hot(places((1, width), 1) == places((2 * width, 1), 0) % each))
    for out, side in ((keep, core), (give, 1 - core)):
        for i in range(pairs):
            at = pl.multiple_of((2 * i + side) * shard_rows, 16)
            out[i, :shard_rows, :] = wide[pl.ds(at, shard_rows), :]
            out[i, shard_rows:, :] = jnp.where(
                side == 0,
                lines[2 * i * small : (2 * i + 1) * small],
                lines[(2 * i + 1) * small : (2 * i + 2) * small],
            ).astype(BF16)


def sums_kernel(scalars, *refs):
    enter_ref, hidden_ref, gains, *values, dgain, keep, give, wide = refs
    normed, _ = norm_parts(enter_ref[...].astype(F32))
    x1 = (normed * gains[0:1, :]).astype(BF16)
    normed, _ = norm_parts(hidden_ref[...])
    x2 = (normed * gains[1:2, :]).astype(BF16)
    own_sums(scalars[1], x1, x2, *(ref[...] for ref in values), dgain, keep, give, wide)


def forward_kernel(cfg, combine, packed, scalars, *refs):
    stride, chunk, capacity, rows, head_width, tile, split, shard_rows = cfg
    refs = list(refs)
    take = lambda number: [refs.pop(0) for _ in range(number)]
    if combine:
        hidden_in, returned, gates_in, slots_in = take(4)
    else:
        (tokens_ref,) = take(1)
    cos_ref, sin_ref, seg_col, seg_row = take(4)
    params = take(2 if packed else 3)
    pick_cols, pick_rows, slot_cols, slot_rows = take(4)
    send, q_out, k_out, v_out, o_out, h_out, gates_out = take(7)
    if combine:
        y_out, apart_out = take(2)
    if packed:
        wide, wr, gains = take(3)
        unpack_rows(scalars[1], *params, shard_rows, wide, wr, gains)
    else:
        wide, wr, gains = params
    group = send.shape[0] // rows

    if combine:
        line = slot_line(returned.shape[0], group, split, rows, rows, capacity)
        first = gather_rows([slots_in[:, 0:1]], line, returned, chunk)
        second = gather_rows([slots_in[:, 1:2]], line, returned, chunk)
        whole = hidden_in[...] + gates_in[:, 0:1] * first + gates_in[:, 1:2] * second
        apart_out[...] = first - second
        leaving = whole.astype(BF16)
        y_out[...] = leaving
        entering = leaving.astype(F32)
    else:
        entering = tokens_ref[...].astype(F32)

    half = head_width // 2
    width = entering.shape[1]
    cosine, sine = wide_tables(cos_ref, sin_ref)
    normed, _ = norm_parts(entering)
    x1 = (normed * gains[0:1, :]).astype(BF16)
    q_all, k_all, v_all = (dot(x1, wide[i * width : (i + 1) * width, :]) for i in range(3))
    scale = 1.0 / math.sqrt(head_width)
    queries, keys, values = [], [], []
    for at in range(0, width, LANES):
        lanes = slice(at, at + LANES)
        q, k, v = q_all[:, lanes], k_all[:, lanes], v_all[:, lanes]
        q = (q * cosine + swap_halves(q, half) * sine).astype(BF16).astype(F32) * scale
        queries.append(q.astype(BF16))
        keys.append((k * cosine + swap_halves(k, half) * sine).astype(BF16))
        values.append(v.astype(BF16))
    for out, parts in ((q_out, queries), (k_out, keys), (v_out, values)):
        out[...] = jnp.concatenate(parts, axis=1)
    mixed = attend(queries, keys, values, seg_col[...], seg_row[...], head_width, tile)
    mixed = jnp.concatenate([part.astype(BF16) for part in mixed], axis=1)
    o_out[...] = mixed
    hidden = entering + dot(mixed, wide[3 * width :, :])
    h_out[...] = hidden
    normed, _ = norm_parts(hidden)
    x2 = (normed * gains[1:2, :]).astype(BF16)
    logits = dot(x2, wr[...])
    signs = [
        jnp.where(pick_cols[:, k : k + 1] == places(logits.shape, 1), logits, 0.0) for k in range(2)
    ]
    gap = jnp.sum(signs[0] - signs[1], axis=1, keepdims=True)
    gates_out[:, 0:1] = jax.nn.sigmoid(gap)
    gates_out[:, 1:2] = jax.nn.sigmoid(-gap)
    scatter_rows(send, split, stride, rows, slot_rows[...], [x2])


def row_tiles(total, rows):
    return [(at,) for at in range(0, total, rows)]


def expert_kernel(rows, x_ref, gate_ref, up_ref, down_ref, out_ref):
    def grown(at):
        x = x_ref[at : at + rows, :]
        return dot(x, gate_ref[...]), dot(x, up_ref[...])

    def folded(at, gate, up):
        return ((gate * jax.nn.sigmoid(gate) * up).astype(BF16),)

    def out(at, hidden):
        out_ref[at : at + rows, :] = dot(hidden, down_ref[...]).astype(BF16)
        return ()

    staged(row_tiles(x_ref.shape[0], rows), grown, folded, out)


def expert_pull_kernel(
    rows, stride, out_stride, spare, x_ref, gate_ref, up_ref, g_ref, down_ref, dx_ref, act_ref, dgate_ref, dup_ref
):
    def spaced(at):
        return at // stride * out_stride

    def grown(at):
        x = x_ref[at : at + rows, :]
        gate, up = dot(x, gate_ref[...]), dot(x, up_ref[...])
        g = g_ref[spaced(at) : spaced(at + rows), :]
        if stride != out_stride:
            g = g.astype(F32)
            kept = [g[top : top + stride] for top in range(0, g.shape[0], out_stride)]
            g = jnp.concatenate(kept, axis=0).astype(BF16)
        return gate, up, dot(g, down_ref[...], 1, 1)

    def folded(at, gate, up, grad):
        sigmoid = jax.nn.sigmoid(gate)
        silu = gate * sigmoid
        act = (silu * up).astype(BF16)
        dup = (grad * silu).astype(BF16)
        dgate = (grad * up * (sigmoid + silu * (1.0 - sigmoid))).astype(BF16)
        for ref, value in ((act_ref, act), (dup_ref, dup), (dgate_ref, dgate)):
            ref[at : at + rows, :] = value
        inner = jnp.sum(grad * act.astype(F32), axis=1, keepdims=True) if spare else None
        return dgate, dup, inner

    def out(at, dgate, dup, inner):
        dx = dot(dgate, gate_ref[...], 1, 1) + dot(dup, up_ref[...], 1, 1)
        if spare:
            eye = places((stride, LANES), 0) == places((stride, LANES), 1)
            width = dx.shape[1]
            line = places((out_stride, 1), 0)
            blocks = []
            for top in range(0, rows, stride):
                row = jnp.sum(
                    jnp.where(eye, inner[top : top + stride], 0.0), axis=0, keepdims=True
                )
                high = row.astype(BF16).astype(F32)
                extra = jnp.concatenate(
                    [high, row - high, jnp.zeros((1, width - 2 * LANES), F32)], axis=1
                )
                block = dx[top : top + stride]
                if stride != out_stride:
                    pad = jnp.zeros((out_stride - stride, width), F32)
                    block = jnp.concatenate([block, pad], axis=0)
                blocks.append(jnp.where(line == spare, extra, block))
            dx = jnp.concatenate(blocks, axis=0)
        dx_ref[spaced(at) : spaced(at + rows), :] = dx.astype(BF16)
        return ()

    staged(row_tiles(x_ref.shape[0], rows), grown, folded, out)


def down_kernel(rows, act_ref, down_ref, out_ref):
    for (at,) in row_tiles(act_ref.shape[0], rows):
        out_ref[at : at + rows, :] = dot(act_ref[at : at + rows, :], down_ref[...]).astype(BF16)


def finish_kernel(cfg, hidden, returned, gates, slots, out_ref):
    stride, rows, capacity, chunk, split = cfg
    total = returned.shape[0]
    line = slot_line(total, total // rows, split, stride, rows, capacity)
    first = gather_rows([slots[:, 0:1]], line, returned, chunk)
    second = gather_rows([slots[:, 1:2]], line, returned, chunk)
    out_ref[...] = (hidden[...] + gates[:, 0:1] * first + gates[:, 1:2] * second).astype(BF16)


def backward_kernel(cfg, top, closing, *refs):
    stride, spare, chunk, capacity, next_stride, head_width, tile, split = cfg
    refs = list(refs)
    take = lambda number: [refs.pop(0) for _ in range(number)]
    if closing:
        scalars, o_ref = take(2)
    returned, grad_top, gates, pick_cols, slot_cols = take(5)
    apart = None if top else take(1)[0]
    enter_ref, hidden_ref, q_ref, k_ref, v_ref, cos_ref, sin_ref, seg_col, seg_row = take(9)
    wide, wr, gains = take(3)
    if not closing:
        next_gates, next_slots = take(2)
    grad_out, low_out = take(2)
    if closing:
        keep, give, dgain_out, wide_sums = take(4)
    else:
        dq_out, dk_out, dv_out, branch_out, dz_out, dgain_out, send = take(7)

    group = returned.shape[0] // stride
    line = slot_line(returned.shape[0], group, split, stride, stride, capacity)
    width = wide.shape[1]
    grad_y = grad_top[...].astype(F32)
    c1, c2 = gates[:, 0:1], gates[:, 1:2]
    if top:
        parts = [
            gather_rows([slot_cols[:, k : k + 1]], line, returned, chunk) for k in range(2)
        ]
        dx2 = c1 * parts[0] + c2 * parts[1]
        lines = one_hot(
            places((group, returned.shape[0]), 1)
            == places((group, returned.shape[0]), 0) * stride + spare
        )
        extra = dot(lines, returned[...]).astype(BF16)
        inner = []
        for k in range(2):
            pick = pick_cols[:, k : k + 1]
            held = dot(one_hot(pick == places((1, group), 1) // split), extra)
            held = held[:, 0:LANES] + held[:, LANES : 2 * LANES]
            rank = slot_cols[:, k : k + 1] - pick * stride
            inner.append(
                jnp.sum(
                    jnp.where(rank == places(held.shape, 1), held, 0.0), axis=1, keepdims=True
                )
            )
        apart_grad = inner[0] - inner[1]
    else:
        dx2 = gather_rows([slot_cols[:, 0:1], slot_cols[:, 1:2]], line, returned, chunk)
        apart_grad = jnp.sum(grad_y * apart[...], axis=1, keepdims=True)
    grad_gap = apart_grad * c1 * c2
    ids = places((grad_y.shape[0], wr.shape[1]), 1)
    dz = (
        jnp.where(pick_cols[:, 0:1] == ids, grad_gap, 0.0)
        - jnp.where(pick_cols[:, 1:2] == ids, grad_gap, 0.0)
    ).astype(BF16)
    if not closing:
        dz_out[...] = dz
    dx2 = dx2 + dot(dz, wr[...], 1, 1)
    normed, inverse = norm_parts(hidden_ref[...])
    x2 = (normed * gains[1:2, :]).astype(BF16)
    middle, grad_gain = norm_pull(dx2, normed, inverse, gains[1:2, :])
    dgain_out[1:2, :] = grad_gain
    grad_hidden = grad_y + middle
    branch = grad_hidden.astype(BF16)
    if not closing:
        branch_out[...] = branch
    grad_mixed = dot(branch, wide[3 * width :, :], 1, 1).astype(BF16)

    half = head_width // 2
    cosine, sine = wide_tables(cos_ref, sin_ref)
    scale = 1.0 / math.sqrt(head_width)
    blocks = [slice(at, at + LANES) for at in range(0, width, LANES)]
    pulled = attend_pull(
        *([ref[:, lanes] for lanes in blocks] for ref in (q_ref, k_ref, v_ref)),
        [grad_mixed[:, lanes] for lanes in blocks],
        seg_col[...],
        seg_row[...],
        head_width,
        tile,
    )
    turned = [[], [], []]
    for dq, dk, dv in pulled:
        dq = dq * scale
        turned[0].append((dq * cosine - swap_halves(dq, half) * sine).astype(BF16))
        turned[1].append((dk * cosine - swap_halves(dk, half) * sine).astype(BF16))
        turned[2].append(dv.astype(BF16))
    dq, dk, dv = (jnp.concatenate(parts, axis=1) for parts in turned)
    dx1 = (
        dot(dq, wide[:width, :], 1, 1)
        + dot(dk, wide[width : 2 * width, :], 1, 1)
        + dot(dv, wide[2 * width : 3 * width, :], 1, 1)
    )
    normed, inverse = norm_parts(enter_ref[...].astype(F32))
    lower, grad_gain = norm_pull(dx1, normed, inverse, gains[0:1, :])
    dgain_out[0:1, :] = grad_gain
    grad_enter = grad_hidden + lower
    grad_out[...] = grad_enter
    rounded = grad_enter.astype(BF16)
    low_out[...] = rounded
    if closing:
        x1 = (normed * gains[0:1, :]).astype(BF16)
        own_sums(
            scalars[1], x1, x2, o_ref[...], dq, dk, dv, branch, dz, dgain_out, keep, give, wide_sums
        )
    else:
        dq_out[...], dk_out[...], dv_out[...] = dq, dk, dv
        loads = [(next_gates[:, k : k + 1] * rounded.astype(F32)).astype(BF16) for k in range(2)]
        scatter_rows(send, split, next_stride, next_stride, next_slots[...], loads)


def per_device(
    tokens, segments, routes, grad_top, w_attn, norm_gains, w_route, w_gate, w_up, w_down
):
    section = lax.axis_index("section")
    place = lax.axis_index("dp")
    group = lax.axis_size("dp")
    half = group // 2
    micro_count, rows_local, length, width = tokens.shape
    count = rows_local * length
    shard_rows = w_attn.shape[1]
    route_shard, gain_shard = w_route.shape[1], norm_gains.shape[1]
    experts = route_shard * group // width
    split = group // experts
    capacity = 9 * count // (4 * experts)
    head_width = width // HEADS
    half_width = head_width // 2
    strides = (round_up(capacity, 8), round_up(capacity + 1, 8))
    spares = (0, capacity)
    sizes = tuple(group * stride for stride in strides)
    chunks = tuple(min(size, 16 * stride) for size, stride in zip(sizes, strides))
    tile = min(512, count)
    aligned = shard_rows % 16 == 0
    hidden_units = w_gate.shape[-1]

    fence = lax.optimization_barrier
    to_second, to_first = ((0, 1),), ((1, 0),)

    def across(array, pairs=((0, 1), (1, 0))):
        return lax.ppermute(array, "section", list(pairs))

    def round_dp(array, bit):
        return lax.ppermute(array, "dp", [(i, i ^ bit) for i in range(group)])

    scalars = jnp.stack([section, place % 2]).astype(I32)

    small_rows = 8

    def wide_row(row):
        return jnp.pad(row, ((0, 0), (0, width - row.shape[1])))

    own_pack = jnp.concatenate(
        [
            w_attn[0],
            wide_row(w_route),
            wide_row(norm_gains),
            jnp.zeros((small_rows - 2, width), BF16),
        ]
    )
    far_pack = across(own_pack)
    packs = (
        jnp.where(section == 0, own_pack, far_pack),
        jnp.where(section == 0, far_pack, own_pack),
    )

    def doubled(held, bit):
        return merged(held, round_dp(held, bit), bit)

    def merged(held, other, bit):
        high = (place // bit) % 2 == 1
        return jnp.where(
            high, jnp.stack([other, held], axis=1), jnp.stack([held, other], axis=1)
        ).reshape(-1, *held.shape[1:])

    bits = [group >> step for step in range(1, group.bit_length())]

    def unpack(held):
        other = round_dp(held, 1)
        if aligned:
            return [held, other]
        full = merged(held, other, 1)
        route = full[:, shard_rows, :route_shard].reshape(width, experts)
        gain = full[:, shard_rows + 1, :gain_shard].reshape(2, width).astype(F32)
        return [full[:, :shard_rows].reshape(4 * width, width), route, gain]

    def exchange(rows):
        blocks = rows.reshape(group, -1, width)
        moved = lax.all_to_all(blocks, "dp", split_axis=0, concat_axis=0, tiled=True)
        return moved.reshape(rows.shape)

    def to_owner(array, layer):
        return across(array.astype(BF16), ((1 - layer, layer),))

    own_experts = (w_gate[0, 0], w_up[0, 0], w_down[0, 0])

    def own_rows(array):
        return lax.dynamic_index_in_dim(array, section, 0, keepdims=False).reshape(count, width)

    own_routes = lax.dynamic_index_in_dim(routes[0], section, 0, keepdims=False)
    far_routes = lax.dynamic_index_in_dim(routes[0], 1 - section, 0, keepdims=False)
    own_routes, far_routes = own_routes.reshape(count, 2).T, far_routes.reshape(count, 2).T
    far_routes = across(tie(far_routes, far_pack))
    offset = jnp.arange(rows_local, dtype=I32)[:, None] * length
    segment = (lax.dynamic_index_in_dim(segments, section, 0, keepdims=False) + offset).reshape(count)
    firsts = jnp.sum((segment[:, None] > segment[None, :]).astype(I32), axis=1)
    offsets = (jnp.arange(count, dtype=I32) - firsts).astype(F32)
    freqs = jnp.exp(
        jnp.arange(half_width, dtype=F32) * (-2.0 * math.log(10000.0) / head_width)
    )
    angles = offsets[:, None] * freqs
    seg_row = segment[None, :]
    tables_out = [((count, 2), I32), ((2, count), I32)] * 4 + [((count, 1), I32)]
    *tables, seg_col = call(
        functools.partial(tables_kernel, strides, experts),
        tables_out,
        [scalars, own_routes, far_routes, seg_row],
        "tables",
        2 * 2 * count * count * experts,
        scalars=(0,),
    )
    pick_cols, pick_rows, slot_cols, slot_rows = (tables[i::4] for i in range(4))

    tokens_flops = 2 * count * width
    attn_flops = tokens_flops * (4 * width + 2 * count * (LANES // head_width) * 2)
    move_flops = [tokens_flops * size for size in sizes]
    expert_flops = [2 * size * width * hidden_units for size in sizes]

    blocks = 1
    while 2 * blocks * strides[0] <= 640 and group % (2 * blocks) == 0:
        blocks *= 2
    tile_rows = blocks * strides[0]

    def forward(layer, lead, combine, params):
        outs = [((sizes[0], width), BF16)]
        outs += [((count, width), BF16)] * 4
        outs += [((count, width), F32), ((count, 2), F32)]
        if combine:
            outs += [((count, width), BF16), ((count, width), F32)]
        if aligned:
            outs += [((4 * width, width), BF16), ((width, experts), BF16), ((2, width), F32)]
        cfg = (strides[layer], chunks[0], capacity, strides[0], head_width, tile)
        cfg += (split, shard_rows)
        results = call(
            functools.partial(forward_kernel, cfg, combine, aligned),
            outs,
            [scalars, *lead, cosine, sine, seg_col, seg_row, *params]
            + [pick_cols[layer], pick_rows[layer], slot_cols[layer], slot_rows[layer]],
            f"layer{layer}_forward",
            attn_flops + move_flops[layer] * (3 if combine else 1),
            scalars=(0,),
        )
        return results if aligned else [*results, *params]

    def backward(layer, args):
        top, closing = layer == 1, layer == 0 and aligned
        rows, line = ((count, width), BF16), ((2, width), F32)
        outs = [((count, width), F32), rows]
        scratch = []
        if closing:
            outs += [((half, shard_rows + small_rows, width), BF16)] * 2
            scratch = [pltpu.VMEM((2, width), F32), pltpu.VMEM((4 * width, width), BF16)]
        else:
            outs += [rows] * 4 + [((count, experts), BF16), line, ((sizes[0], width), BF16)]
        cfg = (strides[layer], spares[layer], chunks[layer], capacity, strides[0], head_width, tile)
        return call(
            functools.partial(backward_kernel, cfg + (split,), top, closing),
            outs,
            args,
            f"layer{layer}_backward",
            3 * attn_flops + move_flops[layer] * (4 if top else 1),
            scratch=scratch,
            scalars=(0,) if closing else (),
        )

    def pulled(rows):
        return jnp.einsum("nd,nf->df", *rows, preferred_element_type=F32)

    def by_core(entering, hidden, gains, o, dq, dk, dv, branch, dz, dgain):
        if aligned:
            block = ((half, shard_rows + small_rows, width), BF16)
            return call(
                sums_kernel,
                [block, block],
                [scalars, entering, hidden, gains, o, dq, dk, dv, branch, dz, dgain],
                "own_sums",
                4 * tokens_flops * width,
                scratch=[pltpu.VMEM((4 * width, width), BF16)],
                scalars=(0,),
            )
        x1 = (norm_parts(entering.astype(F32))[0] * gains[0:1]).astype(BF16)
        x2 = (norm_parts(hidden)[0] * gains[1:2]).astype(BF16)
        matrix = jnp.concatenate(
            [pulled((x1, dq)), pulled((x1, dk)), pulled((x1, dv)), pulled((o, branch))], axis=0
        )
        route = pulled((x2, dz)).reshape(group, 1, route_shard)
        gain = dgain.reshape(group, 1, gain_shard)
        blocks = jnp.concatenate(
            [
                matrix.reshape(group, shard_rows, width),
                jnp.pad(route, ((0, 0), (0, 0), (0, width - route_shard))),
                jnp.pad(gain, ((0, 0), (0, 0), (0, width - gain_shard))),
                jnp.zeros((group, small_rows - 2, width), F32),
            ],
            axis=1,
        ).astype(BF16)
        pairs = blocks.reshape(half, 2, *blocks.shape[1:])
        return (
            lax.dynamic_index_in_dim(pairs, place % 2, 1, keepdims=False),
            lax.dynamic_index_in_dim(pairs, 1 - place % 2, 1, keepdims=False),
        )

    def paired(keep, give):
        return added(keep, round_dp(give, 1))

    def spread(blocks):
        sets = [[2 * chip + c for chip in range(half)] for c in range(2)]
        return lax.all_to_all(
            blocks, "dp", split_axis=0, concat_axis=0, tiled=True, axis_index_groups=sets
        )

    def halved(blocks, bit):
        pairs = blocks.reshape(-1, 2, *blocks.shape[1:])
        own = (place // 2 // bit) % 2
        keep = lax.dynamic_index_in_dim(pairs, own, 1, keepdims=False)
        give = lax.dynamic_index_in_dim(pairs, 1 - own, 1, keepdims=False)
        return keep, round_dp(give, 2 * bit)

    def added(keep, got):
        return (keep.astype(F32) + got.astype(F32)).astype(BF16)

    def summed(moved):
        return jnp.sum(moved.astype(F32), axis=0)

    def by_micro(first, far_first, second, far_second):
        return jnp.where(
            section == 0,
            jnp.stack([first, far_first.astype(first.dtype)]),
            jnp.stack([far_second.astype(second.dtype), second]),
        ).reshape(1, micro_count, rows_local, length, width)

    def joined(first, far_first, second, far_second):
        whole = jnp.where(
            section == 0, first + far_first.astype(F32), second + far_second.astype(F32)
        )
        return whole[None, None]

    def hosted(index, far):
        own = own_experts[index]
        return jnp.where(section == 0, own, far), jnp.where(section == 0, far, own)

    other = round_dp(packs[0][None], bits[0])
    other, slot_rows = fence((other, slot_rows))
    gathered = merged(packs[0][None], other, bits[0])
    other = round_dp(gathered, bits[1])
    tokens, grad_top = tie((tokens, grad_top), gathered)
    token_rows, top_rows = own_rows(tokens), own_rows(grad_top)
    (top_send,) = call(
        functools.partial(scatter_kernel, strides[1], split, capacity),
        [((sizes[1], width), BF16)],
        [pick_cols[1], pick_rows[1], slot_cols[1], slot_rows[1], top_rows],
        "top_send",
        move_flops[1],
        scratch=[pltpu.VMEM((group, width), F32)],
    )
    other, top_send = fence((other, top_send))
    gathered = merged(gathered, other, bits[1])
    other = round_dp(gathered, bits[2])
    angles = tie(angles, gathered)
    cosine, sine = jnp.cos(angles), jnp.sin(angles)
    held1 = packs[1][None]
    other1 = round_dp(tie(held1, gathered), bits[0])
    other, cosine, sine, other1 = fence((other, cosine, sine, other1))
    far_gate = across(tie(own_experts[0], far_pack))
    top_received = exchange(tie(top_send, other, far_gate))
    gathered = merged(gathered, other, bits[2])
    for bit in bits[3:-1]:
        gathered = doubled(gathered, bit)

    far_up = across(tie(own_experts[1], gathered))
    results = forward(0, [token_rows], False, unpack(gathered))
    send0, q0, k0, v0, o0, h0, gates0, *params0 = results
    send0, far_up, top_received = fence((send0, far_up, top_received))
    received0 = exchange(send0)
    held1 = merged(held1, tie(other1, send0), bits[0])
    other1 = round_dp(held1, bits[1])
    far_down = across(tie(own_experts[2], send0))
    gates_up_down = [hosted(i, far) for i, far in enumerate((far_gate, far_up, far_down))]
    experts0, experts1 = zip(*gates_up_down)
    received0, experts0, experts1 = fence((received0, experts0, experts1))
    (result0,) = call(
        functools.partial(expert_kernel, tile_rows),
        [((sizes[0], width), BF16)],
        [received0, *experts0],
        "layer0_experts",
        3 * expert_flops[0],
        limit=20 << 20,
    )
    result0, other1 = fence((result0, other1))
    held1 = merged(held1, other1, bits[1])
    for bit in bits[2:-1]:
        held1 = doubled(held1, bit)
    params1 = unpack(held1)
    returned0 = exchange(result0)

    returned0, params1 = fence((returned0, params1))
    results = forward(1, [h0, returned0, gates0, slot_cols[0]], True, params1)
    send1, q1, k1, v1, o1, h1, gates1, y0, apart0, *params1 = results
    send1, y0 = fence((send1, y0))
    received1 = exchange(send1)
    far_y0 = across(y0, to_first)
    received1, far_y0 = fence((received1, far_y0))

    hidden_out = [((sizes[0], hidden_units), BF16)] * 3
    dx1_send, act1, dgate1, dup1 = call(
        functools.partial(expert_pull_kernel, tile_rows, strides[0], strides[1], capacity),
        [((sizes[1], width), BF16), *hidden_out],
        [received1, *experts1[:2], top_received, experts1[2]],
        "layer1_experts",
        5 * expert_flops[1],
    )
    dx1_send, act1, dgate1, dup1 = fence((dx1_send, act1, dgate1, dup1))
    dx1_back = exchange(dx1_send)
    top_blocks = top_received.reshape(group, strides[1], width)
    partner = top_blocks[:, capacity, : strides[0]].astype(F32).reshape(sizes[0], 1)
    logits = jnp.dot(received1, params1[1], preferred_element_type=F32)
    ids = jnp.arange(experts, dtype=I32)
    sign = (ids == place // split).astype(F32) - (ids.astype(F32) == partner).astype(F32)
    gate_slots = jax.nn.sigmoid(jnp.sum(logits * sign, axis=1, keepdims=True))
    scaled = (received1.astype(F32) * gate_slots).astype(BF16)
    top_kept = top_blocks[:, : strides[0]].reshape(sizes[0], width)
    scaled_top = (top_kept.astype(F32) * gate_slots).astype(BF16)
    gate1 = pulled((scaled, dgate1))
    far_gate1 = to_owner(gate1, 1)
    (result1,) = call(
        functools.partial(down_kernel, tile_rows),
        [((sizes[0], width), BF16)],
        [act1, experts1[2]],
        "layer1_down",
        expert_flops[1],
    )
    up1, down1 = pulled((scaled, dup1)), pulled((act1, scaled_top))
    low_up1, low_down1 = up1.astype(BF16), down1.astype(BF16)
    dx1_back, result1, gate1, up1, down1, low_up1, low_down1, far_gate1 = fence(
        (dx1_back, result1, gate1, up1, down1, low_up1, low_down1, far_gate1)
    )

    returned1 = exchange(result1)
    results = backward(
        1,
        [dx1_back, top_rows, gates1, pick_cols[1], slot_cols[1], y0, h1, q1, k1, v1]
        + [cosine, sine, seg_col, seg_row, *params1, gates0, slot_rows[0]],
    )
    results, returned1 = fence((results, returned1))
    grad1, low1, dq1, dk1, dv1, branch1, dz1, dgain1, dr0_send = results
    dr0 = exchange(dr0_send)
    far_up1 = to_owner(tie(low_up1, dr0_send), 1)
    blocks1 = paired(*by_core(y0, h1, params1[2], o1, dq1, dk1, dv1, branch1, dz1, dgain1))
    chip_bits = [1 << step for step in range(half.bit_length() - 1)]
    keep1, got1 = halved(blocks1, chip_bits[0])
    (y1,) = call(
        functools.partial(finish_kernel, (strides[1], strides[0], capacity, chunks[0], split)),
        [((count, width), BF16)],
        [h1, returned1, gates1, slot_cols[1]],
        "layer1_out",
        2 * move_flops[1],
    )
    dr0, y1 = fence((dr0, y1))

    dx0_send, act0, dgate0, dup0 = call(
        functools.partial(expert_pull_kernel, tile_rows, strides[0], strides[0], 0),
        [((sizes[0], width), BF16), *hidden_out],
        [received0, *experts0[:2], dr0, experts0[2]],
        "layer0_experts_pull",
        5 * expert_flops[0],
    )
    dx0_send, act0, dgate0, dup0, far_up1, keep1, got1 = fence(
        (dx0_send, act0, dgate0, dup0, far_up1, keep1, got1)
    )
    dx0_back = exchange(dx0_send)
    gate0 = pulled((received0, dgate0))
    far_gate0 = to_owner(gate0, 0)
    up0, down0 = pulled((received0, dup0)), pulled((act0, dr0))
    far_down1 = to_owner(tie(low_down1, gate0), 1)
    far_y1 = across(tie(y1, gate0), to_second)
    low_up0, low_down0 = up0.astype(BF16), down0.astype(BF16)
    low_up0 = (low_up0[: width // 2], low_up0[width // 2 :])
    keep1, got1 = tie((keep1, got1), dx0_send)
    for bit in chip_bits[1:-1]:
        keep1, got1 = halved(added(keep1, got1), bit)
    dx0_back, gate0, up0, down0, low_up0, low_down0, keep1, got1 = fence(
        (dx0_back, gate0, up0, down0, low_up0, low_down0, keep1, got1)
    )

    closing = [scalars, o0] if aligned else []
    results = backward(
        0,
        closing
        + [dx0_back, low1, gates0, pick_cols[0], slot_cols[0], apart0, token_rows, h0, q0, k0, v0]
        + [cosine, sine, seg_col, seg_row, *params0]
        + ([] if aligned else [gates0, slot_rows[0]]),
    )
    far_up0_a = to_owner(low_up0[0], 0)
    results, far_gate0, far_up0_a, far_down1, far_y1 = fence(
        (results, far_gate0, far_up0_a, far_down1, far_y1)
    )
    if aligned:
        grad0, low0, keep, give = results
    else:
        grad0, low0, dq0, dk0, dv0, branch0, dz0, dgain0, _ = results
        keep, give = by_core(token_rows, h0, params0[2], o0, dq0, dk0, dv0, branch0, dz0, dgain0)

    far_up0_b = to_owner(tie(low_up0[1], grad0), 0)
    far_up0 = jnp.concatenate([far_up0_a, far_up0_b])
    far_down0 = to_owner(tie(low_down0, grad0), 0)
    blocks0 = paired(keep, give)
    moved0 = spread(blocks0)
    low0, low1, y0, y1, keep1, got1 = tie((low0, low1, y0, y1, keep1, got1), blocks0)
    far_low = across(jnp.where(section == 0, low1, low0))
    keep1, got1 = halved(added(keep1, got1), chip_bits[-1])
    gate0, up0, down0, gate1, up1, down1 = tie((gate0, up0, down0, gate1, up1, down1), blocks0)
    gate_out = joined(gate0, far_gate0, gate1, far_gate1)
    up_out = joined(up0, far_up0, up1, far_up1)
    down_out = joined(down0, far_down0, down1, far_down1)
    layer_out = by_micro(y0, far_y0, y1, far_y1)
    sums1 = keep1[0].astype(F32) + got1[0].astype(F32)
    moved0, gate_out, up_out, down_out, layer_out, sums1 = fence(
        (moved0, gate_out, up_out, down_out, layer_out, sums1)
    )
    sums0 = summed(moved0)
    far_sums = across(jnp.where(section == 0, sums1, sums0))
    far_low = tie(far_low, sums0)
    input_grads = by_micro(grad0, far_low, grad1, far_low)
    total = jnp.where(section == 0, sums0, sums1) + far_sums
    return (
        layer_out,
        input_grads,
        total[:shard_rows][None],
        total[shard_rows + 1, :gain_shard][None],
        total[shard_rows, :route_shard][None],
        gate_out,
        up_out,
        down_out,
    )


def solution(mesh):
    in_specs = (
        P(None, "dp", None, None),
        P(None, "dp", None),
        P("section", None, "dp", None, None),
        P(None, "dp", None, None),
        P("section", "dp", None),
        P("section", "dp"),
        P("section", "dp"),
        P("section", "dp", None, None),
        P("section", "dp", None, None),
        P("section", "dp", None, None),
    )
    out_specs = (
        P("section", None, "dp", None, None),
        P("section", None, "dp", None, None),
        P("section", "dp", None),
        P("section", "dp"),
        P("section", "dp"),
        P("section", "dp", None, None),
        P("section", "dp", None, None),
        P("section", "dp", None, None),
    )
    return jax.shard_map(
        per_device, mesh=mesh, in_specs=in_specs, out_specs=out_specs, check_vma=False
    )
```

```python
import functools
import math

import jax
import jax.numpy as jnp
from jax import lax
from jax.experimental import pallas as pl
from jax.experimental.pallas import tpu as pltpu
from jax.sharding import PartitionSpec as P

HEADS = 6
NORM_EPSILON = 1e-05
LANES = 128
F32 = jnp.float32
BF16 = jnp.bfloat16
I32 = jnp.int32
VMEM_LIMIT = 56 * 1024 * 1024


def dot(left, right, left_dim=1, right_dim=0):
    return lax.dot_general(
        left, right, (((left_dim,), (right_dim,)), ((), ())), preferred_element_type=F32
    )


def places(shape, dim):
    return lax.broadcasted_iota(I32, shape, dim)


def tie(value, *others):
    return lax.optimization_barrier((value, others))[0]


def round_up(value, step):
    return -(-value // step) * step


def call(body, outs, args, name, flops, scratch=(), scalars=(), limit=VMEM_LIMIT):
    shapes = [jax.ShapeDtypeStruct(shape, dtype) for shape, dtype in outs]
    moved = sum(math.prod(a.shape) * a.dtype.itemsize for a in list(args) + shapes)
    return pl.pallas_call(
        body,
        out_shape=shapes,
        in_specs=[
            pl.BlockSpec(memory_space=pltpu.SMEM if index in scalars else pltpu.VMEM)
            for index in range(len(args))
        ],
        out_specs=[pl.BlockSpec(memory_space=pltpu.VMEM) for _ in shapes],
        scratch_shapes=list(scratch),
        compiler_params=pltpu.CompilerParams(vmem_limit_bytes=limit),
        cost_estimate=pl.CostEstimate(flops=flops, bytes_accessed=moved, transcendentals=0),
        name=name,
    )(*args)


def norm_parts(values):
    inverse = lax.rsqrt(jnp.mean(values * values, axis=-1, keepdims=True) + NORM_EPSILON)
    return values * inverse, inverse


def norm_pull(grad_out, normed, inverse, gain):
    grad_gain = jnp.sum(grad_out * normed, axis=0, keepdims=True)
    grad_normed = grad_out * gain
    inner = jnp.mean(grad_normed * normed, axis=-1, keepdims=True)
    return inverse * (grad_normed - normed * inner), grad_gain


def swap_halves(values, half):
    low = places((1, LANES), 1) % (2 * half) < half
    return jnp.where(
        low, pltpu.roll(values, LANES - half, 1), pltpu.roll(values, half, 1)
    )


def wide_tables(cos_ref, sin_ref):
    half = cos_ref.shape[1]
    cosine = jnp.concatenate([cos_ref[...]] * (LANES // half), axis=1)
    sine = jnp.concatenate([sin_ref[...]] * (LANES // half), axis=1)
    return cosine, jnp.where(places((1, LANES), 1) % (2 * half) < half, -sine, sine)


def head_lanes(values, head, width):
    lane = places((1, LANES), 1)
    return jnp.where((lane >= head * width) & (lane < (head + 1) * width), values, 0.0)


def staged(jobs, *stages):
    values = {}
    for step in range(len(jobs) + len(stages) - 1):
        for late, stage in enumerate(stages):
            index = step - late
            if 0 <= index < len(jobs):
                values[index] = stage(*jobs[index], *values.get(index, ()))
    return [values[index] for index in range(len(jobs))]


def attend(queries, keys, values, seg_col, seg_row, width, tile):
    count = queries[0].shape[0]
    heads = LANES // width
    turned = [jnp.transpose(v.astype(F32)).astype(BF16) for v in values]
    jobs = [
        (block, head, at)
        for block in range(len(queries))
        for head in range(heads)
        for at in range(0, count, tile)
    ]

    def scores(block, head, at):
        own = head_lanes(keys[block].astype(F32), head, width).astype(BF16)
        return (dot(own, queries[block][at : at + tile], 1, 1),)

    def terms(block, head, at, score):
        score = jnp.where(seg_col == seg_row[:, at : at + tile], score, -1e30)
        term = jnp.exp(score - jnp.max(score, axis=0, keepdims=True))
        return ((term * (1.0 / jnp.sum(term, axis=0, keepdims=True))).astype(BF16),)

    def mixed(block, head, at, weights):
        return dot(turned[block][head * width : (head + 1) * width], weights)

    parts = staged(jobs, scores, terms, mixed)
    each = count // tile
    outs = []
    for block in range(len(queries)):
        rows = []
        for head in range(heads):
            first = (block * heads + head) * each
            rows.append(jnp.concatenate(parts[first : first + each], axis=1))
        outs.append(jnp.transpose(jnp.concatenate(rows, axis=0)))
    return outs


def attend_pull(queries, keys, values, grads, seg_col, seg_row, width, tile):
    count = queries[0].shape[0]
    heads = LANES // width
    turned = [jnp.transpose(k.astype(F32)).astype(BF16) for k in keys]
    jobs = [
        (block, head, at)
        for block in range(len(queries))
        for head in range(heads)
        for at in range(0, count, tile)
    ]

    def scores(block, head, at):
        own_keys = head_lanes(keys[block].astype(F32), head, width).astype(BF16)
        own_values = head_lanes(values[block].astype(F32), head, width).astype(BF16)
        return (
            dot(own_keys, queries[block][at : at + tile], 1, 1),
            dot(own_values, grads[block][at : at + tile], 1, 1),
        )

    def terms(block, head, at, score, pulled):
        score = jnp.where(seg_col == seg_row[:, at : at + tile], score, -1e30)
        term = jnp.exp(score - jnp.max(score, axis=0, keepdims=True))
        weights = term * (1.0 / jnp.sum(term, axis=0, keepdims=True))
        inner = jnp.sum(weights * pulled, axis=0, keepdims=True)
        return weights.astype(BF16), (weights * (pulled - inner)).astype(BF16)

    def mixed(block, head, at, weights, grad_scores):
        return (
            dot(turned[block][head * width : (head + 1) * width], grad_scores),
            dot(grad_scores, queries[block][at : at + tile]),
            dot(weights, grads[block][at : at + tile]),
        )

    parts = staged(jobs, scores, terms, mixed)
    each = count // tile
    outs = []
    for block in range(len(queries)):
        rows, grad_keys, grad_values = [], 0.0, 0.0
        for head in range(heads):
            first = (block * heads + head) * each
            own = parts[first : first + each]
            rows.append(jnp.concatenate([part[0] for part in own], axis=1))
            grad_keys = grad_keys + head_lanes(sum(part[1] for part in own), head, width)
            grad_values = grad_values + head_lanes(sum(part[2] for part in own), head, width)
        outs.append((jnp.transpose(jnp.concatenate(rows, axis=0)), grad_keys, grad_values))
    return outs


def one_hot(hits):
    return jnp.where(hits, 1.0, 0.0).astype(BF16)


def scatter_rows(out_ref, split, stride, rows, slot_rows, loads, extra_ref=None, extra_at=0):
    blocks = out_ref.shape[0] // rows
    count = slot_rows.shape[1]
    first, second = slot_rows[0:1], slot_rows[1:2]

    def hits(slots, block):
        return (slots - block // split * stride) == places((rows, count), 0)

    def write(step, carry):
        pair = (2 * step, 2 * step + 1)
        if len(loads) == 1:
            chosen = one_hot(
                jnp.concatenate([hits(first, b) | hits(second, b) for b in pair], axis=0)
            )
            lines = dot(chosen, loads[0])
        else:
            lines = dot(
                one_hot(jnp.concatenate([hits(first, b) for b in pair], axis=0)), loads[0]
            ) + dot(one_hot(jnp.concatenate([hits(second, b) for b in pair], axis=0)), loads[1])
        if extra_ref is not None:
            line = places((rows, 1), 0)
            lines = jnp.concatenate(
                [
                    jnp.where(
                        line == extra_at,
                        extra_ref[pl.ds(b, 1), :],
                        lines[i * rows : (i + 1) * rows],
                    )
                    for i, b in enumerate(pair)
                ],
                axis=0,
            )
        at = step * 2 * rows if blocks <= 16 else pl.multiple_of(step * 2 * rows, 16)
        out_ref[pl.ds(at, 2 * rows), :] = lines.astype(BF16)
        return carry

    if blocks <= 16:
        for step in range(blocks // 2):
            write(step, 0)
    else:
        lax.fori_loop(0, blocks // 2, write, 0)


def slot_line(total, group, split, stride, rows, capacity):
    row = places((1, total), 1)
    at = row % rows
    return jnp.where(at < capacity, row // rows // split * stride + at, -1)


def gather_rows(slots, line, rows_ref, chunk):
    total = 0.0
    for at in range(0, rows_ref.shape[0], chunk):
        part = line[:, at : at + chunk]
        hits = slots[0] == part
        for more in slots[1:]:
            hits = hits | (more == part)
        total = total + dot(one_hot(hits), rows_ref[at : at + chunk, :])
    return total


def tables_kernel(strides, experts, scalars, *refs):
    own_ref, far_ref, seg_ref, *outs = refs
    count = seg_ref.shape[1]
    first = scalars[0] == 0
    after = one_hot(places((count, count), 0) < places((count, count), 1))
    seg_col = outs.pop()
    seg_col[...] = jnp.transpose(jnp.broadcast_to(seg_ref[...], (8, count)).astype(F32))[
        :, 0:1
    ].astype(I32)
    for layer, stride in enumerate(strides):
        pick_cols, pick_rows, slot_cols, slot_rows = outs[4 * layer : 4 * layer + 4]
        own = first if layer == 0 else jnp.logical_not(first)
        rows = jnp.where(own, own_ref[...], far_ref[...])
        pick_rows[...] = rows
        marks = [rows[k : k + 1, :] == places((experts, count), 0) for k in range(2)]
        ranks = dot(one_hot(marks[0] | marks[1]), after)
        wanted = []
        for k in range(2):
            rank = jnp.sum(jnp.where(marks[k], ranks, 0.0), axis=0, keepdims=True)
            wanted.append(rows[k : k + 1, :] * stride + rank.astype(I32))
            slot_rows[k : k + 1, :] = wanted[k]
        lines = [rows[0:1, :], rows[1:2, :], *wanted]
        lines = jnp.concatenate([line.astype(F32) for line in lines] * 2, axis=0)
        cols = jnp.transpose(lines).astype(I32)
        pick_cols[...] = cols[:, 0:2]
        slot_cols[...] = cols[:, 2:4]


def scatter_kernel(
    stride, split, spare, pick_cols, pick_rows, slot_cols, slot_rows, load_ref, out_ref, extra_ref
):
    group, count = extra_ref.shape[0], load_ref.shape[0]
    members = places((group, 1), 0) // split
    extra_ref[...] = jnp.zeros_like(extra_ref)
    for k in range(2):
        rank = slot_cols[:, k : k + 1] - pick_cols[:, k : k + 1] * stride
        line = one_hot(rank == places((count, LANES), 1))
        other = pick_rows[1 - k : 2 - k, :].astype(F32)
        held = jnp.where(members == pick_rows[k : k + 1, :], other, 0.0).astype(BF16)
        extra_ref[:, 0:LANES] += dot(held, line)
    scatter_rows(
        out_ref, split, stride, stride, slot_rows[...], [load_ref[...]], extra_ref, spare
    )


def unpack_rows(core, own_ref, other_ref, shard_rows, wide_ref, route_ref, gains_ref):
    pairs, rows, width = own_ref.shape
    group = 2 * pairs
    small = rows - shard_rows
    lines = []
    for i in range(group):
        own = core == i % 2
        wide_ref[i * shard_rows : (i + 1) * shard_rows, :] = jnp.where(
            own, own_ref[i // 2, :shard_rows, :], other_ref[i // 2, :shard_rows, :]
        )
        lines.append(
            jnp.where(
                own,
                own_ref[i // 2, shard_rows:, :].astype(F32),
                other_ref[i // 2, shard_rows:, :].astype(F32),
            )
        )
    lines = jnp.concatenate(lines, axis=0).astype(BF16)
    experts = route_ref.shape[1]
    each = width // group
    row, line = places((width, 1), 0), places((1, group * small), 1)
    spread = dot(one_hot(line == row // each * small), lines)
    lane = places((1, width), 1)
    spread = jnp.where(lane // experts == row % each, spread, 0.0).astype(BF16)
    fold = one_hot(places((width, 1), 0) % experts == places((1, experts), 1))
    route_ref[...] = dot(spread, fold).astype(BF16)
    each = 2 * width // group
    lane = places((1, 2 * width), 1)
    spread = dot(lines, one_hot(places((width, 1), 0) == lane % each))
    line = places((group * small, 1), 0)
    spread = jnp.where(line == lane // each * small + 1, spread, 0.0)
    gains = jnp.sum(spread, axis=0, keepdims=True)
    gains_ref[0:1, :] = gains[:, :width]
    gains_ref[1:2, :] = gains[:, width:]


def own_sums(core, x1, x2, o, dq, dk, dv, branch, dz, dgain, keep, give, wide):
    width, experts = x1.shape[1], dz.shape[1]
    pairs, rows, _ = keep.shape
    group = 2 * pairs
    shard_rows = 4 * width // group
    small = rows - shard_rows
    x1_turned = jnp.transpose(x1.astype(F32)).astype(BF16)
    for i, grads in enumerate((dq, dk, dv)):
        wide[i * width : (i + 1) * width, :] = dot(x1_turned, grads).astype(BF16)
    wide[3 * width :, :] = dot(jnp.transpose(o.astype(F32)).astype(BF16), branch).astype(BF16)
    route = dot(jnp.transpose(x2.astype(F32)).astype(BF16), dz).astype(BF16)
    each = width // group
    row, lane = places((width, 1), 0), places((1, width), 1)
    spread = dot(route, one_hot(places((experts, 1), 0) == lane % experts))
    spread = jnp.where(lane // experts == row % each, spread, 0.0).astype(BF16)
    line = places((group * small, 1), 0)
    lines = dot(one_hot(line == places((1, width), 1) // each * small), spread)
    each = 2 * width // group
    lane = places((1, 2 * width), 1)
    gains = jnp.concatenate([dgain[0:1, :], dgain[1:2, :]], axis=1)
    held = jnp.where(line == lane // each * small + 1, gains, 0.0).astype(BF16)
    lines = lines + dot(held, one_hot(places((1, width), 1) == places((2 * width, 1), 0) % each))
    for out, side in ((keep, core), (give, 1 - core)):
        for i in range(pairs):
            at = pl.multiple_of((2 * i + side) * shard_rows, 16)
            out[i, :shard_rows, :] = wide[pl.ds(at, shard_rows), :]
            out[i, shard_rows:, :] = jnp.where(
                side == 0,
                lines[2 * i * small : (2 * i + 1) * small],
                lines[(2 * i + 1) * small : (2 * i + 2) * small],
            ).astype(BF16)


def sums_kernel(scalars, *refs):
    enter_ref, hidden_ref, gains, *values, dgain, keep, give, wide = refs
    normed, _ = norm_parts(enter_ref[...].astype(F32))
    x1 = (normed * gains[0:1, :]).astype(BF16)
    normed, _ = norm_parts(hidden_ref[...])
    x2 = (normed * gains[1:2, :]).astype(BF16)
    own_sums(scalars[1], x1, x2, *(ref[...] for ref in values), dgain, keep, give, wide)


def forward_kernel(cfg, combine, packed, scalars, *refs):
    stride, chunk, capacity, rows, head_width, tile, split, shard_rows = cfg
    refs = list(refs)
    take = lambda number: [refs.pop(0) for _ in range(number)]
    if combine:
        hidden_in, returned, gates_in, slots_in = take(4)
    else:
        (tokens_ref,) = take(1)
    cos_ref, sin_ref, seg_col, seg_row = take(4)
    params = take(2 if packed else 3)
    pick_cols, pick_rows, slot_cols, slot_rows = take(4)
    send, q_out, k_out, v_out, o_out, h_out, gates_out = take(7)
    if combine:
        y_out, apart_out = take(2)
    if packed:
        wide, wr, gains = take(3)
        unpack_rows(scalars[1], *params, shard_rows, wide, wr, gains)
    else:
        wide, wr, gains = params
    group = send.shape[0] // rows

    if combine:
        line = slot_line(returned.shape[0], group, split, rows, rows, capacity)
        first = gather_rows([slots_in[:, 0:1]], line, returned, chunk)
        second = gather_rows([slots_in[:, 1:2]], line, returned, chunk)
        whole = hidden_in[...] + gates_in[:, 0:1] * first + gates_in[:, 1:2] * second
        apart_out[...] = first - second
        leaving = whole.astype(BF16)
        y_out[...] = leaving
        entering = leaving.astype(F32)
    else:
        entering = tokens_ref[...].astype(F32)

    half = head_width // 2
    width = entering.shape[1]
    cosine, sine = wide_tables(cos_ref, sin_ref)
    normed, _ = norm_parts(entering)
    x1 = (normed * gains[0:1, :]).astype(BF16)
    q_all, k_all, v_all = (dot(x1, wide[i * width : (i + 1) * width, :]) for i in range(3))
    scale = 1.0 / math.sqrt(head_width)
    queries, keys, values = [], [], []
    for at in range(0, width, LANES):
        lanes = slice(at, at + LANES)
        q, k, v = q_all[:, lanes], k_all[:, lanes], v_all[:, lanes]
        q = (q * cosine + swap_halves(q, half) * sine).astype(BF16).astype(F32) * scale
        queries.append(q.astype(BF16))
        keys.append((k * cosine + swap_halves(k, half) * sine).astype(BF16))
        values.append(v.astype(BF16))
    for out, parts in ((q_out, queries), (k_out, keys), (v_out, values)):
        out[...] = jnp.concatenate(parts, axis=1)
    mixed = attend(queries, keys, values, seg_col[...], seg_row[...], head_width, tile)
    mixed = jnp.concatenate([part.astype(BF16) for part in mixed], axis=1)
    o_out[...] = mixed
    hidden = entering + dot(mixed, wide[3 * width :, :])
    h_out[...] = hidden
    normed, _ = norm_parts(hidden)
    x2 = (normed * gains[1:2, :]).astype(BF16)
    logits = dot(x2, wr[...])
    signs = [
        jnp.where(pick_cols[:, k : k + 1] == places(logits.shape, 1), logits, 0.0) for k in range(2)
    ]
    gap = jnp.sum(signs[0] - signs[1], axis=1, keepdims=True)
    gates_out[:, 0:1] = jax.nn.sigmoid(gap)
    gates_out[:, 1:2] = jax.nn.sigmoid(-gap)
    scatter_rows(send, split, stride, rows, slot_rows[...], [x2])


def row_tiles(total, rows):
    return [(at,) for at in range(0, total, rows)]


def expert_kernel(rows, x_ref, gate_ref, up_ref, down_ref, out_ref):
    def grown(at):
        x = x_ref[at : at + rows, :]
        return dot(x, gate_ref[...]), dot(x, up_ref[...])

    def folded(at, gate, up):
        return ((gate * jax.nn.sigmoid(gate) * up).astype(BF16),)

    def out(at, hidden):
        out_ref[at : at + rows, :] = dot(hidden, down_ref[...]).astype(BF16)
        return ()

    staged(row_tiles(x_ref.shape[0], rows), grown, folded, out)


def expert_pull_kernel(
    rows, stride, out_stride, spare, x_ref, gate_ref, up_ref, g_ref, down_ref, dx_ref, act_ref, dgate_ref, dup_ref
):
    def spaced(at):
        return at // stride * out_stride

    def grown(at):
        x = x_ref[at : at + rows, :]
        gate, up = dot(x, gate_ref[...]), dot(x, up_ref[...])
        g = g_ref[spaced(at) : spaced(at + rows), :]
        if stride != out_stride:
            g = g.astype(F32)
            kept = [g[top : top + stride] for top in range(0, g.shape[0], out_stride)]
            g = jnp.concatenate(kept, axis=0).astype(BF16)
        return gate, up, dot(g, down_ref[...], 1, 1)

    def folded(at, gate, up, grad):
        sigmoid = jax.nn.sigmoid(gate)
        silu = gate * sigmoid
        act = (silu * up).astype(BF16)
        dup = (grad * silu).astype(BF16)
        dgate = (grad * up * (sigmoid + silu * (1.0 - sigmoid))).astype(BF16)
        for ref, value in ((act_ref, act), (dup_ref, dup), (dgate_ref, dgate)):
            ref[at : at + rows, :] = value
        inner = jnp.sum(grad * act.astype(F32), axis=1, keepdims=True) if spare else None
        return dgate, dup, inner

    def out(at, dgate, dup, inner):
        dx = dot(dgate, gate_ref[...], 1, 1) + dot(dup, up_ref[...], 1, 1)
        if spare:
            eye = places((stride, LANES), 0) == places((stride, LANES), 1)
            width = dx.shape[1]
            line = places((out_stride, 1), 0)
            blocks = []
            for top in range(0, rows, stride):
                row = jnp.sum(
                    jnp.where(eye, inner[top : top + stride], 0.0), axis=0, keepdims=True
                )
                high = row.astype(BF16).astype(F32)
                extra = jnp.concatenate(
                    [high, row - high, jnp.zeros((1, width - 2 * LANES), F32)], axis=1
                )
                block = dx[top : top + stride]
                if stride != out_stride:
                    pad = jnp.zeros((out_stride - stride, width), F32)
                    block = jnp.concatenate([block, pad], axis=0)
                blocks.append(jnp.where(line == spare, extra, block))
            dx = jnp.concatenate(blocks, axis=0)
        dx_ref[spaced(at) : spaced(at + rows), :] = dx.astype(BF16)
        return ()

    staged(row_tiles(x_ref.shape[0], rows), grown, folded, out)


def down_kernel(rows, act_ref, down_ref, out_ref):
    for (at,) in row_tiles(act_ref.shape[0], rows):
        out_ref[at : at + rows, :] = dot(act_ref[at : at + rows, :], down_ref[...]).astype(BF16)


def finish_kernel(cfg, hidden, returned, gates, slots, out_ref):
    stride, rows, capacity, chunk, split = cfg
    total = returned.shape[0]
    line = slot_line(total, total // rows, split, stride, rows, capacity)
    first = gather_rows([slots[:, 0:1]], line, returned, chunk)
    second = gather_rows([slots[:, 1:2]], line, returned, chunk)
    out_ref[...] = (hidden[...] + gates[:, 0:1] * first + gates[:, 1:2] * second).astype(BF16)


def backward_kernel(cfg, top, closing, *refs):
    stride, spare, chunk, capacity, next_stride, head_width, tile, split = cfg
    refs = list(refs)
    take = lambda number: [refs.pop(0) for _ in range(number)]
    if closing:
        scalars, o_ref = take(2)
    returned, grad_top, gates, pick_cols, slot_cols = take(5)
    apart = None if top else take(1)[0]
    enter_ref, hidden_ref, q_ref, k_ref, v_ref, cos_ref, sin_ref, seg_col, seg_row = take(9)
    wide, wr, gains = take(3)
    if not closing:
        next_gates, next_slots = take(2)
    grad_out, low_out = take(2)
    if closing:
        keep, give, dgain_out, wide_sums = take(4)
    else:
        dq_out, dk_out, dv_out, branch_out, dz_out, dgain_out, send = take(7)

    group = returned.shape[0] // stride
    line = slot_line(returned.shape[0], group, split, stride, stride, capacity)
    width = wide.shape[1]
    grad_y = grad_top[...].astype(F32)
    c1, c2 = gates[:, 0:1], gates[:, 1:2]
    if top:
        parts = [
            gather_rows([slot_cols[:, k : k + 1]], line, returned, chunk) for k in range(2)
        ]
        dx2 = c1 * parts[0] + c2 * parts[1]
        lines = one_hot(
            places((group, returned.shape[0]), 1)
            == places((group, returned.shape[0]), 0) * stride + spare
        )
        extra = dot(lines, returned[...]).astype(BF16)
        inner = []
        for k in range(2):
            pick = pick_cols[:, k : k + 1]
            held = dot(one_hot(pick == places((1, group), 1) // split), extra)
            held = held[:, 0:LANES] + held[:, LANES : 2 * LANES]
            rank = slot_cols[:, k : k + 1] - pick * stride
            inner.append(
                jnp.sum(
                    jnp.where(rank == places(held.shape, 1), held, 0.0), axis=1, keepdims=True
                )
            )
        apart_grad = inner[0] - inner[1]
    else:
        dx2 = gather_rows([slot_cols[:, 0:1], slot_cols[:, 1:2]], line, returned, chunk)
        apart_grad = jnp.sum(grad_y * apart[...], axis=1, keepdims=True)
    grad_gap = apart_grad * c1 * c2
    ids = places((grad_y.shape[0], wr.shape[1]), 1)
    dz = (
        jnp.where(pick_cols[:, 0:1] == ids, grad_gap, 0.0)
        - jnp.where(pick_cols[:, 1:2] == ids, grad_gap, 0.0)
    ).astype(BF16)
    if not closing:
        dz_out[...] = dz
    dx2 = dx2 + dot(dz, wr[...], 1, 1)
    normed, inverse = norm_parts(hidden_ref[...])
    x2 = (normed * gains[1:2, :]).astype(BF16)
    middle, grad_gain = norm_pull(dx2, normed, inverse, gains[1:2, :])
    dgain_out[1:2, :] = grad_gain
    grad_hidden = grad_y + middle
    branch = grad_hidden.astype(BF16)
    if not closing:
        branch_out[...] = branch
    grad_mixed = dot(branch, wide[3 * width :, :], 1, 1).astype(BF16)

    half = head_width // 2
    cosine, sine = wide_tables(cos_ref, sin_ref)
    scale = 1.0 / math.sqrt(head_width)
    blocks = [slice(at, at + LANES) for at in range(0, width, LANES)]
    pulled = attend_pull(
        *([ref[:, lanes] for lanes in blocks] for ref in (q_ref, k_ref, v_ref)),
        [grad_mixed[:, lanes] for lanes in blocks],
        seg_col[...],
        seg_row[...],
        head_width,
        tile,
    )
    turned = [[], [], []]
    for dq, dk, dv in pulled:
        dq = dq * scale
        turned[0].append((dq * cosine - swap_halves(dq, half) * sine).astype(BF16))
        turned[1].append((dk * cosine - swap_halves(dk, half) * sine).astype(BF16))
        turned[2].append(dv.astype(BF16))
    dq, dk, dv = (jnp.concatenate(parts, axis=1) for parts in turned)
    dx1 = (
        dot(dq, wide[:width, :], 1, 1)
        + dot(dk, wide[width : 2 * width, :], 1, 1)
        + dot(dv, wide[2 * width : 3 * width, :], 1, 1)
    )
    normed, inverse = norm_parts(enter_ref[...].astype(F32))
    lower, grad_gain = norm_pull(dx1, normed, inverse, gains[0:1, :])
    dgain_out[0:1, :] = grad_gain
    grad_enter = grad_hidden + lower
    grad_out[...] = grad_enter
    rounded = grad_enter.astype(BF16)
    low_out[...] = rounded
    if closing:
        x1 = (normed * gains[0:1, :]).astype(BF16)
        own_sums(
            scalars[1], x1, x2, o_ref[...], dq, dk, dv, branch, dz, dgain_out, keep, give, wide_sums
        )
    else:
        dq_out[...], dk_out[...], dv_out[...] = dq, dk, dv
        loads = [(next_gates[:, k : k + 1] * rounded.astype(F32)).astype(BF16) for k in range(2)]
        scatter_rows(send, split, next_stride, next_stride, next_slots[...], loads)


def per_device(
    tokens, segments, routes, grad_top, w_attn, norm_gains, w_route, w_gate, w_up, w_down
):
    section = lax.axis_index("section")
    place = lax.axis_index("dp")
    group = lax.axis_size("dp")
    half = group // 2
    micro_count, rows_local, length, width = tokens.shape
    count = rows_local * length
    shard_rows = w_attn.shape[1]
    route_shard, gain_shard = w_route.shape[1], norm_gains.shape[1]
    experts = route_shard * group // width
    split = group // experts
    capacity = 9 * count // (4 * experts)
    head_width = width // HEADS
    half_width = head_width // 2
    strides = (round_up(capacity, 8), round_up(capacity + 1, 8))
    spares = (0, capacity)
    sizes = tuple(group * stride for stride in strides)
    chunks = tuple(min(size, 16 * stride) for size, stride in zip(sizes, strides))
    tile = min(512, count)
    aligned = shard_rows % 16 == 0
    hidden_units = w_gate.shape[-1]

    fence = lax.optimization_barrier
    to_second, to_first = ((0, 1),), ((1, 0),)

    def across(array, pairs=((0, 1), (1, 0))):
        return lax.ppermute(array, "section", list(pairs))

    def round_dp(array, bit):
        return lax.ppermute(array, "dp", [(i, i ^ bit) for i in range(group)])

    scalars = jnp.stack([section, place % 2]).astype(I32)

    small_rows = 8

    def wide_row(row):
        return jnp.pad(row, ((0, 0), (0, width - row.shape[1])))

    own_pack = jnp.concatenate(
        [
            w_attn[0],
            wide_row(w_route),
            wide_row(norm_gains),
            jnp.zeros((small_rows - 2, width), BF16),
        ]
    )
    far_pack = across(own_pack)
    packs = (
        jnp.where(section == 0, own_pack, far_pack),
        jnp.where(section == 0, far_pack, own_pack),
    )

    def doubled(held, bit):
        return merged(held, round_dp(held, bit), bit)

    def merged(held, other, bit):
        high = (place // bit) % 2 == 1
        return jnp.where(
            high, jnp.stack([other, held], axis=1), jnp.stack([held, other], axis=1)
        ).reshape(-1, *held.shape[1:])

    bits = [group >> step for step in range(1, group.bit_length())]

    def unpack(held):
        other = round_dp(held, 1)
        if aligned:
            return [held, other]
        full = merged(held, other, 1)
        route = full[:, shard_rows, :route_shard].reshape(width, experts)
        gain = full[:, shard_rows + 1, :gain_shard].reshape(2, width).astype(F32)
        return [full[:, :shard_rows].reshape(4 * width, width), route, gain]

    def exchange(rows):
        blocks = rows.reshape(group, -1, width)
        moved = lax.all_to_all(blocks, "dp", split_axis=0, concat_axis=0, tiled=True)
        return moved.reshape(rows.shape)

    def to_owner(array, layer):
        return across(array.astype(BF16), ((1 - layer, layer),))

    own_experts = (w_gate[0, 0], w_up[0, 0], w_down[0, 0])

    def own_rows(array):
        return lax.dynamic_index_in_dim(array, section, 0, keepdims=False).reshape(count, width)

    own_routes = lax.dynamic_index_in_dim(routes[0], section, 0, keepdims=False)
    far_routes = lax.dynamic_index_in_dim(routes[0], 1 - section, 0, keepdims=False)
    own_routes, far_routes = own_routes.reshape(count, 2).T, far_routes.reshape(count, 2).T
    far_routes = across(tie(far_routes, far_pack))
    offset = jnp.arange(rows_local, dtype=I32)[:, None] * length
    segment = (lax.dynamic_index_in_dim(segments, section, 0, keepdims=False) + offset).reshape(count)
    firsts = jnp.sum((segment[:, None] > segment[None, :]).astype(I32), axis=1)
    offsets = (jnp.arange(count, dtype=I32) - firsts).astype(F32)
    freqs = jnp.exp(
        jnp.arange(half_width, dtype=F32) * (-2.0 * math.log(10000.0) / head_width)
    )
    angles = offsets[:, None] * freqs
    seg_row = segment[None, :]
    tables_out = [((count, 2), I32), ((2, count), I32)] * 4 + [((count, 1), I32)]
    *tables, seg_col = call(
        functools.partial(tables_kernel, strides, experts),
        tables_out,
        [scalars, own_routes, far_routes, seg_row],
        "tables",
        2 * 2 * count * count * experts,
        scalars=(0,),
    )
    pick_cols, pick_rows, slot_cols, slot_rows = (tables[i::4] for i in range(4))

    tokens_flops = 2 * count * width
    attn_flops = tokens_flops * (4 * width + 2 * count * (LANES // head_width) * 2)
    move_flops = [tokens_flops * size for size in sizes]
    expert_flops = [2 * size * width * hidden_units for size in sizes]

    blocks = 1
    while 2 * blocks * strides[0] <= 640 and group % (2 * blocks) == 0:
        blocks *= 2
    tile_rows = blocks * strides[0]

    def forward(layer, lead, combine, params):
        outs = [((sizes[0], width), BF16)]
        outs += [((count, width), BF16)] * 4
        outs += [((count, width), F32), ((count, 2), F32)]
        if combine:
            outs += [((count, width), BF16), ((count, width), F32)]
        if aligned:
            outs += [((4 * width, width), BF16), ((width, experts), BF16), ((2, width), F32)]
        cfg = (strides[layer], chunks[0], capacity, strides[0], head_width, tile)
        cfg += (split, shard_rows)
        results = call(
            functools.partial(forward_kernel, cfg, combine, aligned),
            outs,
            [scalars, *lead, cosine, sine, seg_col, seg_row, *params]
            + [pick_cols[layer], pick_rows[layer], slot_cols[layer], slot_rows[layer]],
            f"layer{layer}_forward",
            attn_flops + move_flops[layer] * (3 if combine else 1),
            scalars=(0,),
        )
        return results if aligned else [*results, *params]

    def backward(layer, args):
        top, closing = layer == 1, layer == 0 and aligned
        rows, line = ((count, width), BF16), ((2, width), F32)
        outs = [((count, width), F32), rows]
        scratch = []
        if closing:
            outs += [((half, shard_rows + small_rows, width), BF16)] * 2
            scratch = [pltpu.VMEM((2, width), F32), pltpu.VMEM((4 * width, width), BF16)]
        else:
            outs += [rows] * 4 + [((count, experts), BF16), line, ((sizes[0], width), BF16)]
        cfg = (strides[layer], spares[layer], chunks[layer], capacity, strides[0], head_width, tile)
        return call(
            functools.partial(backward_kernel, cfg + (split,), top, closing),
            outs,
            args,
            f"layer{layer}_backward",
            3 * attn_flops + move_flops[layer] * (4 if top else 1),
            scratch=scratch,
            scalars=(0,) if closing else (),
        )

    def pulled(rows):
        return jnp.einsum("nd,nf->df", *rows, preferred_element_type=F32)

    def by_core(entering, hidden, gains, o, dq, dk, dv, branch, dz, dgain):
        if aligned:
            block = ((half, shard_rows + small_rows, width), BF16)
            return call(
                sums_kernel,
                [block, block],
                [scalars, entering, hidden, gains, o, dq, dk, dv, branch, dz, dgain],
                "own_sums",
                4 * tokens_flops * width,
                scratch=[pltpu.VMEM((4 * width, width), BF16)],
                scalars=(0,),
            )
        x1 = (norm_parts(entering.astype(F32))[0] * gains[0:1]).astype(BF16)
        x2 = (norm_parts(hidden)[0] * gains[1:2]).astype(BF16)
        matrix = jnp.concatenate(
            [pulled((x1, dq)), pulled((x1, dk)), pulled((x1, dv)), pulled((o, branch))], axis=0
        )
        route = pulled((x2, dz)).reshape(group, 1, route_shard)
        gain = dgain.reshape(group, 1, gain_shard)
        blocks = jnp.concatenate(
            [
                matrix.reshape(group, shard_rows, width),
                jnp.pad(route, ((0, 0), (0, 0), (0, width - route_shard))),
                jnp.pad(gain, ((0, 0), (0, 0), (0, width - gain_shard))),
                jnp.zeros((group, small_rows - 2, width), F32),
            ],
            axis=1,
        ).astype(BF16)
        pairs = blocks.reshape(half, 2, *blocks.shape[1:])
        return (
            lax.dynamic_index_in_dim(pairs, place % 2, 1, keepdims=False),
            lax.dynamic_index_in_dim(pairs, 1 - place % 2, 1, keepdims=False),
        )

    def paired(keep, give):
        return added(keep, round_dp(give, 1))

    def spread(blocks):
        sets = [[2 * chip + c for chip in range(half)] for c in range(2)]
        return lax.all_to_all(
            blocks, "dp", split_axis=0, concat_axis=0, tiled=True, axis_index_groups=sets
        )

    def halved(blocks, bit):
        pairs = blocks.reshape(-1, 2, *blocks.shape[1:])
        own = (place // 2 // bit) % 2
        keep = lax.dynamic_index_in_dim(pairs, own, 1, keepdims=False)
        give = lax.dynamic_index_in_dim(pairs, 1 - own, 1, keepdims=False)
        return keep, round_dp(give, 2 * bit)

    def added(keep, got):
        return (keep.astype(F32) + got.astype(F32)).astype(BF16)

    def summed(moved):
        return jnp.sum(moved.astype(F32), axis=0)

    def by_micro(first, far_first, second, far_second):
        return jnp.where(
            section == 0,
            jnp.stack([first, far_first.astype(first.dtype)]),
            jnp.stack([far_second.astype(second.dtype), second]),
        ).reshape(1, micro_count, rows_local, length, width)

    def joined(first, far_first, second, far_second):
        whole = jnp.where(
            section == 0, first + far_first.astype(F32), second + far_second.astype(F32)
        )
        return whole[None, None]

    def hosted(index, far):
        own = own_experts[index]
        return jnp.where(section == 0, own, far), jnp.where(section == 0, far, own)

    other = round_dp(packs[0][None], bits[0])
    other, slot_rows = fence((other, slot_rows))
    gathered = merged(packs[0][None], other, bits[0])
    other = round_dp(gathered, bits[1])
    tokens, grad_top = tie((tokens, grad_top), gathered)
    token_rows, top_rows = own_rows(tokens), own_rows(grad_top)
    (top_send,) = call(
        functools.partial(scatter_kernel, strides[1], split, capacity),
        [((sizes[1], width), BF16)],
        [pick_cols[1], pick_rows[1], slot_cols[1], slot_rows[1], top_rows],
        "top_send",
        move_flops[1],
        scratch=[pltpu.VMEM((group, width), F32)],
    )
    other, top_send = fence((other, top_send))
    gathered = merged(gathered, other, bits[1])
    other = round_dp(gathered, bits[2])
    angles = tie(angles, gathered)
    cosine, sine = jnp.cos(angles), jnp.sin(angles)
    held1 = packs[1][None]
    other1 = round_dp(tie(held1, gathered), bits[0])
    other, cosine, sine, other1 = fence((other, cosine, sine, other1))
    far_gate = across(tie(own_experts[0], far_pack))
    top_received = exchange(tie(top_send, other, far_gate))
    gathered = merged(gathered, other, bits[2])
    for bit in bits[3:-1]:
        gathered = doubled(gathered, bit)

    far_up = across(tie(own_experts[1], gathered))
    results = forward(0, [token_rows], False, unpack(gathered))
    send0, q0, k0, v0, o0, h0, gates0, *params0 = results
    send0, far_up, top_received = fence((send0, far_up, top_received))
    received0 = exchange(send0)
    held1 = merged(held1, tie(other1, send0), bits[0])
    other1 = round_dp(held1, bits[1])
    far_down = across(tie(own_experts[2], send0))
    gates_up_down = [hosted(i, far) for i, far in enumerate((far_gate, far_up, far_down))]
    experts0, experts1 = zip(*gates_up_down)
    received0, experts0, experts1 = fence((received0, experts0, experts1))
    (result0,) = call(
        functools.partial(expert_kernel, tile_rows),
        [((sizes[0], width), BF16)],
        [received0, *experts0],
        "layer0_experts",
        3 * expert_flops[0],
        limit=20 << 20,
    )
    result0, other1 = fence((result0, other1))
    held1 = merged(held1, other1, bits[1])
    for bit in bits[2:-1]:
        held1 = doubled(held1, bit)
    params1 = unpack(held1)
    returned0 = exchange(result0)

    returned0, params1 = fence((returned0, params1))
    results = forward(1, [h0, returned0, gates0, slot_cols[0]], True, params1)
    send1, q1, k1, v1, o1, h1, gates1, y0, apart0, *params1 = results
    send1, y0 = fence((send1, y0))
    received1 = exchange(send1)
    far_y0 = across(y0, to_first)
    received1, far_y0 = fence((received1, far_y0))

    hidden_out = [((sizes[0], hidden_units), BF16)] * 3
    dx1_send, act1, dgate1, dup1 = call(
        functools.partial(expert_pull_kernel, tile_rows, strides[0], strides[1], capacity),
        [((sizes[1], width), BF16), *hidden_out],
        [received1, *experts1[:2], top_received, experts1[2]],
        "layer1_experts",
        5 * expert_flops[1],
    )
    dx1_send, act1, dgate1, dup1 = fence((dx1_send, act1, dgate1, dup1))
    dx1_back = exchange(dx1_send)
    top_blocks = top_received.reshape(group, strides[1], width)
    partner = top_blocks[:, capacity, : strides[0]].astype(F32).reshape(sizes[0], 1)
    logits = jnp.dot(received1, params1[1], preferred_element_type=F32)
    ids = jnp.arange(experts, dtype=I32)
    sign = (ids == place // split).astype(F32) - (ids.astype(F32) == partner).astype(F32)
    gate_slots = jax.nn.sigmoid(jnp.sum(logits * sign, axis=1, keepdims=True))
    scaled = (received1.astype(F32) * gate_slots).astype(BF16)
    top_kept = top_blocks[:, : strides[0]].reshape(sizes[0], width)
    scaled_top = (top_kept.astype(F32) * gate_slots).astype(BF16)
    gate1 = pulled((scaled, dgate1))
    far_gate1 = to_owner(gate1, 1)
    (result1,) = call(
        functools.partial(down_kernel, tile_rows),
        [((sizes[0], width), BF16)],
        [act1, experts1[2]],
        "layer1_down",
        expert_flops[1],
    )
    up1, down1 = pulled((scaled, dup1)), pulled((act1, scaled_top))
    low_up1, low_down1 = up1.astype(BF16), down1.astype(BF16)
    dx1_back, result1, gate1, up1, down1, low_up1, low_down1, far_gate1 = fence(
        (dx1_back, result1, gate1, up1, down1, low_up1, low_down1, far_gate1)
    )

    returned1 = exchange(result1)
    results = backward(
        1,
        [dx1_back, top_rows, gates1, pick_cols[1], slot_cols[1], y0, h1, q1, k1, v1]
        + [cosine, sine, seg_col, seg_row, *params1, gates0, slot_rows[0]],
    )
    results, returned1 = fence((results, returned1))
    grad1, low1, dq1, dk1, dv1, branch1, dz1, dgain1, dr0_send = results
    dr0 = exchange(dr0_send)
    far_up1 = to_owner(tie(low_up1, dr0_send), 1)
    blocks1 = paired(*by_core(y0, h1, params1[2], o1, dq1, dk1, dv1, branch1, dz1, dgain1))
    chip_bits = [1 << step for step in range(half.bit_length() - 1)]
    keep1, got1 = halved(blocks1, chip_bits[0])
    (y1,) = call(
        functools.partial(finish_kernel, (strides[1], strides[0], capacity, chunks[0], split)),
        [((count, width), BF16)],
        [h1, returned1, gates1, slot_cols[1]],
        "layer1_out",
        2 * move_flops[1],
    )
    dr0, y1 = fence((dr0, y1))

    dx0_send, act0, dgate0, dup0 = call(
        functools.partial(expert_pull_kernel, tile_rows, strides[0], strides[0], 0),
        [((sizes[0], width), BF16), *hidden_out],
        [received0, *experts0[:2], dr0, experts0[2]],
        "layer0_experts_pull",
        5 * expert_flops[0],
    )
    dx0_send, act0, dgate0, dup0, far_up1, keep1, got1 = fence(
        (dx0_send, act0, dgate0, dup0, far_up1, keep1, got1)
    )
    dx0_back = exchange(dx0_send)
    gate0 = pulled((received0, dgate0))
    far_gate0 = to_owner(gate0, 0)
    up0, down0 = pulled((received0, dup0)), pulled((act0, dr0))
    far_down1 = to_owner(tie(low_down1, gate0), 1)
    far_y1 = across(tie(y1, gate0), to_second)
    low_up0, low_down0 = up0.astype(BF16), down0.astype(BF16)
    low_up0 = (low_up0[: width // 2], low_up0[width // 2 :])
    keep1, got1 = tie((keep1, got1), dx0_send)
    for bit in chip_bits[1:-1]:
        keep1, got1 = halved(added(keep1, got1), bit)
    dx0_back, gate0, up0, down0, low_up0, low_down0 = fence(
        (dx0_back, gate0, up0, down0, low_up0, low_down0)
    )

    closing = [scalars, o0] if aligned else []
    results = backward(
        0,
        closing
        + [dx0_back, low1, gates0, pick_cols[0], slot_cols[0], apart0, token_rows, h0, q0, k0, v0]
        + [cosine, sine, seg_col, seg_row, *params0]
        + ([] if aligned else [gates0, slot_rows[0]]),
    )
    far_up0_a = to_owner(low_up0[0], 0)
    results, far_gate0, far_up0_a, far_down1, far_y1, keep1, got1 = fence(
        (results, far_gate0, far_up0_a, far_down1, far_y1, keep1, got1)
    )
    if aligned:
        grad0, low0, keep, give = results
    else:
        grad0, low0, dq0, dk0, dv0, branch0, dz0, dgain0, _ = results
        keep, give = by_core(token_rows, h0, params0[2], o0, dq0, dk0, dv0, branch0, dz0, dgain0)

    far_up0_b = to_owner(tie(low_up0[1], grad0), 0)
    far_up0 = jnp.concatenate([far_up0_a, far_up0_b])
    far_down0 = to_owner(tie(low_down0, grad0), 0)
    blocks0 = paired(keep, give)
    moved0 = spread(blocks0)
    low0, low1, y0, y1, keep1, got1 = tie((low0, low1, y0, y1, keep1, got1), blocks0)
    far_low = across(jnp.where(section == 0, low1, low0))
    keep1, got1 = halved(added(keep1, got1), chip_bits[-1])
    gate0, up0, down0, gate1, up1, down1 = tie((gate0, up0, down0, gate1, up1, down1), blocks0)
    gate_out = joined(gate0, far_gate0, gate1, far_gate1)
    up_out = joined(up0, far_up0, up1, far_up1)
    down_out = joined(down0, far_down0, down1, far_down1)
    layer_out = by_micro(y0, far_y0, y1, far_y1)
    sums1 = keep1[0].astype(F32) + got1[0].astype(F32)
    moved0, gate_out, up_out, down_out, layer_out, sums1 = fence(
        (moved0, gate_out, up_out, down_out, layer_out, sums1)
    )
    sums0 = summed(moved0)
    far_sums = across(jnp.where(section == 0, sums1, sums0))
    far_low = tie(far_low, sums0)
    input_grads = by_micro(grad0, far_low, grad1, far_low)
    total = jnp.where(section == 0, sums0, sums1) + far_sums
    return (
        layer_out,
        input_grads,
        total[:shard_rows][None],
        total[shard_rows + 1, :gain_shard][None],
        total[shard_rows, :route_shard][None],
        gate_out,
        up_out,
        down_out,
    )


def solution(mesh):
    in_specs = (
        P(None, "dp", None, None),
        P(None, "dp", None),
        P("section", None, "dp", None, None),
        P(None, "dp", None, None),
        P("section", "dp", None),
        P("section", "dp"),
        P("section", "dp"),
        P("section", "dp", None, None),
        P("section", "dp", None, None),
        P("section", "dp", None, None),
    )
    out_specs = (
        P("section", None, "dp", None, None),
        P("section", None, "dp", None, None),
        P("section", "dp", None),
        P("section", "dp"),
        P("section", "dp"),
        P("section", "dp", None, None),
        P("section", "dp", None, None),
        P("section", "dp", None, None),
    )
    return jax.shard_map(
        per_device, mesh=mesh, in_specs=in_specs, out_specs=out_specs, check_vma=False
    )
```
